32 devices in a mesh: section: 2 (over x), dp: 4 (over z), tensor: 4 (over y, core).
Axes of the slice: x: 2, y: 2, z: 4, core: 2. Of those that a mesh axis runs over, the one named last changes fastest.
Arguments:
- boundary: bfloat16 [2, 2, 1024, 4, 768], P('section', None, 'tensor', 'dp'), may hold values from -6 to 6
- document_lengths: int32 [2, 4, 6], P(None, 'dp'), may hold values from 1 to 832, 1024 in all within a row
- norm_gain: float32 [2, 768], P('section'), may hold values from 0.25 to 1.75
- norm_bias: float32 [2, 768], P('section'), may hold values from -3 to 3
- pair_weight: bfloat16 [2, 768, 2, 768], P('section', None, None, 'tensor'), may hold values from -0.21875 to 0.21875
- value_weight: bfloat16 [2, 768, 768], P('section', None, 'tensor'), may hold values from -0.375 to 0.375
- query_bias: float32 [2, 768], P('section', 'tensor'), may hold values from -3 to 3
- value_bias: float32 [2, 768], P('section', 'tensor'), may hold values from -3 to 3
- inner_gain: float32 [2, 768], P('section', 'tensor'), may hold values from 0.25 to 1.75
- inner_bias: float32 [2, 768], P('section', 'tensor'), may hold values from -3 to 3
- merge_weight: bfloat16 [2, 768, 768], P('section', 'tensor'), may hold values from -0.375 to 0.375
- merge_bias: float32 [2, 768], P('section'), may hold values from -3 to 3
- second_gain: float32 [2, 768], P('section'), may hold values from 0.25 to 1.75
- second_bias: float32 [2, 768], P('section'), may hold values from -3 to 3
- expand_weight: bfloat16 [2, 768, 3072], P('section', None, 'tensor'), may hold values from -0.375 to 0.375
- expand_bias: float32 [2, 3072], P('section', 'tensor'), may hold values from -3 to 3
- hidden_gain: float32 [2, 3072], P('section', 'tensor'), may hold values from 0.25 to 1.75
- hidden_bias: float32 [2, 3072], P('section', 'tensor'), may hold values from -3 to 3
- shrink_weight: bfloat16 [2, 3072, 768], P('section', 'tensor'), may hold values from -0.1875 to 0.1875
- shrink_bias: float32 [2, 768], P('section'), may hold values from -3 to 3
Outputs:
- boundary_result: bfloat16 [2, 2, 1024, 4, 768], P('section', None, 'tensor', 'dp')
- norm_gain_gradient: float32 [2, 768], P('section')
- norm_bias_gradient: float32 [2, 768], P('section')
- pair_weight_gradient: float32 [2, 768, 2, 768], P('section', 'dp', None, 'tensor')
- value_weight_gradient: float32 [2, 768, 768], P('section', 'dp', 'tensor')
- query_bias_gradient: float32 [2, 768], P('section', 'tensor')
- value_bias_gradient: float32 [2, 768], P('section', 'tensor')
- inner_gain_gradient: float32 [2, 768], P('section', 'tensor')
- inner_bias_gradient: float32 [2, 768], P('section', 'tensor')
- merge_weight_gradient: float32 [2, 768, 768], P('section', 'tensor', 'dp')
- merge_bias_gradient: float32 [2, 768], P('section')
- second_gain_gradient: float32 [2, 768], P('section')
- second_bias_gradient: float32 [2, 768], P('section')
- expand_weight_gradient: float32 [2, 768, 3072], P('section', 'dp', 'tensor')
- expand_bias_gradient: float32 [2, 3072], P('section', 'tensor')
- hidden_gain_gradient: float32 [2, 3072], P('section', 'tensor')
- hidden_bias_gradient: float32 [2, 3072], P('section', 'tensor')
- shrink_weight_gradient: float32 [2, 3072, 768], P('section', 'tensor', 'dp')
- shrink_bias_gradient: float32 [2, 768], P('section')
The draws below stay inside these ranges and needn't reach their ends.
Inputs may be any that keep to these rules, and one draw needn't show every extreme that they name: `document_lengths`: in every row the 6 lengths sum to 1024, and the longest is exactly 832.
All inputs are finite; a program needn't handle non-finite values.
Results may differ from the reference program's by a relative error of at most 0.028.
Values may be sent and summed in bfloat16 or wider, within the bound.
No kernel may reach another device: no remote copies, remote signals or barrier semaphores. Data moves between devices by JAX's collectives and lax.ppermute only.
A program may use at most 192 MiB of HBM per device.

```python
import math
import jax
import jax.numpy as jnp
import numpy as np
from jax import lax

D = 768
HEADS = 12
HEAD_DIM = 64
FF = 3072
SEQ = 1024
MB = 2
LAYERS = 2
NDOC = 6
ROWS = 4
N_TENSOR = 4


def levels(own_key, dims, cuts, smallest, high):
    def one(position, parts):
        steps = jax.random.uniform(jax.random.fold_in(jax.random.fold_in(own_key, 6), position), (parts,), jnp.float32, smallest / len(cuts), high / len(cuts))
        return jnp.repeat(jnp.exp(steps), dims[position] // parts).reshape((-1,) + (1,) * (len(dims) - position - 1))

    level = one(*cuts[0])
    for cut in cuts[1:]:
        level = level * one(*cut)
    return level


def length_profile(count, total, reach, slope):
    portions = [(1 << 20) // math.isqrt(standing ** slope) + 1 for standing in range(2, count + 1)]
    rest, holding = total - reach - (count - 1), [1] * (count - 1)
    while rest > 0:
        free = [i for i in range(count - 1) if holding[i] < reach]
        whole, remaining = sum([portions[i] for i in free]), rest
        for i in free:
            addition = min(reach - holding[i], max(1, remaining * portions[i] // whole), rest)
            holding[i] = holding[i] + addition
            rest = rest - addition
    return np.array([reach] + holding)


def uneven_parts(stream_key, amount, total, reach, lean):
    if amount == 2:
        one = jax.random.randint(stream_key, (), max(1, total - reach), min(reach, total - 1) + 1)
        return jnp.stack([one, total - one])
    sizes = jnp.asarray(length_profile(amount, total, reach, lean), jnp.int32)
    pairs = (amount - 1) // 2
    source_of, taker = sizes[1:1 + 2 * pairs:2], sizes[2:2 + 2 * pairs:2]
    margin = jnp.minimum(source_of - 1, reach - taker)
    shifted = jax.random.randint(jax.random.fold_in(stream_key, 1), (pairs,), 0, 1 << 20) % (margin + 1)
    sizes = sizes.at[1:1 + 2 * pairs:2].set(source_of - shifted).at[2:2 + 2 * pairs:2].set(taker + shifted)
    return sizes[jax.random.permutation(jax.random.fold_in(stream_key, 2), amount)]


def bell_draw(stream_key, dims, deviation, most, cuts=(), kind=jnp.bfloat16):
    values = deviation * jax.random.normal(stream_key, dims, jnp.float32)
    if cuts:
        values = values * levels(stream_key, dims, cuts, -0.22, 0.18)
    return jnp.clip(values, -most, most).astype(kind)


def setup_inputs(seed: int = 0) -> dict:
    streams_of = jax.random.split(jax.random.key(seed), 21)
    boundary = bell_draw(streams_of[0], (2, MB, SEQ, ROWS, D), 1.0, 6.0, ((0, 2), (2, 4), (3, 4)))
    document_lengths = jax.vmap(lambda own: uneven_parts(own, NDOC, SEQ, SEQ * 13 // 16, 2))(jax.random.split(streams_of[1], MB * ROWS)).reshape((MB, ROWS, NDOC)).astype(jnp.int32)
    norm_gain = jnp.clip(1.0 + 0.15 * jax.random.normal(streams_of[2], (LAYERS, D), jnp.float32), 0.25, 1.75)
    norm_bias = bell_draw(streams_of[3], (LAYERS, D), 0.5, 3.0, ((0, 2),), jnp.float32)
    pair_weight = bell_draw(streams_of[4], (LAYERS, D, 2, D), D ** -0.5, 0.21875, ((0, 2), (3, 4)))
    value_weight = bell_draw(streams_of[5], (LAYERS, D, D), (D * 10 // 32) ** -0.5, 0.375, ((0, 2), (2, 4)))
    query_bias = bell_draw(streams_of[6], (LAYERS, D), 0.5, 3.0, ((0, 2), (1, 4)), jnp.float32)
    value_bias = bell_draw(streams_of[7], (LAYERS, D), 0.5, 3.0, ((0, 2), (1, 4)), jnp.float32)
    inner_gain = jnp.clip(1.0 + 0.15 * jax.random.normal(streams_of[8], (LAYERS, D), jnp.float32), 0.25, 1.75)
    inner_bias = bell_draw(streams_of[9], (LAYERS, D), 0.5, 3.0, ((0, 2), (1, 4)), jnp.float32)
    merge_weight = bell_draw(streams_of[10], (LAYERS, D, D), (D * 10 // 32) ** -0.5, 0.375, ((0, 2), (1, 4)))
    merge_bias = bell_draw(streams_of[11], (LAYERS, D), 0.5, 3.0, ((0, 2),), jnp.float32)
    second_gain = jnp.clip(1.0 + 0.15 * jax.random.normal(streams_of[12], (LAYERS, D), jnp.float32), 0.25, 1.75)
    second_bias = bell_draw(streams_of[13], (LAYERS, D), 0.5, 3.0, ((0, 2),), jnp.float32)
    expand_weight = bell_draw(streams_of[14], (LAYERS, D, FF), (D * 10 // 32) ** -0.5, 0.375, ((0, 2), (2, 4)))
    expand_bias = bell_draw(streams_of[15], (LAYERS, FF), 0.5, 3.0, ((0, 2), (1, 4)), jnp.float32)
    hidden_gain = jnp.clip(1.0 + 0.15 * jax.random.normal(streams_of[16], (LAYERS, FF), jnp.float32), 0.25, 1.75)
    hidden_bias = bell_draw(streams_of[17], (LAYERS, FF), 0.5, 3.0, ((0, 2), (1, 4)), jnp.float32)
    shrink_weight = bell_draw(streams_of[18], (LAYERS, FF, D), (FF * 10 // 32) ** -0.5, 0.1875, ((0, 2), (1, 4)))
    shrink_bias = bell_draw(streams_of[19], (LAYERS, D), 0.5, 3.0, ((0, 2),), jnp.float32)
    return {"boundary": boundary, "document_lengths": document_lengths, "norm_gain": norm_gain, "norm_bias": norm_bias, "pair_weight": pair_weight, "value_weight": value_weight, "query_bias": query_bias, "value_bias": value_bias, "inner_gain": inner_gain, "inner_bias": inner_bias, "merge_weight": merge_weight, "merge_bias": merge_bias, "second_gain": second_gain, "second_bias": second_bias, "expand_weight": expand_weight, "expand_bias": expand_bias, "hidden_gain": hidden_gain, "hidden_bias": hidden_bias, "shrink_weight": shrink_weight, "shrink_bias": shrink_bias}


@jax.custom_vjp
def low(v):
    return lax.optimization_barrier(v.astype(jnp.bfloat16)).astype(jnp.float32)

@jax.custom_vjp
def low_back(v):
    return v

def low_keep(v):
    return (low(v), None)

def low_pass(kept, grad):
    return (grad,)

def back_keep(v):
    return (v, None)

def back_low(kept, grad):
    return (low(grad),)
low.defvjp(low_keep, low_pass)
low_back.defvjp(back_keep, back_low)
EPS = 1e-05
HIGH = lax.Precision.HIGHEST

def norm(values, gain, bias):
    mean = lax.optimization_barrier(jnp.mean(values, axis=-1, keepdims=True))
    spread = lax.optimization_barrier(jnp.mean(values * values, axis=-1, keepdims=True)) - mean * mean
    return (values - mean) * lax.rsqrt(spread + EPS) * gain + bias

def document_ids(lengths):
    ends = jnp.cumsum(lengths, axis=-1)
    positions = jnp.arange(SEQ, dtype=jnp.int32)
    return lax.optimization_barrier(jnp.sum((positions[:, None, None] >= ends[None, :, :]).astype(jnp.int32), axis=-1))

def attention(query, keys, values, documents):
    scores = jnp.einsum('qghd,kghd->ghqk', query, keys, precision=HIGH) * HEAD_DIM ** (-0.5)
    scores = low_back(scores)
    positions = jnp.arange(SEQ, dtype=jnp.int32)
    allowed = (documents.T[:, None, :, None] == documents.T[:, None, None, :]) & (positions[None, None, None, :] <= positions[None, None, :, None])
    scores = jnp.where(allowed, scores, -1e+30)
    top = lax.optimization_barrier(jnp.max(scores, axis=-1, keepdims=True))
    weights = jnp.exp(scores - top)
    probs = low(weights / lax.optimization_barrier(jnp.sum(weights, axis=-1, keepdims=True)))
    return jnp.einsum('ghqk,kghd->qghd', probs, values, precision=HIGH)

def split_sum(left, weight):
    length, group, inner = left.shape
    pieces = left.reshape(length, group, N_TENSOR, inner // N_TENSOR)
    blocks = weight.reshape(N_TENSOR, inner // N_TENSOR, weight.shape[-1])
    partials = low(jnp.einsum('sgke,ked->ksgd', pieces, blocks, precision=HIGH))
    return lax.optimization_barrier(jnp.sum(partials, axis=0))

def copies(values):
    return jnp.stack([low_back(values) for index in range(N_TENSOR)])

def layer(inputs, documents, params):
    norm_gain, norm_bias, pair_weight, value_weight, query_bias, value_bias, inner_gain, inner_bias, merge_weight, merge_bias, second_gain, second_bias, expand_weight, expand_bias, hidden_gain, hidden_bias, shrink_weight, shrink_bias = params
    length, group, width = inputs.shape
    heads_shape = (length, group, HEADS, HEAD_DIM)
    block_width = width // N_TENSOR
    normed = copies(low(norm(inputs, norm_gain, norm_bias)))
    pair_blocks = pair_weight.reshape(width, 2, N_TENSOR, block_width)
    value_blocks = value_weight.reshape(width, N_TENSOR, block_width)
    paired = jnp.einsum('ksgd,dcke->sgcke', normed, pair_blocks, precision=HIGH).reshape(length, group, 2, width)
    valued = jnp.einsum('ksgd,dke->sgke', normed, value_blocks, precision=HIGH).reshape(length, group, width)
    paired = low_back(paired)
    valued = low_back(valued)
    query = low(paired[:, :, 0] + query_bias).reshape(heads_shape)
    keys = low(paired[:, :, 1]).reshape(heads_shape)
    values = low(valued + value_bias).reshape(heads_shape)
    mixed = low_back(attention(query, keys, values, documents)).reshape(length, group, width)
    merged = low(norm(mixed, inner_gain, inner_bias))
    middle = inputs + (low_back(split_sum(merged, merge_weight)) + merge_bias)
    second = copies(low(norm(middle, second_gain, second_bias)))
    expand_blocks = expand_weight.reshape(width, N_TENSOR, FF // N_TENSOR)
    expanded = jnp.einsum('ksgd,dkf->sgkf', second, expand_blocks, precision=HIGH).reshape(length, group, FF)
    expanded = low_back(expanded) + expand_bias
    hidden = jax.nn.gelu(expanded, approximate=False)
    shrunk = low(norm(hidden, hidden_gain, hidden_bias))
    return middle + (low_back(split_sum(shrunk, shrink_weight)) + shrink_bias)

def stack_forward(inputs, lengths, params):
    documents = document_ids(lengths)
    hidden = inputs
    for index in range(LAYERS):
        hidden = layer(hidden, documents, tuple((item[index] for item in params)))
        if index + 1 < LAYERS:
            hidden = low_back(low(hidden))
    return hidden

def reference(boundary, document_lengths, norm_gain, norm_bias, pair_weight, value_weight, query_bias, value_bias, inner_gain, inner_bias, merge_weight, merge_bias, second_gain, second_bias, expand_weight, expand_bias, hidden_gain, hidden_bias, shrink_weight, shrink_bias):
    params = tuple((item.astype(jnp.float32) for item in (norm_gain, norm_bias, pair_weight, value_weight, query_bias, value_bias, inner_gain, inner_bias, merge_weight, merge_bias, second_gain, second_bias, expand_weight, expand_bias, hidden_gain, hidden_bias, shrink_weight, shrink_bias)))
    group = math.gcd(MB * ROWS, max(1, 4096 // SEQ))
    count = MB * ROWS // group

    def to_groups(array):
        return array.transpose(0, 2, 1, 3).reshape(count, group, SEQ, D).transpose(0, 2, 1, 3)

    def from_groups(array):
        return array.transpose(0, 2, 1, 3).reshape(MB, ROWS, SEQ, D).transpose(0, 2, 1, 3)
    inputs = to_groups(boundary[0].astype(jnp.float32))
    cotangent = to_groups(boundary[1].astype(jnp.float32))
    lengths = document_lengths.reshape(count, group, NDOC).astype(jnp.int32)

    def whole(block_inputs, block_params):

        def step(carry, item):
            block, block_lengths = item
            return (carry, jax.checkpoint(stack_forward)(block, block_lengths, block_params))
        return lax.scan(step, None, (block_inputs, lengths))[1]
    outputs, back = jax.vjp(whole, inputs, params)
    input_gradient, grads = back(cotangent)
    boundary_result = jnp.stack([from_groups(input_gradient), from_groups(outputs)]).astype(jnp.bfloat16)
    return (boundary_result, grads[0], grads[1], grads[2], grads[3], grads[4], grads[5], grads[6], grads[7], grads[8], grads[9], grads[10], grads[11], grads[12], grads[13], grads[14], grads[15], grads[16], grads[17])
```

```python
from functools import partial

import jax
import jax.numpy as jnp
from jax import lax
from jax.experimental import pallas as pl
from jax.experimental.pallas import tpu as pltpu
from jax.sharding import PartitionSpec as P

HEAD_DIM = 64
EPS = 1e-05
MASKED = -1e30
CORES = 2
STAT_ROWS = 16
BF = jnp.bfloat16
F32 = jnp.float32

NORM_GAIN, NORM_BIAS, HEADS = range(3)
(MERGE_ADD, SECOND_GAIN, SECOND_BIAS, SHRINK_ADD, MERGE_GW, MERGE_GW_THERE, SHRINK_GW,
 SHRINK_GW_THERE, EXPAND_BIAS, HIDDEN_GAIN, HIDDEN_BIAS) = range(11)
SHARD_COLUMNS = 3
COLUMNS = 16
FAR = 1 << 30
SECTION, DP, TENSOR = "section", "dp", "tensor"
IN_SECTION, IN_CHIP, IN_CORE, IN_DP = range(4)
FEED, ATTEND, HEAD, FEED_STEP, ATTEND_STEP = range(5)
ASIDE = {
    (HEAD, 1, 1): [(FEED, 1)],
    (HEAD, 1, 0): [(FEED_STEP, 1)],
    (FEED, 0, 1): [(ATTEND, 1)],
    (FEED, 0, 0): [(FEED, 0), (ATTEND_STEP, 1)],
    (ATTEND, 0, 1): [(FEED_STEP, 0)],
    (HEAD, 0, 1): [(FEED_STEP, 1), (ATTEND_STEP, 1)],
    (ATTEND, 0, 0): [(FEED_STEP, 1)],
}
VMEM_MB = 14


def nn(a, b):
    return lax.dot_general(a, b, (((1,), (0,)), ((), ())), preferred_element_type=F32)


def tn(a, b):
    return lax.dot_general(a, b, (((0,), (0,)), ((), ())), preferred_element_type=F32)


def nt(a, b):
    return lax.dot_general(a, b, (((1,), (1,)), ((), ())), preferred_element_type=F32)


def column(vec_ref, index, start=0, size=None):
    size = vec_ref.shape[0] if size is None else size
    return vec_ref[start : start + size, index : index + 1]


def shard_column(vec_ref, index, shard):
    return column(vec_ref, index + shard * SHARD_COLUMNS)


def head_column(vec_ref, part, shard, size):
    return column(vec_ref, HEADS + shard, part * size, size)


def row_total(values):
    return jnp.sum(values, axis=0, keepdims=True)


def token_stats(values):
    count = values.shape[0]
    mean = row_total(values) / count
    return mean, lax.rsqrt(row_total(values * values) / count - mean * mean + EPS)


def three_parts(row):
    high = row.astype(BF).astype(F32)
    middle = (row - high).astype(BF).astype(F32)
    return [high, middle, row - high - middle]


def rows_of(rows, first, count, dtype):
    width = rows[0].shape[1]
    index = lax.broadcasted_iota(jnp.int32, (count, width), 0)
    total = jnp.zeros((count, width), F32)
    for place, row in enumerate(rows):
        total = jnp.where(index == first + place, row, total)
    return total.astype(dtype)


def sum_parts(block, first):
    return block[first : first + 1] + block[first + 1 : first + 2] + block[first + 2 : first + 3]


def folded(values):
    total = values[:, :128]
    for place in range(128, values.shape[1], 128):
        total = total + values[:, place : place + 128]
    return total


def token_sum_row(part):
    return row_total(part.T)


def gelu_pair(values):
    cdf = 0.5 * (1.0 + lax.erf(values * (0.5**0.5)))
    density = jnp.exp(values * values * -0.5) * 0.3989422804014327
    return values * cdf, cdf + values * density


def gelu(values):
    return values * (0.5 * (1.0 + lax.erf(values * (0.5**0.5))))


def split_product(out_ref, parts, weights, gains):
    count = sum(part.shape[0] for part in parts)
    first_sum = sum(row_total(part) for part in parts)
    second_sum = sum(row_total(part * part) for part in parts)
    mean = first_sum / count
    product = None
    for part, weight, gain in zip(parts, weights, gains):
        term = tn(weight[...], ((part - mean) * gain).astype(BF))
        product = term if product is None else product + term
    low = product.astype(BF)
    width = product.shape[0]
    out_ref[:width, :] = low
    out_ref[width:, :] = rows_of(three_parts(first_sum) + three_parts(second_sum), 0, STAT_ROWS, BF)
    return low, first_sum, second_sum


def whole_stats(firsts, seconds, share):
    count = len(firsts) * share
    mean = sum(firsts) / count
    return mean, lax.rsqrt(sum(seconds) / count - mean * mean + EPS)


def combined(own_ref, recv_ref, vec_ref, first_column, share):
    width = own_ref.shape[0] - STAT_ROWS
    extra = [ref[width:, :].astype(F32) for ref in (own_ref, recv_ref)]
    firsts = [sum_parts(rows, 0) for rows in extra]
    mean, rstd = whole_stats(firsts, [sum_parts(rows, 3) for rows in extra], share)
    total = own_ref[:width, :].astype(F32) + recv_ref[:width, :].astype(F32)
    for place, first in enumerate(firsts):
        total = total + (first / share - mean) * column(vec_ref, first_column + place)
    return total * rstd, mean, rstd


def write_stats(ref, mean, rstd):
    ref[...] = rows_of([mean, rstd], 0, ref.shape[0], F32)


def project(normed, heads, vec_ref, q_ref, kv_ref):
    width = q_ref.shape[0] // 2
    for shard in range(2):
        projected = nn(heads[shard][...], normed)
        query = projected[:width] + head_column(vec_ref, 0, shard, width)
        value = projected[2 * width :] + head_column(vec_ref, 1, shard, width)
        q_ref[shard * width : (shard + 1) * width, :] = query.astype(BF)
        first = 2 * width * shard
        kv_ref[first : first + width, :] = projected[width : 2 * width].astype(BF)
        kv_ref[first + width : first + 2 * width, :] = value.astype(BF)


def norm_and_project(low, vec_ref, heads, h_ref, n_ref, q_ref, kv_ref):
    h_ref[...] = low
    values = low.astype(F32)
    mean, rstd = token_stats(values)
    normed = (
        (values - mean) * rstd * column(vec_ref, NORM_GAIN) + column(vec_ref, NORM_BIAS)
    ).astype(BF)
    n_ref[...] = normed
    project(normed, heads, vec_ref, q_ref, kv_ref)


def start_kernel(flag_ref, x_ref, vec_ref, heads_own, heads_peer, *outs):
    norm_and_project(x_ref[...].astype(F32).T.astype(BF), vec_ref, (heads_own, heads_peer), *outs)


def columns_of(rows, out_ref):
    filled = jnp.concatenate([rows, jnp.zeros((128 - rows.shape[0], rows.shape[1]), F32)], axis=0)
    out_ref[...] = filled.T


def early_kernel(flag_ref, own_ref, came_ref, own_peer_ref, came_peer_ref, *out_refs):
    first = flag_ref[IN_SECTION] == 0
    sets = []
    for ref, peer in ((own_ref, own_peer_ref[0:1, :]), (came_ref, came_peer_ref[2:3, :])):
        rows = [ref[0:1, :], ref[1:2, :], ref[2:3, :], peer]
        sets.append(rows_of(rows, 0, 8, F32))
    columns_of(jnp.where(first, sets[0], sets[1]), out_refs[0])
    columns_of(jnp.where(first, sets[1], sets[0]), out_refs[1])


def late_kernel(flag_ref, own_ref, came_ref, *out_refs):
    first = flag_ref[IN_SECTION] == 0
    columns_of(jnp.where(first, own_ref[...], came_ref[...]), out_refs[0])
    columns_of(jnp.where(first, came_ref[...], own_ref[...]), out_refs[1])


def pick_kernel(flag_ref, *refs):
    here = flag_ref[IN_CHIP] == 0
    count = (len(refs) - 1) // 3
    pairs, out_refs = refs[: 2 * count], refs[2 * count :]
    for place in range(count):
        left, right = pairs[2 * place][...], pairs[2 * place + 1][...]
        out_refs[place][...] = jnp.where(here, left, right)
        if not place:
            out_refs[-1][...] = jnp.where(here, right, left)


def between_kernel(
    share,
    own_ref,
    recv_ref,
    middle_ref,
    vec_ref,
    next_ref,
    heads_own,
    heads_peer,
    t_ref,
    stat_ref,
    *outs,
):
    product, mean, rstd = combined(own_ref, recv_ref, vec_ref, SHRINK_GW, share)
    write_stats(stat_ref, mean, rstd)
    t_ref[...] = product.astype(BF)
    low = (middle_ref[...] + (product + column(vec_ref, SHRINK_ADD))).astype(BF)
    norm_and_project(low, next_ref, (heads_own, heads_peer), *outs)


def key_pieces(chunk, size, core, start_row, kv_refs):
    block = start_row.shape[1]
    rows = kv_refs[0].shape[0]
    far = pl.multiple_of((1 - core) * rows, rows)
    pieces = []
    for index in range(chunk + 1):
        own_ref, both_ref = kv_refs[2 * index : 2 * index + 2]
        last = index == chunk
        peer_start = jnp.where(core == 1, start_row, FAR) if last else start_row
        places = (index * size + core * block, index * size + (1 - core) * block)
        pieces.append((own_ref, (0, rows // 2), places[0], start_row, last))
        pieces.append((both_ref, (far + rows // 2, far), places[1], peer_start, False))
    return pieces


def piece_rows(piece, shard, row):
    first = piece[1][shard] + row
    if not isinstance(first, int):
        first = pl.multiple_of(first, HEAD_DIM)
    return piece[0][pl.ds(first, HEAD_DIM), :]


def piece_mask(piece, queries):
    ref, rows, first, start_row, diagonal = piece
    shape = (ref.shape[1], queries)
    rows = lax.broadcasted_iota(jnp.int32, shape, 0)
    mask = first + rows >= start_row
    if diagonal:
        mask = mask & (rows <= lax.broadcasted_iota(jnp.int32, shape, 1))
    return mask


def attention_forward_kernel(chunk, size, *refs):
    flag_ref, start_ref, q_ref, merge_own, merge_peer, vec_ref = refs[:6]
    kv_refs = refs[6 : 8 + 2 * chunk]
    out_ref, mixed_ref, lse_ref = refs[8 + 2 * chunk :]
    width = q_ref.shape[0] // 2
    queries = q_ref.shape[1]
    pieces = key_pieces(chunk, size, flag_ref[IN_CORE], start_ref[...], kv_refs)
    masks = [piece_mask(piece, queries) for piece in pieces]
    heads = width // HEAD_DIM
    lse_rows = []
    for shard in range(2):
        for head in range(heads):
            first = shard * width + head * HEAD_DIM
            base = head * HEAD_DIM
            query = (q_ref[first : first + HEAD_DIM, :] * HEAD_DIM ** (-0.5)).astype(BF)
            scores, values, top = [], [], None
            for piece, mask in zip(pieces, masks):
                keys = piece_rows(piece, shard, base)
                values.append(piece_rows(piece, shard, base + width))
                score = jnp.where(mask, tn(keys, query), MASKED)
                scores.append(score)
                piece_top = jnp.max(score, axis=0, keepdims=True)
                top = piece_top if top is None else jnp.maximum(top, piece_top)
            weights = [jnp.exp(score - top) for score in scores]
            total = sum(row_total(weight) for weight in weights)
            inverse = 1.0 / total
            mixed = None
            for weight, value in zip(weights, values):
                term = nn(value, (weight * inverse).astype(BF))
                mixed = term if mixed is None else mixed + term
            mixed_ref[first : first + HEAD_DIM, :] = mixed
            lse_rows.append(top + jnp.log(total))
    lse_ref[...] = rows_of(lse_rows, 0, lse_ref.shape[0], F32)
    split_product(
        out_ref,
        [mixed_ref[:width, :], mixed_ref[width:, :]],
        [merge_own, merge_peer],
        [head_column(vec_ref, 2, shard, width) for shard in range(2)],
    )


def feed_forward_kernel(share, last, chunk, *refs):
    own_ref, recv_ref, h_ref, vec_ref = refs[:4]
    expand, shrink = refs[4:6], refs[6:8]
    refs = refs[8:]
    if last:
        change_ref, refs = refs[0], refs[1:]
        before_refs, refs = refs[: chunk > 0], refs[chunk > 0 :]
    out_ref, middle_ref, second_ref, t_ref, stat_ref, expanded_ref = refs[:6]
    product, mean, rstd = combined(own_ref, recv_ref, vec_ref, MERGE_GW, share)
    write_stats(stat_ref, mean, rstd)
    t_ref[...] = product.astype(BF)
    middle = h_ref[...].astype(F32) + (product + column(vec_ref, MERGE_ADD))
    middle_ref[...] = middle
    mean, rstd = token_stats(middle)
    second = (
        (middle - mean) * rstd * column(vec_ref, SECOND_GAIN) + column(vec_ref, SECOND_BIAS)
    ).astype(BF)
    second_ref[...] = second
    shard = expanded_ref.shape[0] // 2
    hidden = []
    for index in range(2):
        expanded = tn(expand[index][...], second) + shard_column(vec_ref, EXPAND_BIAS, index)
        expanded_ref[index * shard : (index + 1) * shard, :] = expanded
        hidden.append(gelu(expanded))
    gains = [shard_column(vec_ref, HIDDEN_GAIN, index) for index in range(2)]
    low, first_sum, second_sum = split_product(out_ref, hidden, shrink, gains)
    if last:
        dot = row_total(low.astype(F32) * change_ref[...].astype(F32))
        for ref in before_refs:
            refs[6][: 8 * chunk, :] = ref[...]
        refs[6][8 * chunk :, :] = rows_of([first_sum, second_sum, dot], 0, 8, F32)


def cotangent_kernel(x_ref, vec_ref, low_ref, dots_ref):
    change = x_ref[...].astype(F32).T
    low_ref[...] = change.astype(BF)
    dots_ref[...] = rows_of(
        [row_total(change * column(vec_ref, SHRINK_GW + place)) for place in range(2)], 0, 8, F32
    )


def output_kernel(share, own_ref, recv_ref, middle_ref, vec_ref, out_ref):
    product, mean, rstd = combined(own_ref, recv_ref, vec_ref, SHRINK_GW, share)
    output = middle_ref[...] + (product + column(vec_ref, SHRINK_ADD))
    out_ref[...] = output.T.astype(BF)


def upstream_rows(values, product, vec_ref, first_column, count):
    total = column(vec_ref, first_column) + column(vec_ref, first_column + 1)
    return row_total(values * total) / count, row_total(values * product) / count


def norm_back(own_ref, recv_ref, change_ref, h_ref, vec_ref):
    width = own_ref.shape[0]
    normed_change = own_ref[...].astype(F32) + recv_ref[...].astype(F32)
    values = h_ref[...].astype(F32)
    mean, rstd = token_stats(values)
    unit = (values - mean) * rstd
    scaled = normed_change * column(vec_ref, NORM_GAIN)
    first = row_total(scaled) / width
    second = row_total(scaled * unit) / width
    change = change_ref[...] + rstd * (scaled - first - unit * second)
    return change, (normed_change * unit, normed_change)


def feed_backward(low, first, second, mean, rstd, rows, refs):
    vec_ref = refs[0]
    expand, shrink, expanded_ref = refs[1:3], refs[3:5], refs[5]
    out_ref, change_ref, shrunk_ref, sums_ref = refs[6:]
    shard = expanded_ref.shape[0] // 2
    sums = []
    product = None
    for index in range(2):
        here = slice(index * shard, (index + 1) * shard)
        gain = shard_column(vec_ref, HIDDEN_GAIN, index)
        shrunk_change = nn(shrink[index][...], low)
        hidden, slope = gelu_pair(expanded_ref[here, :])
        unit = (hidden - mean) * rstd
        shrunk_ref[here, :] = (unit * gain + shard_column(vec_ref, HIDDEN_BIAS, index)).astype(BF)
        expanded_change = rstd * (shrunk_change * gain - first - unit * second) * slope
        sums.append(
            [
                token_sum_row(folded(part))
                for part in (shrunk_change * unit, shrunk_change, expanded_change)
            ]
        )
        expanded_low = expanded_change.astype(BF)
        change_ref[here, :] = expanded_low
        term = nn(expand[index][...], expanded_low)
        product = term if product is None else product + term
    out_ref[...] = product.astype(BF)
    rows = [row for pair in zip(*sums) for row in pair] + rows
    sums_ref[...] = rows_of(rows, 0, 16, F32)


def turn_kernel(share, chunk, own_ref, recv_ref, low_ref, dots_ref, *refs):
    at = 8 * chunk
    firsts = [ref[at : at + 1, :] for ref in (own_ref, recv_ref)]
    seconds = [ref[at + 1 : at + 2, :] for ref in (own_ref, recv_ref)]
    mean, rstd = whole_stats(firsts, seconds, share)
    count = 2 * share
    second = own_ref[at + 2 : at + 3, :] + recv_ref[at + 2 : at + 3, :]
    first = 0.0
    for place, total in enumerate(firsts):
        dot = dots_ref[place : place + 1, :]
        first = first + dot
        second = second + (total / share - mean) * dot
    low = low_ref[...]
    zero = jnp.zeros((1, low.shape[0]), F32)
    rows = [zero, zero, token_sum_row(folded(low.astype(F32)))]
    feed_backward(low, first / count, second * rstd / count, mean, rstd, rows, refs)


def layer_back_kernel(
    share, own_ref, recv_ref, change_ref, h_ref, upper_ref, t_ref, stat_ref, *refs
):
    change, rows = norm_back(own_ref, recv_ref, change_ref, h_ref, upper_ref)
    low = change.astype(BF)
    up_ref, refs = refs[6], refs[:6] + refs[7:]
    up_ref[...] = low
    values = low.astype(F32)
    first, second = upstream_rows(values, t_ref[...].astype(F32), refs[0], SHRINK_GW, 2 * share)
    rows = [token_sum_row(folded(part)) for part in rows + (values,)]
    feed_backward(low, first, second, stat_ref[0:1, :], stat_ref[1:2, :], rows, refs)


def write_pieces(refs, first, values):
    rows = refs[0].shape[0]
    for place, ref in enumerate(refs):
        ref[:, first : first + values.shape[1]] = values[place * rows : (place + 1) * rows].astype(BF)


def feed_weights_kernel(pieces, *refs):
    refs, outs = refs[: -1 - pieces], refs[-1 - pieces :]
    shard = outs[0].shape[1] // 2
    chunks = len(refs) // 4
    for index, out_refs in ((1, outs[1:]), (0, outs[:1])):
        here = slice(index * shard, (index + 1) * shard)
        shrink = expand = None
        for chunk in range(chunks):
            up, shrunk, change, second = refs[4 * chunk : 4 * chunk + 4]
            term = nt(up[...], shrunk[here, :])
            shrink = term if shrink is None else shrink + term
            term = nt(second[...], change[here, :])
            expand = term if expand is None else expand + term
        write_pieces(out_refs, 0, shrink)
        write_pieces(out_refs, shard, expand)


def attention_backward_kernel(chunk, size, later, *refs):
    own_part, recv_part, up_ref, middle_ref, t_ref, stat_ref, late_ref, vec_ref = refs[:8]
    flag_ref, start_ref, q_ref, merge_own, merge_peer, mixed_ref, lse_ref = refs[8:15]
    refs = refs[15:]
    kv_refs, refs = refs[: 2 * chunk + 2], refs[2 * chunk + 2 :]
    later_refs, refs = refs[:later], refs[later:]
    low_ref, change_ref, gq_ref, merged_ref = refs[:4]
    own_sum, recv_low, sums_ref = refs[4:7]
    before_sums = refs[7 : 7 + 2 * chunk]
    recv_sum, mixed_change_ref = refs[7 + 2 * chunk :]

    width = up_ref.shape[0]
    second_change = own_part[...].astype(F32) + recv_part[...].astype(F32)
    middle = middle_ref[...]
    mean, rstd = token_stats(middle)
    unit = (middle - mean) * rstd
    scaled = second_change * column(late_ref, SECOND_GAIN)
    first = row_total(scaled) / width
    second = row_total(scaled * unit) / width
    change = up_ref[...].astype(F32) + rstd * (scaled - first - unit * second)
    change_ref[...] = change
    low = change.astype(BF)
    low_ref[...] = low
    rows = [
        token_sum_row(folded(part)) for part in (second_change * unit, second_change, change)
    ]
    first, second = upstream_rows(
        low.astype(F32), t_ref[...].astype(F32), late_ref, MERGE_GW, width
    )
    mean, rstd = stat_ref[0:1, :], stat_ref[1:2, :]
    head_width = q_ref.shape[0] // 2
    norm_parts = []
    for shard, merge in ((0, merge_own), (1, merge_peer)):
        here = slice(shard * head_width, (shard + 1) * head_width)
        gain = head_column(vec_ref, 2, shard, head_width)
        merged_change = nn(merge[...], low)
        unit = (mixed_ref[here, :] - mean) * rstd
        merged_ref[here, :] = (unit * gain + head_column(vec_ref, 3, shard, head_width)).astype(BF)
        norm_parts.append((folded(merged_change * unit), folded(merged_change)))
        mixed_change_ref[here, :] = (
            rstd * (merged_change * gain - first - unit * second)
        ).astype(BF)

    queries = q_ref.shape[1]
    pieces = key_pieces(chunk, size, flag_ref[IN_CORE], start_ref[...], kv_refs)
    masks = [piece_mask(piece, queries) for piece in pieces]
    totals = list(before_sums) + [own_sum, recv_sum]
    for place, ref in enumerate((own_sum, recv_sum)):
        ref[...] = later_refs[place][...] if later else jnp.zeros(ref.shape, F32)
    for ref in before_sums:
        ref[...] = jnp.zeros(ref.shape, F32)
    factor = HEAD_DIM ** (-0.5)
    query_parts = []
    for shard in range(2):
        query_folds = []
        for head in range(head_width // HEAD_DIM):
            place = shard * head_width + head * HEAD_DIM
            here = slice(place, place + HEAD_DIM)
            query = q_ref[here, :]
            scaled_query = (query * factor).astype(BF)
            mixed_change = mixed_change_ref[here, :]
            row = shard * (head_width // HEAD_DIM) + head
            lse = lse_ref[row : row + 1, :]
            delta = row_total(mixed_change.astype(F32) * mixed_ref[here, :])
            query_change = None
            for index, (piece, mask, total_ref) in enumerate(zip(pieces, masks, totals)):
                keys = piece_rows(piece, shard, head * HEAD_DIM)
                values = piece_rows(piece, shard, head_width + head * HEAD_DIM)
                first = 2 * head_width * ((1 - shard) if index % 2 else shard) + head * HEAD_DIM
                key_rows = slice(first, first + HEAD_DIM)
                value_rows = slice(first + head_width, first + head_width + HEAD_DIM)
                probs = jnp.where(mask, jnp.exp(tn(keys, scaled_query) - lse), 0.0)
                score_change = (probs * (tn(values, mixed_change) - delta)).astype(BF)
                term = nn(keys, score_change)
                query_change = term if query_change is None else query_change + term
                total_ref[key_rows, :] += nt(scaled_query, score_change)
                total_ref[value_rows, :] += nt(mixed_change, probs.astype(BF))
            query_change = query_change * factor
            query_folds.append(folded(query_change))
            gq_ref[here, :] = query_change.astype(BF)
        query_parts.append(jnp.concatenate(query_folds, axis=0))
    recv_low[...] = recv_sum[...].astype(BF)
    for shard in range(2):
        gain_part, bias_part = norm_parts[shard]
        packed = [query_parts[shard], jnp.zeros(gain_part.shape, F32), gain_part, bias_part]
        rows.append(token_sum_row(jnp.concatenate(packed, axis=0)))
    sums_ref[...] = rows_of(rows, 0, 8, F32)


def heads_backward_kernel(norm, *refs):
    flag_ref, gq_ref, own_sum, came_ref = refs[:4]
    heads_refs = refs[4:6]
    out_ref, joined_ref, sums_ref = refs[-3:]
    width = gq_ref.shape[0] // 2
    product = None
    rows = []
    for shard in range(2):
        rows_here = own_sum.shape[0]
        first = pl.multiple_of((1 - flag_ref[IN_CORE]) * rows_here + shard * 2 * width, 2 * width)
        came = came_ref[pl.ds(first, 2 * width), :].astype(F32)
        total = own_sum[2 * width * shard : 2 * width * (shard + 1), :] + came
        value_part = folded(total[width:])
        zero = jnp.zeros(value_part.shape, F32)
        rows.append(token_sum_row(jnp.concatenate([zero, value_part, zero, zero], axis=0)))
        first = 3 * width * shard
        joined_ref[first : first + width, :] = gq_ref[shard * width : (shard + 1) * width, :]
        joined_ref[first + width : first + 3 * width, :] = total.astype(BF)
        term = tn(heads_refs[shard][...], joined_ref[first : first + 3 * width, :])
        product = term if product is None else product + term
    low = product.astype(BF)
    out_ref[...] = low
    if norm:
        normed_change = low.astype(F32)
        values = refs[6][...].astype(F32)
        mean, rstd = token_stats(values)
        for part in (normed_change * ((values - mean) * rstd), normed_change):
            rows.append(token_sum_row(folded(part)))
    sums_ref[...] = rows_of(rows, 0, 8, F32)


def attention_weights_kernel(pieces, *refs):
    refs, outs = refs[: -1 - pieces], refs[-1 - pieces :]
    chunks = len(refs) // 4
    width = refs[3].shape[0] // 2
    for index, out_refs in ((1, outs[1:]), (0, outs[:1])):
        heads = merge = None
        for chunk in range(chunks):
            up, joined, normed, merged = refs[4 * chunk : 4 * chunk + 4]
            term = nt(normed[...], joined[3 * width * index : 3 * width * (index + 1), :])
            heads = term if heads is None else heads + term
            term = nt(up[...], merged[width * index : width * (index + 1), :])
            merge = term if merge is None else merge + term
        write_pieces(out_refs, 0, heads)
        write_pieces(out_refs, 3 * width, merge)


def final_kernel(own_ref, recv_ref, change_ref, h_ref, vec_ref, out_ref):
    out_ref[...] = norm_back(own_ref, recv_ref, change_ref, h_ref, vec_ref)[0].T.astype(BF)


def fold_kernel(after_bit, flag, flag_ref, stay_ref, *refs):
    came_refs, (keep_ref, give_ref) = refs[:-2], refs[-2:]
    each = came_refs[0].shape[0]
    bit = flag_ref[flag]
    for out_ref, mine in ((give_ref, 1 - bit), (keep_ref, bit)):
        for place in range(keep_ref.shape[0]):
            high, low = place // after_bit, place % after_bit
            if len(came_refs) == 1:
                index = (2 * high + mine) * after_bit + low
                out_ref[place] = (
                    stay_ref[index].astype(F32) + came_refs[0][index].astype(F32)
                ).astype(BF)
                continue
            first = 2 * high * after_bit + low
            pair = [
                stay_ref[index].astype(F32) + came_refs[index // each][index % each].astype(F32)
                for index in (first, first + after_bit)
            ]
            out_ref[place] = jnp.where(mine == 0, pair[0], pair[1]).astype(BF)


def collect_kernel(layers, counts, flag_ref, *refs):
    give_ref, keep_ref = refs[-2:]
    refs = list(refs[:-2])
    groups = {}
    for name, count in counts:
        groups[name] = refs[:count]
        refs = refs[count:]
    first_section, first_chip = flag_ref[IN_SECTION] == 0, flag_ref[IN_CHIP] == 0
    tables = []
    for layer in range(layers):

        def row(index, name, at=layer):
            return sum(ref[index : index + 1, :] for ref in groups[name, at])

        norm = [
            row(6 + place, "feed", layer - 1) if layer else row(2 + place, "heads")
            for place in range(2)
        ]
        shared = norm + [row(2, "attend"), row(8, "feed"), row(0, "attend"), row(1, "attend")]
        shared = [
            item if not layer and place < 2 else jnp.where(first_chip, item, 0.0)
            for place, item in enumerate(shared)
        ]
        split = []
        for shard in range(2):
            split += [row(2 * place + shard, "feed") for place in range(3)]
            split.append(row(3 + shard, "attend") + row(shard, "heads"))
        tables.append(rows_of(shared, 0, 16, F32) + rows_of(split, 8, 16, F32))
    keep_ref[...] = jnp.where(first_section, tables[0], tables[1])
    give_ref[...] = jnp.where(first_section, tables[1], tables[0])


def call(kernel, outs, args, scratch=(), scalars=(), deps=(), token=False):
    specs = [
        pl.BlockSpec(memory_space=pltpu.SMEM if place in scalars else pltpu.VMEM)
        for place in range(len(args))
    ]
    specs += [pl.BlockSpec(memory_space=pl.ANY)] * len(deps)
    used, given = len(args), len(args) + len(deps)
    outs = list(outs) + [arr((8, 128), F32)] * token

    def run(*refs):
        out_refs, inner = refs[given : given + len(outs)], refs[given + len(outs) :]
        kernel(*refs[:used], *out_refs[: len(outs) - token], *inner)
        if token:
            out_refs[-1][...] = jnp.zeros((8, 128), F32)

    return pl.pallas_call(
        run,
        out_shape=outs,
        in_specs=specs,
        out_specs=[pl.BlockSpec(memory_space=pltpu.VMEM)] * len(outs),
        scratch_shapes=list(scratch),
        compiler_params=pltpu.CompilerParams(vmem_limit_bytes=VMEM_MB * 1024 * 1024),
        cost_estimate=pl.CostEstimate(flops=0, bytes_accessed=0, transcendentals=0),
        name=(kernel.func if isinstance(kernel, partial) else kernel).__name__,
    )(*args, *deps)


def arr(shape, dtype):
    return jax.ShapeDtypeStruct(shape, dtype)


def step_swap(values, axis, step):
    count = lax.axis_size(axis)
    return lax.ppermute(values, axis, [(i, i ^ step) for i in range(count)])


def core_swap(block):
    return step_swap(block, TENSOR, 1)


def both_cores_of(block):
    count = lax.axis_size(TENSOR)
    groups = [[i, i + 1] for i in range(0, count, CORES)]
    return lax.all_gather(block, TENSOR, axis=0, tiled=True, axis_index_groups=groups)


def chip_swap(block):
    return step_swap(block, TENSOR, 2)


def section_swap(block):
    return step_swap(block, SECTION, 1)


class OverRows:
    def __init__(self, flags, own, peers, sections_last=False):
        count = lax.axis_size(DP)
        rows, columns = own.shape[0] // count, own.shape[1]
        steps = []
        while 1 << len(steps) < count:
            steps.append((DP, 1 << len(steps), IN_DP + len(steps)))
        sections = (SECTION, 1, IN_SECTION)
        self.flags = flags
        self.bits = steps[::-1] + [sections]
        self.steps = steps + [sections] if sections_last else [sections] + steps
        shape = (2 * count, rows // 2, columns)
        self.stay = own.reshape(shape)
        each = (shape[0] // len(peers),) + shape[1:]
        self.came = [core_swap(peer.reshape(each)) for peer in peers]

    def advance(self, deps):
        item = self.steps.pop(0)
        axis, step, flag = item
        place = self.bits.index(item)
        self.bits.pop(place)
        half = self.stay.shape[0] // 2
        out = arr((half,) + self.stay.shape[1:], BF)
        keep, give, token = call(
            partial(fold_kernel, 1 << (len(self.bits) - place), flag),
            [out, out],
            [self.flags, self.stay, *self.came],
            scalars=(0,),
            deps=deps,
            token=True,
        )
        self.stay, self.came = keep, [step_swap(give, axis, step)]
        return [token]

    def finish(self):
        return self.stay[0].astype(F32) + self.came[0][0].astype(F32)


def after(value, *others):
    return lax.optimization_barrier((value,) + others)[0]


def other_section(weight, *behind):
    odd = lax.axis_index(DP) & 1
    rows = weight.shape[0] // 2
    half = lax.dynamic_slice_in_dim(weight, odd * rows, rows, 0)
    return section_swap(after(half, *behind))


def both_halves(came, *behind):
    return came, step_swap(after(came, *behind), DP, 1)


def body(
    boundary,
    document_lengths,
    norm_gain,
    norm_bias,
    pair_weight,
    value_weight,
    query_bias,
    value_bias,
    inner_gain,
    inner_bias,
    merge_weight,
    merge_bias,
    second_gain,
    second_bias,
    expand_weight,
    expand_bias,
    hidden_gain,
    hidden_bias,
    shrink_weight,
    shrink_bias,
):
    section = lax.axis_index(SECTION)
    first = section == 0
    place = lax.axis_index(TENSOR)
    core = place & (CORES - 1)
    chip = place >> (CORES - 1)
    block = boundary.shape[2]
    width = boundary.shape[4]
    head_width = value_weight.shape[-1]
    shard = expand_weight.shape[-1]
    chunks = lax.axis_size(TENSOR) // CORES
    size = CORES * block
    row_length = chunks * size
    layers = 2
    row_place = lax.axis_index(DP)
    odd = row_place & 1
    bits = [(row_place >> bit) & 1 for bit in range(max(1, (lax.axis_size(DP) - 1).bit_length()))]
    flags = jnp.stack([section, chip, core] + bits).astype(jnp.int32)
    chip_first = chip == 0

    own = boundary[0, :, :, 0, :]
    mine = jnp.where(first, own[0], own[1])
    away = jnp.where(first, own[1], own[0])
    heads_vector = jnp.concatenate([query_bias[0], value_bias[0], inner_gain[0], inner_bias[0]])
    early = jnp.concatenate(
        [norm_gain, norm_bias, heads_vector[None], jnp.zeros((1, width), F32)], axis=0
    )
    early_came = section_swap(early)
    came = section_swap(after(away, early))
    inputs = jnp.where(first, mine, came)
    inputs_there = chip_swap(inputs)
    cotangent = jnp.where(first, came, mine)
    cotangent_there = chip_swap(after(cotangent, inputs_there))

    def by_chunk(here, there):
        return [jnp.where(chip_first, here, there), jnp.where(chip_first, there, here)]

    inputs = by_chunk(inputs, inputs_there)
    cotangent = by_chunk(cotangent, cotangent_there)

    lengths = jnp.where(first, document_lengths[0, 0], document_lengths[1, 0])
    ends = jnp.cumsum(lengths)
    positions = jnp.arange(row_length, dtype=jnp.int32)
    starts = jnp.max(
        jnp.where(positions[:, None] >= ends[None, :], ends[None, :], 0), axis=-1
    ).astype(jnp.int32)[None]
    starts = [
        lax.dynamic_slice_in_dim(starts, i * size + core * block, block, 1) for i in range(chunks)
    ]

    table = jnp.stack([heads_vector, expand_bias[0], hidden_gain[0], hidden_bias[0]])
    table_peer = core_swap(table)
    vector_columns = arr((width, 128), F32)
    early = call(
        early_kernel,
        [vector_columns] * layers,
        [flags, early, early_came, table_peer, core_swap(early_came)],
        scalars=(0,),
    )
    merge32 = after(merge_weight[0], away).astype(F32)
    shrink32 = after(shrink_weight[0], away).astype(F32)
    shares = jnp.stack(
        [
            jnp.sum(merge32 * inner_gain[0][:, None], axis=0),
            jnp.sum(shrink32 * hidden_gain[0][:, None], axis=0),
            jnp.sum(merge32 * inner_bias[0][:, None], axis=0),
            jnp.sum(shrink32 * hidden_bias[0][:, None], axis=0),
        ]
    )
    shares = shares + core_swap(shares)
    shares_there = chip_swap(shares)
    biases = shares + shares_there
    vectors = jnp.stack(
        [
            merge_bias[0] + biases[2],
            second_gain[0],
            second_bias[0],
            shrink_bias[0] + biases[3],
            shares[0],
            shares_there[0],
            shares[1],
            shares_there[1],
        ]
    )
    vectors = jnp.concatenate(
        [vectors, table[1:], table_peer[1:], jnp.zeros((COLUMNS - 14, width), F32)]
    )
    late = call(
        late_kernel,
        [vector_columns] * layers,
        [flags, vectors, section_swap(after(vectors, inputs_there))],
        scalars=(0,),
    )

    heads_weight = jnp.concatenate(
        [
            pair_weight[0].transpose(1, 2, 0).reshape(2 * head_width, width),
            value_weight[0].T,
        ],
        axis=0,
    )
    given = (heads_weight, merge_weight[0], expand_weight[0], shrink_weight[0])
    given_peer = [core_swap(item) for item in given]
    halves = [other_section(item, away) for item in given]
    there = [both_halves(halves[0], inputs), both_halves(halves[1], inputs_there)]
    there_peer = [[core_swap(item) for item in pair] for pair in there]

    even = odd == 0

    def layer_weight(layer, own, came, other):
        upper = jnp.where(even, came, other)
        lower = jnp.where(even, other, came)
        away = jnp.concatenate([upper, lower], axis=0)
        return jnp.where(first, away, own) if layer else jnp.where(first, own, away)

    def both_cores(index, pair, pair_peer):
        return [
            (
                layer_weight(layer, given[index], *pair),
                layer_weight(layer, given_peer[index], *pair_peer),
            )
            for layer in range(layers)
        ]

    heads_w, merge_w = [both_cores(index, there[index], there_peer[index]) for index in range(2)]

    act = arr((width, block), BF)
    act32 = arr((width, block), F32)
    carried = arr((width + STAT_ROWS, block), BF)
    stats = arr((8, block), F32)
    heads2 = arr((2 * head_width, block), BF)
    keyed = arr((4 * head_width, block), BF)
    keyed32 = arr((4 * head_width, block), F32)
    wide = arr((2 * shard, block), BF)
    few = arr((8, width), F32)
    many = arr((16, width), F32)
    inner_share = 2 * head_width
    hidden_share = 2 * shard

    sums_of = {}

    def note(name, layer, table):
        sums_of.setdefault((name, layer), []).append(table)

    keyed = arr((4 * head_width, block), BF)
    keyed32 = arr((4 * head_width, block), F32)
    kept = []
    previous = []
    for layer in range(layers):
        save = [dict() for i in range(chunks)]
        for i in range(chunks):
            item = save[i]
            outs = [act, act, heads2, keyed]
            if layer:
                lower = kept[-1][i]
                results = call(
                    partial(between_kernel, hidden_share),
                    [act, stats] + outs,
                    [*lower["part"], lower["middle"], late[layer - 1], early[layer], *heads_w[layer]],
                    deps=previous,
                )
                lower.update(t_shrink=results[0], stat_shrink=results[1])
                results = results[2:]
            else:
                results = call(
                    start_kernel,
                    outs,
                    [flags, inputs[i], early[0], *heads_w[0]],
                    scalars=(0,),
                    deps=previous,
                )
            item["h"], item["n"], item["q"] = results[:3]
            item["kv"] = [results[3], both_cores_of(results[3])]
            before = [ref for j in range(i + 1) for ref in save[j]["kv"]]
            chip_part, item["mixed"], item["lse"] = call(
                partial(attention_forward_kernel, i, size),
                [carried, arr((2 * head_width, block), F32), stats],
                [flags, starts[i], item["q"], *merge_w[layer], early[layer], *before],
                scalars=(0,),
                deps=previous,
            )
            item["part"] = (chip_part, chip_swap(chip_part))
            previous = [chip_part]
        if not layer:
            changes = [
                call(
                    cotangent_kernel, [act, stats], [cotangent[i], late[layers - 1]],
                    deps=previous,
                )
                for i in range(chunks)
            ]
            there += [both_halves(halves[2], save[0]["h"]), both_halves(halves[3], save[1]["h"])]
            there_peer += [
                [core_swap(after(item, save[0]["part"][0])) for item in pair] for pair in there[2:]
            ]
            expand_w, shrink_w = [
                both_cores(index, there[index], there_peer[index]) for index in (2, 3)
            ]
        turn_rows = []
        for i in range(chunks):
            item = save[i]
            last = layer + 1 == layers
            results = call(
                partial(feed_forward_kernel, inner_share, last, i),
                [carried, act32, act, act, stats, arr((2 * shard, block), F32)]
                + ([arr((8 * i + 8, block), F32)] if last else []),
                [*item["part"], item["h"], late[layer], *expand_w[layer], *shrink_w[layer]]
                + ([changes[i][0]] + turn_rows if last else []),
                deps=previous,
            )
            chip_part, item["middle"], item["second"] = results[:3]
            item["t_merge"], item["stat_merge"], item["expanded"] = results[3:6]
            if last:
                item["part"] = chip_part
                turn_rows = [results[6]]
            else:
                item["part"] = (chip_part, chip_swap(chip_part))
            previous = [chip_part]
        kept.append(save)
    turn_rows.append(chip_swap(turn_rows[0]))

    top = kept[-1]
    keep, keep_middle, give = call(
        pick_kernel,
        [carried, act32, carried],
        [flags, top[0]["part"], top[1]["part"], top[0]["middle"], top[1]["middle"]],
        scalars=(0,),
        deps=previous,
    )
    output_parts = (keep, chip_swap(after(give, turn_rows[1])), keep_middle)
    previous = [keep]

    feed_sums = [None] * layers
    attend_sums = [None] * layers

    def feed_weights(layer, deps):
        args = []
        for item in kept[layer]:
            args += [item[name] for name in ("up", "shrunk", "change", "second")]
        grad = arr((width, 2 * shard), BF)
        pieces = 4
        piece = arr((width // pieces, 2 * shard), BF)
        own, *peers, token = call(
            partial(feed_weights_kernel, pieces), [grad] + [piece] * pieces, args, deps=deps, token=True
        )
        feed_sums[layer] = OverRows(flags, own, peers)
        return [token]

    def attention_weights(layer, deps):
        args = []
        for item in kept[layer]:
            args += [item[name] for name in ("up_middle", "joined", "n", "merged")]
        grad = arr((width, 4 * head_width), BF)
        pieces = 2
        piece = arr((width // pieces, 4 * head_width), BF)
        own, *peers, token = call(
            partial(attention_weights_kernel, pieces),
            [grad] + [piece] * pieces,
            args,
            deps=deps,
            token=True,
        )
        attend_sums[layer] = OverRows(flags, own, peers, layer > 0)
        return [token]

    def aside(point, deps):
        for kind, layer in ASIDE.get(point, ()):
            if kind == FEED:
                deps = feed_weights(layer, deps)
            elif kind == ATTEND:
                deps = attention_weights(layer, deps)
            else:
                deps = (feed_sums if kind == FEED_STEP else attend_sums)[layer].advance(deps)
        return deps

    for layer in reversed(range(layers)):
        save = kept[layer]
        for i in reversed(range(chunks)):
            item = save[i]
            common = [late[layer], *expand_w[layer], *shrink_w[layer], item["expanded"]]
            outs = [act, wide, wide, many]
            if layer + 1 == layers:
                item["up"], dots = changes[i]
                results = call(
                    partial(turn_kernel, hidden_share, i),
                    outs,
                    [*turn_rows, item["up"], dots] + common,
                    deps=previous,
                )
            else:
                upper = kept[layer + 1][i]
                results = call(
                    partial(layer_back_kernel, hidden_share),
                    [act] + outs,
                    [
                        *upper["part"],
                        upper["middle_change"],
                        upper["h"],
                        early[layer + 1],
                        item["t_shrink"],
                        item["stat_shrink"],
                    ]
                    + common,
                    deps=previous,
                )
                item["up"], results = results[0], results[1:]
            chip_part, item["change"], item["shrunk"], table = results
            note("feed", layer, table)
            item["part"] = (chip_part, chip_swap(chip_part))
            previous = [chip_part]
            previous = aside((FEED, layer, i), previous)
        later = [[] for i in range(chunks)]
        for i in reversed(range(chunks)):
            item = save[i]
            before = [ref for j in range(i + 1) for ref in save[j]["kv"]]
            results = call(
                partial(attention_backward_kernel, i, size, len(later[i])),
                [act, act32, heads2, heads2, keyed32, keyed, few] + [keyed32] * (2 * i),
                [
                    *item["part"],
                    item["up"],
                    item["middle"],
                    item["t_merge"],
                    item["stat_merge"],
                    late[layer],
                    early[layer],
                    flags,
                    starts[i],
                    item["q"],
                    *merge_w[layer],
                    item["mixed"],
                    item["lse"],
                    *before,
                    *later[i],
                ],
                scratch=[
                    pltpu.VMEM((4 * head_width, block), F32),
                    pltpu.VMEM((2 * head_width, block), BF),
                ],
                scalars=(8,),
                deps=previous,
            )
            item["up_middle"], item["middle_change"], gq, item["merged"] = results[:4]
            own_sum, recv_low, table = results[4:7]
            for j in range(i):
                later[j] += results[7 + 2 * j : 9 + 2 * j]
            note("attend", layer, table)
            previous = aside((ATTEND, layer, i), [table])
            chip_part, item["joined"], table = call(
                partial(heads_backward_kernel, not layer),
                [act, arr((6 * head_width, block), BF), few],
                [flags, gq, own_sum, both_cores_of(recv_low), *heads_w[layer]]
                + ([] if layer else [item["h"]]),
                scalars=(0,),
                deps=previous,
            )
            note("heads", layer, table)
            item["part"] = (chip_part, chip_swap(chip_part)) if layer else chip_part
            previous = [chip_part]
            previous = aside((HEAD, layer, i), previous)
        if layer + 1 == layers:
            output = call(
                partial(output_kernel, hidden_share),
                [arr((block, width), BF)],
                [*output_parts, late[layer]],
            )[0]

    previous = attention_weights(0, previous)
    keep, keep_change, keep_h, give = call(
        pick_kernel,
        [act, act32, act, act],
        [flags] + [kept[0][i][name] for name in ("part", "middle_change", "h") for i in range(2)],
        scalars=(0,),
        deps=previous,
    )
    keep_there = chip_swap(give)
    previous = feed_sums[0].advance([keep])
    previous = attend_sums[0].advance(previous)
    counts = [(key, len(tables)) for key, tables in sums_of.items()]
    give, keep_rows = call(
        partial(collect_kernel, layers, counts),
        [many, many],
        [flags] + [table for tables in sums_of.values() for table in tables],
        scalars=(0,),
        deps=previous,
    )
    rows = keep_rows + section_swap(give)
    last = call(
        final_kernel,
        [arr((block, width), BF)],
        [keep, keep_there, keep_change, keep_h, early[0]],
        deps=[give],
    )[0]
    previous = attend_sums[1].advance([last])
    previous = attend_sums[0].advance(previous)
    rows_peer = core_swap(after(rows, *previous))
    rows = jnp.concatenate([rows[:8] + rows_peer[:8], rows[8:12] + rows_peer[12:]])
    waiting = [feed_sums[0], attend_sums[0]]
    step = 1
    while any(item.steps for item in waiting):
        for item in waiting:
            if item.steps:
                previous = item.advance(previous)
                if step < lax.axis_size(DP):
                    rows = rows + step_swap(after(rows, *previous), DP, step)
                    step *= 2
    for item in (attend_sums[1], feed_sums[1]):
        while item.steps:
            previous = item.advance(previous)
    while step < lax.axis_size(DP):
        rows = rows + step_swap(rows, DP, step)
        step *= 2

    def own_layer(reduced):
        halves = [item.finish() for item in reduced]
        given = section_swap(jnp.where(first, halves[1], halves[0]).astype(BF)).astype(F32)
        upper = jnp.where(first, halves[0], given)
        lower = jnp.where(first, given, halves[1])
        return jnp.concatenate([upper, lower], axis=0)

    feed = own_layer(feed_sums)
    attend = own_layer(attend_sums)

    shared = rows[:8]
    shared = (shared + chip_swap(shared))[:6, None]
    split = rows[8:12, None]

    theirs = section_swap(jnp.where(first, output, last))
    kept_here = jnp.where(first, last, output)
    final = jnp.stack(
        [jnp.where(first, kept_here, theirs), jnp.where(first, theirs, kept_here)]
    )[None, :, :, None, :]

    rows_here = attend.shape[0]
    pair_gradient = attend[:, : 2 * head_width].reshape(rows_here, 2, head_width)
    value_gradient = attend[:, 2 * head_width : 3 * head_width]
    merge_gradient = attend[:, 3 * head_width :].T
    shrink_gradient = feed[:, :shard].T
    expand_gradient = feed[:, shard:]
    packed = split[3]

    def packed_part(index):
        return packed[:, index * head_width : (index + 1) * head_width]

    return (
        final,
        shared[0],
        shared[1],
        pair_gradient[None],
        value_gradient[None],
        packed_part(0),
        packed_part(1),
        packed_part(2),
        packed_part(3),
        merge_gradient[None],
        shared[2],
        shared[4],
        shared[5],
        expand_gradient[None],
        split[2],
        split[0],
        split[1],
        shrink_gradient[None],
        shared[3],
    )


def solution(mesh):
    in_specs = (
        P(SECTION, None, TENSOR, DP, None),
        P(None, DP, None),
        P(SECTION, None),
        P(SECTION, None),
        P(SECTION, None, None, TENSOR),
        P(SECTION, None, TENSOR),
        P(SECTION, TENSOR),
        P(SECTION, TENSOR),
        P(SECTION, TENSOR),
        P(SECTION, TENSOR),
        P(SECTION, TENSOR, None),
        P(SECTION, None),
        P(SECTION, None),
        P(SECTION, None),
        P(SECTION, None, TENSOR),
        P(SECTION, TENSOR),
        P(SECTION, TENSOR),
        P(SECTION, TENSOR),
        P(SECTION, TENSOR, None),
        P(SECTION, None),
    )
    out_specs = (
        P(SECTION, None, TENSOR, DP, None),
        P(SECTION, None),
        P(SECTION, None),
        P(SECTION, DP, None, TENSOR),
        P(SECTION, DP, TENSOR),
        P(SECTION, TENSOR),
        P(SECTION, TENSOR),
        P(SECTION, TENSOR),
        P(SECTION, TENSOR),
        P(SECTION, TENSOR, DP),
        P(SECTION, None),
        P(SECTION, None),
        P(SECTION, None),
        P(SECTION, DP, TENSOR),
        P(SECTION, TENSOR),
        P(SECTION, TENSOR),
        P(SECTION, TENSOR),
        P(SECTION, TENSOR, DP),
        P(SECTION, None),
    )
    return jax.shard_map(body, mesh=mesh, in_specs=in_specs, out_specs=out_specs, check_vma=False)
```

```python
from functools import partial

import jax
import jax.numpy as jnp
from jax import lax
from jax.experimental import pallas as pl
from jax.experimental.pallas import tpu as pltpu
from jax.sharding import PartitionSpec as P

HEAD_DIM = 64
EPS = 1e-05
MASKED = -1e30
CORES = 2
STAT_ROWS = 16
BF = jnp.bfloat16
F32 = jnp.float32

NORM_GAIN, NORM_BIAS, HEADS = range(3)
(MERGE_ADD, SECOND_GAIN, SECOND_BIAS, SHRINK_ADD, MERGE_GW, MERGE_GW_THERE, SHRINK_GW,
 SHRINK_GW_THERE, EXPAND_BIAS, HIDDEN_GAIN, HIDDEN_BIAS) = range(11)
SHARD_COLUMNS = 3
COLUMNS = 16
FAR = 1 << 30
SECTION, DP, TENSOR = "section", "dp", "tensor"
IN_SECTION, IN_CHIP, IN_CORE, IN_DP = range(4)
FEED, ATTEND, HEAD, FEED_STEP, ATTEND_STEP = range(5)
ASIDE = {
    (HEAD, 1, 1): [(FEED, 1)],
    (HEAD, 1, 0): [(FEED_STEP, 1)],
    (FEED, 0, 1): [(ATTEND, 1)],
    (FEED, 0, 0): [(FEED, 0), (ATTEND_STEP, 1)],
    (ATTEND, 0, 1): [(FEED_STEP, 0)],
    (HEAD, 0, 1): [(FEED_STEP, 1), (ATTEND_STEP, 1)],
    (ATTEND, 0, 0): [(FEED_STEP, 1)],
}
VMEM_MB = 14


def nn(a, b):
    return lax.dot_general(a, b, (((1,), (0,)), ((), ())), preferred_element_type=F32)


def tn(a, b):
    return lax.dot_general(a, b, (((0,), (0,)), ((), ())), preferred_element_type=F32)


def nt(a, b):
    return lax.dot_general(a, b, (((1,), (1,)), ((), ())), preferred_element_type=F32)


def column(vec_ref, index, start=0, size=None):
    size = vec_ref.shape[0] if size is None else size
    return vec_ref[start : start + size, index : index + 1]


def shard_column(vec_ref, index, shard):
    return column(vec_ref, index + shard * SHARD_COLUMNS)


def head_column(vec_ref, part, shard, size):
    return column(vec_ref, HEADS + shard, part * size, size)


def row_total(values):
    return jnp.sum(values, axis=0, keepdims=True)


def token_stats(values):
    count = values.shape[0]
    mean = row_total(values) / count
    return mean, lax.rsqrt(row_total(values * values) / count - mean * mean + EPS)


def three_parts(row):
    high = row.astype(BF).astype(F32)
    middle = (row - high).astype(BF).astype(F32)
    return [high, middle, row - high - middle]


def rows_of(rows, first, count, dtype):
    width = rows[0].shape[1]
    index = lax.broadcasted_iota(jnp.int32, (count, width), 0)
    total = jnp.zeros((count, width), F32)
    for place, row in enumerate(rows):
        total = jnp.where(index == first + place, row, total)
    return total.astype(dtype)


def sum_parts(block, first):
    return block[first : first + 1] + block[first + 1 : first + 2] + block[first + 2 : first + 3]


def folded(values):
    total = values[:, :128]
    for place in range(128, values.shape[1], 128):
        total = total + values[:, place : place + 128]
    return total


def token_sum_row(part):
    return row_total(part.T)


def gelu_pair(values):
    cdf = 0.5 * (1.0 + lax.erf(values * (0.5**0.5)))
    density = jnp.exp(values * values * -0.5) * 0.3989422804014327
    return values * cdf, cdf + values * density


def gelu(values):
    return values * (0.5 * (1.0 + lax.erf(values * (0.5**0.5))))


def split_product(out_ref, parts, weights, gains):
    count = sum(part.shape[0] for part in parts)
    first_sum = sum(row_total(part) for part in parts)
    second_sum = sum(row_total(part * part) for part in parts)
    mean = first_sum / count
    product = None
    for part, weight, gain in zip(parts, weights, gains):
        term = tn(weight[...], ((part - mean) * gain).astype(BF))
        product = term if product is None else product + term
    low = product.astype(BF)
    width = product.shape[0]
    out_ref[:width, :] = low
    out_ref[width:, :] = rows_of(three_parts(first_sum) + three_parts(second_sum), 0, STAT_ROWS, BF)
    return low, first_sum, second_sum


def whole_stats(firsts, seconds, share):
    count = len(firsts) * share
    mean = sum(firsts) / count
    return mean, lax.rsqrt(sum(seconds) / count - mean * mean + EPS)


def combined(own_ref, recv_ref, vec_ref, first_column, share):
    width = own_ref.shape[0] - STAT_ROWS
    extra = [ref[width:, :].astype(F32) for ref in (own_ref, recv_ref)]
    firsts = [sum_parts(rows, 0) for rows in extra]
    mean, rstd = whole_stats(firsts, [sum_parts(rows, 3) for rows in extra], share)
    total = own_ref[:width, :].astype(F32) + recv_ref[:width, :].astype(F32)
    for place, first in enumerate(firsts):
        total = total + (first / share - mean) * column(vec_ref, first_column + place)
    return total * rstd, mean, rstd


def write_stats(ref, mean, rstd):
    ref[...] = rows_of([mean, rstd], 0, ref.shape[0], F32)


def project(normed, heads, vec_ref, q_ref, kv_ref):
    width = q_ref.shape[0] // 2
    for shard in range(2):
        projected = nn(heads[shard][...], normed)
        query = projected[:width] + head_column(vec_ref, 0, shard, width)
        value = projected[2 * width :] + head_column(vec_ref, 1, shard, width)
        q_ref[shard * width : (shard + 1) * width, :] = query.astype(BF)
        first = 2 * width * shard
        kv_ref[first : first + width, :] = projected[width : 2 * width].astype(BF)
        kv_ref[first + width : first + 2 * width, :] = value.astype(BF)


def norm_and_project(low, vec_ref, heads, h_ref, n_ref, q_ref, kv_ref):
    h_ref[...] = low
    values = low.astype(F32)
    mean, rstd = token_stats(values)
    normed = (
        (values - mean) * rstd * column(vec_ref, NORM_GAIN) + column(vec_ref, NORM_BIAS)
    ).astype(BF)
    n_ref[...] = normed
    project(normed, heads, vec_ref, q_ref, kv_ref)


def first_kernel(flag_ref, mine_ref, came_ref, share_ref, input_ref, change_ref):
    first = flag_ref[IN_SECTION] == 0
    block, width = mine_ref.shape
    mine, came = mine_ref[...], came_ref[...]
    input_ref[:block, :] = jnp.where(first, mine, came)
    change_ref[...] = jnp.where(first, came, mine)
    parts = three_parts(share_ref[...]) + [jnp.zeros(share_ref.shape, F32)]
    input_ref[block:, :] = jnp.concatenate(parts, axis=0).astype(BF)


def chunk_tokens(flag_ref, chunk, here_ref, there_ref, block):
    here, there = here_ref[:block, :], there_ref[:block, :]
    return jnp.where(flag_ref[IN_CHIP] == chunk, here, there).astype(F32).T


def start_kernel(chunk, flag_ref, here_ref, there_ref, vec_ref, heads_own, heads_peer, *outs):
    values = chunk_tokens(flag_ref, chunk, here_ref, there_ref, outs[0].shape[1])
    norm_and_project(values.astype(BF), vec_ref, (heads_own, heads_peer), *outs)


def columns_of(rows, out_ref):
    filled = jnp.concatenate([rows, jnp.zeros((128 - rows.shape[0], rows.shape[1]), F32)], axis=0)
    out_ref[...] = filled.T


def early_kernel(flag_ref, own_ref, came_ref, own_peer_ref, came_peer_ref, *out_refs):
    first = flag_ref[IN_SECTION] == 0
    sets = []
    for ref, peer in ((own_ref, own_peer_ref[0:1, :]), (came_ref, came_peer_ref[2:3, :])):
        rows = [ref[0:1, :], ref[1:2, :], ref[2:3, :], peer]
        sets.append(rows_of(rows, 0, 8, F32))
    columns_of(jnp.where(first, sets[0], sets[1]), out_refs[0])
    columns_of(jnp.where(first, sets[1], sets[0]), out_refs[1])


def late_rows_kernel(
    flag_ref, share_ref, arrived_ref, plain_ref, table_ref, peer_ref, merge_ref, rows_ref, out_ref
):
    def row(ref, index):
        return ref[index : index + 1, :]

    arrived = arrived_ref[arrived_ref.shape[0] - STAT_ROWS :, :].astype(F32)
    there = arrived[:4] + arrived[4:8] + arrived[8:12]
    both = [row(share_ref, index) + there[index : index + 1] for index in (2, 3)]
    rows = [row(plain_ref, 0) + both[0], row(plain_ref, 1), row(plain_ref, 2), row(plain_ref, 3) + both[1]]
    for index in range(2):
        rows += [row(share_ref, index), there[index : index + 1]]
    rows += [row(ref, index) for ref in (table_ref, peer_ref) for index in range(1, 4)]
    rows = rows_of(rows, 0, COLUMNS, F32)
    rows_ref[...] = rows
    half = merge_ref.shape[0] // 2
    first = pl.multiple_of(flag_ref[IN_DP] * half, 16)
    out_ref[:half, :] = merge_ref[pl.ds(first, half), :]
    for place, part in enumerate(three_parts(rows)):
        out_ref[half + place * COLUMNS : half + (place + 1) * COLUMNS, :] = part.astype(BF)


def late_kernel(flag_ref, own_ref, came_ref, *out_refs):
    first = flag_ref[IN_SECTION] == 0
    half = came_ref.shape[0] - 3 * COLUMNS
    parts = came_ref[half:, :].astype(F32)
    came = parts[:COLUMNS] + parts[COLUMNS : 2 * COLUMNS] + parts[2 * COLUMNS :]
    columns_of(jnp.where(first, own_ref[...], came), out_refs[0])
    columns_of(jnp.where(first, came, own_ref[...]), out_refs[1])


def pick_kernel(flag_ref, *refs):
    here = flag_ref[IN_CHIP] == 0
    count = (len(refs) - 1) // 3
    pairs, out_refs = refs[: 2 * count], refs[2 * count :]
    for place in range(count):
        left, right = pairs[2 * place][...], pairs[2 * place + 1][...]
        out_refs[place][...] = jnp.where(here, left, right)
        if not place:
            out_refs[-1][...] = jnp.where(here, right, left)


def between_kernel(
    share,
    own_ref,
    recv_ref,
    middle_ref,
    vec_ref,
    next_ref,
    heads_own,
    heads_peer,
    t_ref,
    stat_ref,
    *outs,
):
    product, mean, rstd = combined(own_ref, recv_ref, vec_ref, SHRINK_GW, share)
    write_stats(stat_ref, mean, rstd)
    t_ref[...] = product.astype(BF)
    low = (middle_ref[...] + (product + column(vec_ref, SHRINK_ADD))).astype(BF)
    norm_and_project(low, next_ref, (heads_own, heads_peer), *outs)


def key_pieces(chunk, size, core, start_row, kv_refs):
    block = start_row.shape[1]
    rows = kv_refs[0].shape[0]
    far = pl.multiple_of((1 - core) * rows, rows)
    pieces = []
    for index in range(chunk + 1):
        own_ref, both_ref = kv_refs[2 * index : 2 * index + 2]
        last = index == chunk
        peer_start = jnp.where(core == 1, start_row, FAR) if last else start_row
        places = (index * size + core * block, index * size + (1 - core) * block)
        pieces.append((own_ref, (0, rows // 2), places[0], start_row, last))
        pieces.append((both_ref, (far + rows // 2, far), places[1], peer_start, False))
    return pieces


def piece_rows(piece, shard, row):
    first = piece[1][shard] + row
    if not isinstance(first, int):
        first = pl.multiple_of(first, HEAD_DIM)
    return piece[0][pl.ds(first, HEAD_DIM), :]


def piece_mask(piece, queries):
    ref, rows, first, start_row, diagonal = piece
    shape = (ref.shape[1], queries)
    rows = lax.broadcasted_iota(jnp.int32, shape, 0)
    mask = first + rows >= start_row
    if diagonal:
        mask = mask & (rows <= lax.broadcasted_iota(jnp.int32, shape, 1))
    return mask


def attention_forward_kernel(chunk, size, *refs):
    flag_ref, start_ref, q_ref, merge_own, merge_peer, vec_ref = refs[:6]
    kv_refs = refs[6 : 8 + 2 * chunk]
    out_ref, mixed_ref, lse_ref = refs[8 + 2 * chunk :]
    width = q_ref.shape[0] // 2
    queries = q_ref.shape[1]
    pieces = key_pieces(chunk, size, flag_ref[IN_CORE], start_ref[...], kv_refs)
    masks = [piece_mask(piece, queries) for piece in pieces]
    heads = width // HEAD_DIM
    lse_rows = []
    for shard in range(2):
        for head in range(heads):
            first = shard * width + head * HEAD_DIM
            base = head * HEAD_DIM
            query = (q_ref[first : first + HEAD_DIM, :] * HEAD_DIM ** (-0.5)).astype(BF)
            scores, values, top = [], [], None
            for piece, mask in zip(pieces, masks):
                keys = piece_rows(piece, shard, base)
                values.append(piece_rows(piece, shard, base + width))
                score = jnp.where(mask, tn(keys, query), MASKED)
                scores.append(score)
                piece_top = jnp.max(score, axis=0, keepdims=True)
                top = piece_top if top is None else jnp.maximum(top, piece_top)
            weights = [jnp.exp(score - top) for score in scores]
            total = sum(row_total(weight) for weight in weights)
            inverse = 1.0 / total
            mixed = None
            for weight, value in zip(weights, values):
                term = nn(value, (weight * inverse).astype(BF))
                mixed = term if mixed is None else mixed + term
            mixed_ref[first : first + HEAD_DIM, :] = mixed
            lse_rows.append(top + jnp.log(total))
    lse_ref[...] = rows_of(lse_rows, 0, lse_ref.shape[0], F32)
    split_product(
        out_ref,
        [mixed_ref[:width, :], mixed_ref[width:, :]],
        [merge_own, merge_peer],
        [head_column(vec_ref, 2, shard, width) for shard in range(2)],
    )


def feed_forward_kernel(share, last, chunk, *refs):
    own_ref, recv_ref, h_ref, vec_ref = refs[:4]
    expand, shrink = refs[4:6], refs[6:8]
    refs = refs[8:]
    if last:
        change_ref, refs = refs[0], refs[1:]
        before_refs, refs = refs[: chunk > 0], refs[chunk > 0 :]
    out_ref, middle_ref, second_ref, t_ref, stat_ref, expanded_ref = refs[:6]
    product, mean, rstd = combined(own_ref, recv_ref, vec_ref, MERGE_GW, share)
    write_stats(stat_ref, mean, rstd)
    t_ref[...] = product.astype(BF)
    middle = h_ref[...].astype(F32) + (product + column(vec_ref, MERGE_ADD))
    middle_ref[...] = middle
    mean, rstd = token_stats(middle)
    second = (
        (middle - mean) * rstd * column(vec_ref, SECOND_GAIN) + column(vec_ref, SECOND_BIAS)
    ).astype(BF)
    second_ref[...] = second
    shard = expanded_ref.shape[0] // 2
    hidden = []
    for index in range(2):
        expanded = tn(expand[index][...], second) + shard_column(vec_ref, EXPAND_BIAS, index)
        expanded_ref[index * shard : (index + 1) * shard, :] = expanded
        hidden.append(gelu(expanded))
    gains = [shard_column(vec_ref, HIDDEN_GAIN, index) for index in range(2)]
    low, first_sum, second_sum = split_product(out_ref, hidden, shrink, gains)
    if last:
        dot = row_total(low.astype(F32) * change_ref[...].astype(F32))
        for ref in before_refs:
            refs[6][: 8 * chunk, :] = ref[...]
        refs[6][8 * chunk :, :] = rows_of([first_sum, second_sum, dot], 0, 8, F32)


def cotangent_kernel(chunk, flag_ref, here_ref, there_ref, vec_ref, low_ref, dots_ref):
    change = chunk_tokens(flag_ref, chunk, here_ref, there_ref, low_ref.shape[1])
    low_ref[...] = change.astype(BF)
    dots_ref[...] = rows_of(
        [row_total(change * column(vec_ref, SHRINK_GW + place)) for place in range(2)], 0, 8, F32
    )


def output_kernel(share, own_ref, recv_ref, middle_ref, vec_ref, out_ref):
    product, mean, rstd = combined(own_ref, recv_ref, vec_ref, SHRINK_GW, share)
    output = middle_ref[...] + (product + column(vec_ref, SHRINK_ADD))
    out_ref[...] = output.T.astype(BF)


def upstream_rows(values, product, vec_ref, first_column, count):
    total = column(vec_ref, first_column) + column(vec_ref, first_column + 1)
    return row_total(values * total) / count, row_total(values * product) / count


def norm_back(own_ref, recv_ref, change_ref, h_ref, vec_ref):
    width = own_ref.shape[0]
    normed_change = own_ref[...].astype(F32) + recv_ref[...].astype(F32)
    values = h_ref[...].astype(F32)
    mean, rstd = token_stats(values)
    unit = (values - mean) * rstd
    scaled = normed_change * column(vec_ref, NORM_GAIN)
    first = row_total(scaled) / width
    second = row_total(scaled * unit) / width
    change = change_ref[...] + rstd * (scaled - first - unit * second)
    return change, (normed_change * unit, normed_change)


def feed_backward(low, first, second, mean, rstd, rows, refs):
    vec_ref = refs[0]
    expand, shrink, expanded_ref = refs[1:3], refs[3:5], refs[5]
    out_ref, change_ref, shrunk_ref, sums_ref = refs[6:]
    shard = expanded_ref.shape[0] // 2
    sums = []
    product = None
    for index in range(2):
        here = slice(index * shard, (index + 1) * shard)
        gain = shard_column(vec_ref, HIDDEN_GAIN, index)
        shrunk_change = nn(shrink[index][...], low)
        hidden, slope = gelu_pair(expanded_ref[here, :])
        unit = (hidden - mean) * rstd
        shrunk_ref[here, :] = (unit * gain + shard_column(vec_ref, HIDDEN_BIAS, index)).astype(BF)
        expanded_change = rstd * (shrunk_change * gain - first - unit * second) * slope
        sums.append(
            [
                token_sum_row(folded(part))
                for part in (shrunk_change * unit, shrunk_change, expanded_change)
            ]
        )
        expanded_low = expanded_change.astype(BF)
        change_ref[here, :] = expanded_low
        term = nn(expand[index][...], expanded_low)
        product = term if product is None else product + term
    out_ref[...] = product.astype(BF)
    rows = [row for pair in zip(*sums) for row in pair] + rows
    sums_ref[...] = rows_of(rows, 0, 16, F32)


def turn_kernel(share, chunk, own_ref, recv_ref, low_ref, dots_ref, *refs):
    at = 8 * chunk
    firsts = [ref[at : at + 1, :] for ref in (own_ref, recv_ref)]
    seconds = [ref[at + 1 : at + 2, :] for ref in (own_ref, recv_ref)]
    mean, rstd = whole_stats(firsts, seconds, share)
    count = 2 * share
    second = own_ref[at + 2 : at + 3, :] + recv_ref[at + 2 : at + 3, :]
    first = 0.0
    for place, total in enumerate(firsts):
        dot = dots_ref[place : place + 1, :]
        first = first + dot
        second = second + (total / share - mean) * dot
    low = low_ref[...]
    zero = jnp.zeros((1, low.shape[0]), F32)
    rows = [zero, zero, token_sum_row(folded(low.astype(F32)))]
    feed_backward(low, first / count, second * rstd / count, mean, rstd, rows, refs)


def layer_back_kernel(
    share, own_ref, recv_ref, change_ref, h_ref, upper_ref, t_ref, stat_ref, *refs
):
    change, rows = norm_back(own_ref, recv_ref, change_ref, h_ref, upper_ref)
    low = change.astype(BF)
    up_ref, refs = refs[6], refs[:6] + refs[7:]
    up_ref[...] = low
    values = low.astype(F32)
    first, second = upstream_rows(values, t_ref[...].astype(F32), refs[0], SHRINK_GW, 2 * share)
    rows = [token_sum_row(folded(part)) for part in rows + (values,)]
    feed_backward(low, first, second, stat_ref[0:1, :], stat_ref[1:2, :], rows, refs)


def write_pieces(refs, first, values):
    rows = refs[0].shape[0]
    for place, ref in enumerate(refs):
        ref[:, first : first + values.shape[1]] = values[place * rows : (place + 1) * rows].astype(BF)


def feed_weights_kernel(pieces, *refs):
    refs, outs = refs[: -1 - pieces], refs[-1 - pieces :]
    shard = outs[0].shape[1] // 2
    chunks = len(refs) // 4
    for index, out_refs in ((1, outs[1:]), (0, outs[:1])):
        here = slice(index * shard, (index + 1) * shard)
        shrink = expand = None
        for chunk in range(chunks):
            up, shrunk, change, second = refs[4 * chunk : 4 * chunk + 4]
            term = nt(up[...], shrunk[here, :])
            shrink = term if shrink is None else shrink + term
            term = nt(second[...], change[here, :])
            expand = term if expand is None else expand + term
        write_pieces(out_refs, 0, shrink)
        write_pieces(out_refs, shard, expand)


def attention_backward_kernel(chunk, size, later, *refs):
    own_part, recv_part, up_ref, middle_ref, t_ref, stat_ref, late_ref, vec_ref = refs[:8]
    flag_ref, start_ref, q_ref, merge_own, merge_peer, mixed_ref, lse_ref = refs[8:15]
    refs = refs[15:]
    kv_refs, refs = refs[: 2 * chunk + 2], refs[2 * chunk + 2 :]
    later_refs, refs = refs[:later], refs[later:]
    low_ref, change_ref, gq_ref, merged_ref = refs[:4]
    own_sum, recv_low, sums_ref = refs[4:7]
    before_sums = refs[7 : 7 + 2 * chunk]
    recv_sum, mixed_change_ref = refs[7 + 2 * chunk :]

    width = up_ref.shape[0]
    second_change = own_part[...].astype(F32) + recv_part[...].astype(F32)
    middle = middle_ref[...]
    mean, rstd = token_stats(middle)
    unit = (middle - mean) * rstd
    scaled = second_change * column(late_ref, SECOND_GAIN)
    first = row_total(scaled) / width
    second = row_total(scaled * unit) / width
    change = up_ref[...].astype(F32) + rstd * (scaled - first - unit * second)
    change_ref[...] = change
    low = change.astype(BF)
    low_ref[...] = low
    rows = [
        token_sum_row(folded(part)) for part in (second_change * unit, second_change, change)
    ]
    first, second = upstream_rows(
        low.astype(F32), t_ref[...].astype(F32), late_ref, MERGE_GW, width
    )
    mean, rstd = stat_ref[0:1, :], stat_ref[1:2, :]
    head_width = q_ref.shape[0] // 2
    norm_parts = []
    for shard, merge in ((0, merge_own), (1, merge_peer)):
        here = slice(shard * head_width, (shard + 1) * head_width)
        gain = head_column(vec_ref, 2, shard, head_width)
        merged_change = nn(merge[...], low)
        unit = (mixed_ref[here, :] - mean) * rstd
        merged_ref[here, :] = (unit * gain + head_column(vec_ref, 3, shard, head_width)).astype(BF)
        norm_parts.append((folded(merged_change * unit), folded(merged_change)))
        mixed_change_ref[here, :] = (
            rstd * (merged_change * gain - first - unit * second)
        ).astype(BF)

    queries = q_ref.shape[1]
    pieces = key_pieces(chunk, size, flag_ref[IN_CORE], start_ref[...], kv_refs)
    masks = [piece_mask(piece, queries) for piece in pieces]
    totals = list(before_sums) + [own_sum, recv_sum]
    for place, ref in enumerate((own_sum, recv_sum)):
        ref[...] = later_refs[place][...] if later else jnp.zeros(ref.shape, F32)
    for ref in before_sums:
        ref[...] = jnp.zeros(ref.shape, F32)
    factor = HEAD_DIM ** (-0.5)
    query_parts = []
    for shard in range(2):
        query_folds = []
        for head in range(head_width // HEAD_DIM):
            place = shard * head_width + head * HEAD_DIM
            here = slice(place, place + HEAD_DIM)
            query = q_ref[here, :]
            scaled_query = (query * factor).astype(BF)
            mixed_change = mixed_change_ref[here, :]
            row = shard * (head_width // HEAD_DIM) + head
            lse = lse_ref[row : row + 1, :]
            delta = row_total(mixed_change.astype(F32) * mixed_ref[here, :])
            query_change = None
            for index, (piece, mask, total_ref) in enumerate(zip(pieces, masks, totals)):
                keys = piece_rows(piece, shard, head * HEAD_DIM)
                values = piece_rows(piece, shard, head_width + head * HEAD_DIM)
                first = 2 * head_width * ((1 - shard) if index % 2 else shard) + head * HEAD_DIM
                key_rows = slice(first, first + HEAD_DIM)
                value_rows = slice(first + head_width, first + head_width + HEAD_DIM)
                probs = jnp.where(mask, jnp.exp(tn(keys, scaled_query) - lse), 0.0)
                score_change = (probs * (tn(values, mixed_change) - delta)).astype(BF)
                term = nn(keys, score_change)
                query_change = term if query_change is None else query_change + term
                total_ref[key_rows, :] += nt(scaled_query, score_change)
                total_ref[value_rows, :] += nt(mixed_change, probs.astype(BF))
            query_change = query_change * factor
            query_folds.append(folded(query_change))
            gq_ref[here, :] = query_change.astype(BF)
        query_parts.append(jnp.concatenate(query_folds, axis=0))
    recv_low[...] = recv_sum[...].astype(BF)
    for shard in range(2):
        gain_part, bias_part = norm_parts[shard]
        packed = [query_parts[shard], jnp.zeros(gain_part.shape, F32), gain_part, bias_part]
        rows.append(token_sum_row(jnp.concatenate(packed, axis=0)))
    sums_ref[...] = rows_of(rows, 0, 8, F32)


def heads_backward_kernel(norm, *refs):
    flag_ref, gq_ref, own_sum, came_ref = refs[:4]
    heads_refs = refs[4:6]
    out_ref, joined_ref, sums_ref = refs[-3:]
    width = gq_ref.shape[0] // 2
    product = None
    rows = []
    for shard in range(2):
        rows_here = own_sum.shape[0]
        first = pl.multiple_of((1 - flag_ref[IN_CORE]) * rows_here + shard * 2 * width, 2 * width)
        came = came_ref[pl.ds(first, 2 * width), :].astype(F32)
        total = own_sum[2 * width * shard : 2 * width * (shard + 1), :] + came
        value_part = folded(total[width:])
        zero = jnp.zeros(value_part.shape, F32)
        rows.append(token_sum_row(jnp.concatenate([zero, value_part, zero, zero], axis=0)))
        first = 3 * width * shard
        joined_ref[first : first + width, :] = gq_ref[shard * width : (shard + 1) * width, :]
        joined_ref[first + width : first + 3 * width, :] = total.astype(BF)
        term = tn(heads_refs[shard][...], joined_ref[first : first + 3 * width, :])
        product = term if product is None else product + term
    low = product.astype(BF)
    out_ref[...] = low
    if norm:
        normed_change = low.astype(F32)
        values = refs[6][...].astype(F32)
        mean, rstd = token_stats(values)
        for part in (normed_change * ((values - mean) * rstd), normed_change):
            rows.append(token_sum_row(folded(part)))
    sums_ref[...] = rows_of(rows, 0, 8, F32)


def attention_weights_kernel(pieces, *refs):
    refs, outs = refs[: -1 - pieces], refs[-1 - pieces :]
    chunks = len(refs) // 4
    width = refs[3].shape[0] // 2
    for index, out_refs in ((1, outs[1:]), (0, outs[:1])):
        heads = merge = None
        for chunk in range(chunks):
            up, joined, normed, merged = refs[4 * chunk : 4 * chunk + 4]
            term = nt(normed[...], joined[3 * width * index : 3 * width * (index + 1), :])
            heads = term if heads is None else heads + term
            term = nt(up[...], merged[width * index : width * (index + 1), :])
            merge = term if merge is None else merge + term
        write_pieces(out_refs, 0, heads)
        write_pieces(out_refs, 3 * width, merge)


def final_kernel(own_ref, recv_ref, change_ref, h_ref, vec_ref, out_ref):
    out_ref[...] = norm_back(own_ref, recv_ref, change_ref, h_ref, vec_ref)[0].T.astype(BF)


def fold_kernel(after_bit, flag, flag_ref, stay_ref, *refs):
    came_refs, (keep_ref, give_ref) = refs[:-2], refs[-2:]
    each = came_refs[0].shape[0]
    bit = flag_ref[flag]
    for out_ref, mine in ((give_ref, 1 - bit), (keep_ref, bit)):
        for place in range(keep_ref.shape[0]):
            high, low = place // after_bit, place % after_bit
            if len(came_refs) == 1:
                index = (2 * high + mine) * after_bit + low
                out_ref[place] = (
                    stay_ref[index].astype(F32) + came_refs[0][index].astype(F32)
                ).astype(BF)
                continue
            first = 2 * high * after_bit + low
            pair = [
                stay_ref[index].astype(F32) + came_refs[index // each][index % each].astype(F32)
                for index in (first, first + after_bit)
            ]
            out_ref[place] = jnp.where(mine == 0, pair[0], pair[1]).astype(BF)


def collect_kernel(layers, counts, flag_ref, *refs):
    give_ref, keep_ref = refs[-2:]
    refs = list(refs[:-2])
    groups = {}
    for name, count in counts:
        groups[name] = refs[:count]
        refs = refs[count:]
    first_section, first_chip = flag_ref[IN_SECTION] == 0, flag_ref[IN_CHIP] == 0
    tables = []
    for layer in range(layers):

        def row(index, name, at=layer):
            return sum(ref[index : index + 1, :] for ref in groups[name, at])

        norm = [
            row(6 + place, "feed", layer - 1) if layer else row(2 + place, "heads")
            for place in range(2)
        ]
        shared = norm + [row(2, "attend"), row(8, "feed"), row(0, "attend"), row(1, "attend")]
        shared = [
            item if not layer and place < 2 else jnp.where(first_chip, item, 0.0)
            for place, item in enumerate(shared)
        ]
        split = []
        for shard in range(2):
            split += [row(2 * place + shard, "feed") for place in range(3)]
            split.append(row(3 + shard, "attend") + row(shard, "heads"))
        tables.append(rows_of(shared, 0, 16, F32) + rows_of(split, 8, 16, F32))
    keep_ref[...] = jnp.where(first_section, tables[0], tables[1])
    give_ref[...] = jnp.where(first_section, tables[1], tables[0])


def call(kernel, outs, args, scratch=(), scalars=(), deps=(), token=False):
    specs = [
        pl.BlockSpec(memory_space=pltpu.SMEM if place in scalars else pltpu.VMEM)
        for place in range(len(args))
    ]
    specs += [pl.BlockSpec(memory_space=pl.ANY)] * len(deps)
    used, given = len(args), len(args) + len(deps)
    outs = list(outs) + [arr((8, 128), F32)] * token

    def run(*refs):
        out_refs, inner = refs[given : given + len(outs)], refs[given + len(outs) :]
        kernel(*refs[:used], *out_refs[: len(outs) - token], *inner)
        if token:
            out_refs[-1][...] = jnp.zeros((8, 128), F32)

    return pl.pallas_call(
        run,
        out_shape=outs,
        in_specs=specs,
        out_specs=[pl.BlockSpec(memory_space=pltpu.VMEM)] * len(outs),
        scratch_shapes=list(scratch),
        compiler_params=pltpu.CompilerParams(vmem_limit_bytes=VMEM_MB * 1024 * 1024),
        cost_estimate=pl.CostEstimate(flops=0, bytes_accessed=0, transcendentals=0),
        name=(kernel.func if isinstance(kernel, partial) else kernel).__name__,
    )(*args, *deps)


def arr(shape, dtype):
    return jax.ShapeDtypeStruct(shape, dtype)


def step_swap(values, axis, step):
    count = lax.axis_size(axis)
    return lax.ppermute(values, axis, [(i, i ^ step) for i in range(count)])


def core_swap(block):
    return step_swap(block, TENSOR, 1)


def both_cores_of(block):
    count = lax.axis_size(TENSOR)
    groups = [[i, i + 1] for i in range(0, count, CORES)]
    return lax.all_gather(block, TENSOR, axis=0, tiled=True, axis_index_groups=groups)


def chip_swap(block):
    return step_swap(block, TENSOR, 2)


def section_swap(block):
    return step_swap(block, SECTION, 1)


class OverRows:
    def __init__(self, flags, own, peers, sections_last=False):
        count = lax.axis_size(DP)
        rows, columns = own.shape[0] // count, own.shape[1]
        steps = []
        while 1 << len(steps) < count:
            steps.append((DP, 1 << len(steps), IN_DP + len(steps)))
        sections = (SECTION, 1, IN_SECTION)
        self.flags = flags
        self.bits = steps[::-1] + [sections]
        self.steps = steps + [sections] if sections_last else [sections] + steps
        shape = (2 * count, rows // 2, columns)
        self.stay = own.reshape(shape)
        each = (shape[0] // len(peers),) + shape[1:]
        self.came = [core_swap(peer.reshape(each)) for peer in peers]

    def advance(self, deps):
        item = self.steps.pop(0)
        axis, step, flag = item
        place = self.bits.index(item)
        self.bits.pop(place)
        half = self.stay.shape[0] // 2
        out = arr((half,) + self.stay.shape[1:], BF)
        keep, give, token = call(
            partial(fold_kernel, 1 << (len(self.bits) - place), flag),
            [out, out],
            [self.flags, self.stay, *self.came],
            scalars=(0,),
            deps=deps,
            token=True,
        )
        self.stay, self.came = keep, [step_swap(give, axis, step)]
        return [token]

    def finish(self):
        return self.stay[0].astype(F32) + self.came[0][0].astype(F32)


def after(value, *others):
    return lax.optimization_barrier((value,) + others)[0]


def other_section(weight, *behind):
    odd = lax.axis_index(DP) & 1
    rows = weight.shape[0] // 2
    half = lax.dynamic_slice_in_dim(weight, odd * rows, rows, 0)
    return section_swap(after(half, *behind))


def both_halves(came, *behind):
    return came, step_swap(after(came, *behind), DP, 1)


def body(
    boundary,
    document_lengths,
    norm_gain,
    norm_bias,
    pair_weight,
    value_weight,
    query_bias,
    value_bias,
    inner_gain,
    inner_bias,
    merge_weight,
    merge_bias,
    second_gain,
    second_bias,
    expand_weight,
    expand_bias,
    hidden_gain,
    hidden_bias,
    shrink_weight,
    shrink_bias,
):
    section = lax.axis_index(SECTION)
    first = section == 0
    place = lax.axis_index(TENSOR)
    core = place & (CORES - 1)
    chip = place >> (CORES - 1)
    block = boundary.shape[2]
    width = boundary.shape[4]
    head_width = value_weight.shape[-1]
    shard = expand_weight.shape[-1]
    chunks = lax.axis_size(TENSOR) // CORES
    size = CORES * block
    row_length = chunks * size
    layers = 2
    row_place = lax.axis_index(DP)
    odd = row_place & 1
    bits = [(row_place >> bit) & 1 for bit in range(max(1, (lax.axis_size(DP) - 1).bit_length()))]
    flags = jnp.stack([section, chip, core] + bits).astype(jnp.int32)

    own = boundary[0, :, :, 0, :]
    mine = lax.dynamic_index_in_dim(own, section, 0, False)
    away = lax.dynamic_index_in_dim(own, 1 - section, 0, False)
    came = section_swap(away)
    heads_vector = jnp.concatenate([query_bias[0], value_bias[0], inner_gain[0], inner_bias[0]])
    early = jnp.concatenate(
        [norm_gain, norm_bias, heads_vector[None], jnp.zeros((1, width), F32)], axis=0
    )
    early_came = section_swap(after(early, away))
    lengths = jnp.where(first, document_lengths[0, 0], document_lengths[1, 0])
    ends = jnp.cumsum(lengths)
    positions = jnp.arange(row_length, dtype=jnp.int32)
    starts = jnp.max(
        jnp.where(positions[:, None] >= ends[None, :], ends[None, :], 0), axis=-1
    ).astype(jnp.int32)[None]
    starts = [
        lax.dynamic_slice_in_dim(starts, i * size + core * block, block, 1) for i in range(chunks)
    ]

    table = jnp.stack([heads_vector, expand_bias[0], hidden_gain[0], hidden_bias[0]])
    table_peer = core_swap(table)
    vector_columns = arr((width, 128), F32)
    early = call(
        early_kernel,
        [vector_columns] * layers,
        [flags, early, early_came, table_peer, core_swap(early_came)],
        scalars=(0,),
    )
    merge32 = after(merge_weight[0], away).astype(F32)
    shrink32 = after(shrink_weight[0], away).astype(F32)
    shares = jnp.stack(
        [
            jnp.sum(merge32 * inner_gain[0][:, None], axis=0),
            jnp.sum(shrink32 * hidden_gain[0][:, None], axis=0),
            jnp.sum(merge32 * inner_bias[0][:, None], axis=0),
            jnp.sum(shrink32 * hidden_bias[0][:, None], axis=0),
        ]
    )
    shares = shares + core_swap(shares)
    inputs, cotangent = call(
        first_kernel,
        [arr((block + STAT_ROWS, width), BF), arr((block, width), BF)],
        [flags, mine, came, shares],
        scalars=(0,),
    )
    inputs_there = chip_swap(inputs)
    cotangent_there = chip_swap(after(cotangent, inputs_there))
    plain = jnp.concatenate([merge_bias, second_gain, second_bias, shrink_bias], axis=0)
    half_merge = merge_weight.shape[1] // 2
    late_rows, merge_given = call(
        late_rows_kernel,
        [arr((COLUMNS, width), F32), arr((half_merge + 3 * COLUMNS, width), BF)],
        [flags, shares, inputs_there, plain, table, table_peer, merge_weight[0]],
        scalars=(0,),
    )

    heads_weight = jnp.concatenate(
        [
            pair_weight[0].transpose(1, 2, 0).reshape(2 * head_width, width),
            value_weight[0].T,
        ],
        axis=0,
    )
    given = (heads_weight, merge_weight[0], expand_weight[0], shrink_weight[0])
    given_peer = [core_swap(item) for item in given]
    heads_half = other_section(given[0], away)
    merge_half = section_swap(merge_given)
    late = call(
        late_kernel, [vector_columns] * layers, [flags, late_rows, merge_half], scalars=(0,)
    )
    expand_half = other_section(given[2], merge_given)
    shrink_whole = section_swap(after(given[3], merge_given))
    there = [both_halves(heads_half, inputs), both_halves(merge_half, inputs_there)]
    there.append(both_halves(expand_half, there[0][1]))
    there_peer = [[core_swap(item) for item in pair] for pair in there[:2]]

    even = odd == 0

    def layer_weight(layer, own, came, other=None):
        if other is None:
            away = came
        else:
            upper = jnp.where(even, came, other)
            lower = jnp.where(even, other, came)
            rows = own.shape[0] // 2
            away = jnp.concatenate([upper[:rows], lower[:rows]], axis=0)
        return jnp.where(first, away, own) if layer else jnp.where(first, own, away)

    def both_cores(index, pair, pair_peer):
        return [
            (
                layer_weight(layer, given[index], *pair),
                layer_weight(layer, given_peer[index], *pair_peer),
            )
            for layer in range(layers)
        ]

    heads_w, merge_w = [both_cores(index, there[index], there_peer[index]) for index in range(2)]

    act = arr((width, block), BF)
    act32 = arr((width, block), F32)
    carried = arr((width + STAT_ROWS, block), BF)
    stats = arr((8, block), F32)
    heads2 = arr((2 * head_width, block), BF)
    keyed = arr((4 * head_width, block), BF)
    keyed32 = arr((4 * head_width, block), F32)
    wide = arr((2 * shard, block), BF)
    few = arr((8, width), F32)
    many = arr((16, width), F32)
    inner_share = 2 * head_width
    hidden_share = 2 * shard

    sums_of = {}

    def note(name, layer, table):
        sums_of.setdefault((name, layer), []).append(table)

    keyed = arr((4 * head_width, block), BF)
    keyed32 = arr((4 * head_width, block), F32)
    changes = [
        call(
            partial(cotangent_kernel, i),
            [act, stats],
            [flags, cotangent, cotangent_there, late[layers - 1]],
            scalars=(0,),
        )
        for i in range(chunks)
    ]
    kept = []
    previous = [dots for low, dots in changes]
    for layer in range(layers):
        save = [dict() for i in range(chunks)]
        for i in range(chunks):
            item = save[i]
            outs = [act, act, heads2, keyed]
            if layer:
                lower = kept[-1][i]
                results = call(
                    partial(between_kernel, hidden_share),
                    [act, stats] + outs,
                    [*lower["part"], lower["middle"], late[layer - 1], early[layer], *heads_w[layer]],
                    deps=previous,
                )
                lower.update(t_shrink=results[0], stat_shrink=results[1])
                results = results[2:]
            else:
                results = call(
                    partial(start_kernel, i),
                    outs,
                    [flags, inputs, inputs_there, early[0], *heads_w[0]],
                    scalars=(0,),
                    deps=previous,
                )
            item["h"], item["n"], item["q"] = results[:3]
            item["kv"] = [results[3], both_cores_of(results[3])]
            before = [ref for j in range(i + 1) for ref in save[j]["kv"]]
            chip_part, item["mixed"], item["lse"] = call(
                partial(attention_forward_kernel, i, size),
                [carried, arr((2 * head_width, block), F32), stats],
                [flags, starts[i], item["q"], *merge_w[layer], early[layer], *before],
                scalars=(0,),
                deps=previous,
            )
            item["part"] = (chip_part, chip_swap(chip_part))
            previous = [chip_part]
        if not layer:
            there.append((after(shrink_whole, save[0]["part"][1]),))
            there_peer.append([core_swap(after(item, save[0]["part"][0])) for item in there[2]])
            there_peer.append([core_swap(there[3][0])])
            expand_w, shrink_w = [
                both_cores(index, there[index], there_peer[index]) for index in (2, 3)
            ]
        turn_rows = []
        for i in range(chunks):
            item = save[i]
            last = layer + 1 == layers
            results = call(
                partial(feed_forward_kernel, inner_share, last, i),
                [carried, act32, act, act, stats, arr((2 * shard, block), F32)]
                + ([arr((8 * i + 8, block), F32)] if last else []),
                [*item["part"], item["h"], late[layer], *expand_w[layer], *shrink_w[layer]]
                + ([changes[i][0]] + turn_rows if last else []),
                deps=previous,
            )
            chip_part, item["middle"], item["second"] = results[:3]
            item["t_merge"], item["stat_merge"], item["expanded"] = results[3:6]
            if last:
                item["part"] = chip_part
                turn_rows = [results[6]]
            else:
                item["part"] = (chip_part, chip_swap(chip_part))
            previous = [chip_part]
        kept.append(save)
    turn_rows.append(chip_swap(turn_rows[0]))

    top = kept[-1]
    keep, keep_middle, give = call(
        pick_kernel,
        [carried, act32, carried],
        [flags, top[0]["part"], top[1]["part"], top[0]["middle"], top[1]["middle"]],
        scalars=(0,),
        deps=previous,
    )
    output_parts = (keep, chip_swap(after(give, turn_rows[1])), keep_middle)
    previous = [keep]

    feed_sums = [None] * layers
    attend_sums = [None] * layers

    def feed_weights(layer, deps):
        args = []
        for item in kept[layer]:
            args += [item[name] for name in ("up", "shrunk", "change", "second")]
        grad = arr((width, 2 * shard), BF)
        pieces = 4
        piece = arr((width // pieces, 2 * shard), BF)
        own, *peers, token = call(
            partial(feed_weights_kernel, pieces), [grad] + [piece] * pieces, args, deps=deps, token=True
        )
        feed_sums[layer] = OverRows(flags, own, peers)
        return [token]

    def attention_weights(layer, deps):
        args = []
        for item in kept[layer]:
            args += [item[name] for name in ("up_middle", "joined", "n", "merged")]
        grad = arr((width, 4 * head_width), BF)
        pieces = 2
        piece = arr((width // pieces, 4 * head_width), BF)
        own, *peers, token = call(
            partial(attention_weights_kernel, pieces),
            [grad] + [piece] * pieces,
            args,
            deps=deps,
            token=True,
        )
        attend_sums[layer] = OverRows(flags, own, peers, layer > 0)
        return [token]

    def aside(point, deps):
        for kind, layer in ASIDE.get(point, ()):
            if kind == FEED:
                deps = feed_weights(layer, deps)
            elif kind == ATTEND:
                deps = attention_weights(layer, deps)
            else:
                deps = (feed_sums if kind == FEED_STEP else attend_sums)[layer].advance(deps)
        return deps

    for layer in reversed(range(layers)):
        save = kept[layer]
        for i in reversed(range(chunks)):
            item = save[i]
            common = [late[layer], *expand_w[layer], *shrink_w[layer], item["expanded"]]
            outs = [act, wide, wide, many]
            if layer + 1 == layers:
                item["up"], dots = changes[i]
                results = call(
                    partial(turn_kernel, hidden_share, i),
                    outs,
                    [*turn_rows, item["up"], dots] + common,
                    deps=previous,
                )
            else:
                upper = kept[layer + 1][i]
                results = call(
                    partial(layer_back_kernel, hidden_share),
                    [act] + outs,
                    [
                        *upper["part"],
                        upper["middle_change"],
                        upper["h"],
                        early[layer + 1],
                        item["t_shrink"],
                        item["stat_shrink"],
                    ]
                    + common,
                    deps=previous,
                )
                item["up"], results = results[0], results[1:]
            chip_part, item["change"], item["shrunk"], table = results
            note("feed", layer, table)
            item["part"] = (chip_part, chip_swap(chip_part))
            previous = [chip_part]
            previous = aside((FEED, layer, i), previous)
        later = [[] for i in range(chunks)]
        for i in reversed(range(chunks)):
            item = save[i]
            before = [ref for j in range(i + 1) for ref in save[j]["kv"]]
            results = call(
                partial(attention_backward_kernel, i, size, len(later[i])),
                [act, act32, heads2, heads2, keyed32, keyed, few] + [keyed32] * (2 * i),
                [
                    *item["part"],
                    item["up"],
                    item["middle"],
                    item["t_merge"],
                    item["stat_merge"],
                    late[layer],
                    early[layer],
                    flags,
                    starts[i],
                    item["q"],
                    *merge_w[layer],
                    item["mixed"],
                    item["lse"],
                    *before,
                    *later[i],
                ],
                scratch=[
                    pltpu.VMEM((4 * head_width, block), F32),
                    pltpu.VMEM((2 * head_width, block), BF),
                ],
                scalars=(8,),
                deps=previous,
            )
            item["up_middle"], item["middle_change"], gq, item["merged"] = results[:4]
            own_sum, recv_low, table = results[4:7]
            for j in range(i):
                later[j] += results[7 + 2 * j : 9 + 2 * j]
            note("attend", layer, table)
            previous = aside((ATTEND, layer, i), [table])
            chip_part, item["joined"], table = call(
                partial(heads_backward_kernel, not layer),
                [act, arr((6 * head_width, block), BF), few],
                [flags, gq, own_sum, both_cores_of(recv_low), *heads_w[layer]]
                + ([] if layer else [item["h"]]),
                scalars=(0,),
                deps=previous,
            )
            note("heads", layer, table)
            item["part"] = (chip_part, chip_swap(chip_part)) if layer else chip_part
            previous = [chip_part]
            previous = aside((HEAD, layer, i), previous)
        if layer + 1 == layers:
            output = call(
                partial(output_kernel, hidden_share),
                [arr((block, width), BF)],
                [*output_parts, late[layer]],
            )[0]

    previous = attention_weights(0, previous)
    keep, keep_change, keep_h, give = call(
        pick_kernel,
        [act, act32, act, act],
        [flags] + [kept[0][i][name] for name in ("part", "middle_change", "h") for i in range(2)],
        scalars=(0,),
        deps=previous,
    )
    keep_there = chip_swap(give)
    previous = feed_sums[0].advance([keep])
    previous = attend_sums[0].advance(previous)
    counts = [(key, len(tables)) for key, tables in sums_of.items()]
    give, keep_rows = call(
        partial(collect_kernel, layers, counts),
        [many, many],
        [flags] + [table for tables in sums_of.values() for table in tables],
        scalars=(0,),
        deps=previous,
    )
    rows = keep_rows + section_swap(give)
    last = call(
        final_kernel,
        [arr((block, width), BF)],
        [keep, keep_there, keep_change, keep_h, early[0]],
        deps=[give],
    )[0]
    previous = attend_sums[1].advance([last])
    previous = attend_sums[0].advance(previous)
    rows_peer = core_swap(after(rows, *previous))
    rows = jnp.concatenate([rows[:8] + rows_peer[:8], rows[8:12] + rows_peer[12:]])
    waiting = [feed_sums[0], attend_sums[0]]
    step = 1
    while any(item.steps for item in waiting):
        for item in waiting:
            if item.steps:
                previous = item.advance(previous)
                if step < lax.axis_size(DP):
                    rows = rows + step_swap(after(rows, *previous), DP, step)
                    step *= 2
    for item in (attend_sums[1], feed_sums[1]):
        while item.steps:
            previous = item.advance(previous)
    while step < lax.axis_size(DP):
        rows = rows + step_swap(rows, DP, step)
        step *= 2

    def own_layer(reduced):
        halves = [item.finish() for item in reduced]
        given = section_swap(jnp.where(first, halves[1], halves[0]).astype(BF)).astype(F32)
        upper = jnp.where(first, halves[0], given)
        lower = jnp.where(first, given, halves[1])
        return jnp.concatenate([upper, lower], axis=0)

    feed = own_layer(feed_sums)
    attend = own_layer(attend_sums)

    shared = rows[:8]
    shared = (shared + chip_swap(shared))[:6, None]
    split = rows[8:12, None]

    theirs = section_swap(jnp.where(first, output, last))
    kept_here = jnp.where(first, last, output)
    final = jnp.stack(
        [jnp.where(first, kept_here, theirs), jnp.where(first, theirs, kept_here)]
    )[None, :, :, None, :]

    rows_here = attend.shape[0]
    pair_gradient = attend[:, : 2 * head_width].reshape(rows_here, 2, head_width)
    value_gradient = attend[:, 2 * head_width : 3 * head_width]
    merge_gradient = attend[:, 3 * head_width :].T
    shrink_gradient = feed[:, :shard].T
    expand_gradient = feed[:, shard:]
    packed = split[3]

    def packed_part(index):
        return packed[:, index * head_width : (index + 1) * head_width]

    return (
        final,
        shared[0],
        shared[1],
        pair_gradient[None],
        value_gradient[None],
        packed_part(0),
        packed_part(1),
        packed_part(2),
        packed_part(3),
        merge_gradient[None],
        shared[2],
        shared[4],
        shared[5],
        expand_gradient[None],
        split[2],
        split[0],
        split[1],
        shrink_gradient[None],
        shared[3],
    )


def solution(mesh):
    in_specs = (
        P(SECTION, None, TENSOR, DP, None),
        P(None, DP, None),
        P(SECTION, None),
        P(SECTION, None),
        P(SECTION, None, None, TENSOR),
        P(SECTION, None, TENSOR),
        P(SECTION, TENSOR),
        P(SECTION, TENSOR),
        P(SECTION, TENSOR),
        P(SECTION, TENSOR),
        P(SECTION, TENSOR, None),
        P(SECTION, None),
        P(SECTION, None),
        P(SECTION, None),
        P(SECTION, None, TENSOR),
        P(SECTION, TENSOR),
        P(SECTION, TENSOR),
        P(SECTION, TENSOR),
        P(SECTION, TENSOR, None),
        P(SECTION, None),
    )
    out_specs = (
        P(SECTION, None, TENSOR, DP, None),
        P(SECTION, None),
        P(SECTION, None),
        P(SECTION, DP, None, TENSOR),
        P(SECTION, DP, TENSOR),
        P(SECTION, TENSOR),
        P(SECTION, TENSOR),
        P(SECTION, TENSOR),
        P(SECTION, TENSOR),
        P(SECTION, TENSOR, DP),
        P(SECTION, None),
        P(SECTION, None),
        P(SECTION, None),
        P(SECTION, DP, TENSOR),
        P(SECTION, TENSOR),
        P(SECTION, TENSOR),
        P(SECTION, TENSOR),
        P(SECTION, TENSOR, DP),
        P(SECTION, None),
    )
    return jax.shard_map(body, mesh=mesh, in_specs=in_specs, out_specs=out_specs, check_vma=False)
```

```python
from functools import partial

import jax
import jax.numpy as jnp
from jax import lax
from jax.experimental import pallas as pl
from jax.experimental.pallas import tpu as pltpu
from jax.sharding import PartitionSpec as P

HEAD_DIM = 64
EPS = 1e-05
MASKED = -1e30
CORES = 2
STAT_ROWS = 16
BF = jnp.bfloat16
F32 = jnp.float32

NORM_GAIN, NORM_BIAS, HEADS = range(3)
(MERGE_ADD, SECOND_GAIN, SECOND_BIAS, SHRINK_ADD, MERGE_GW, MERGE_GW_THERE, SHRINK_GW,
 SHRINK_GW_THERE, EXPAND_BIAS, HIDDEN_GAIN, HIDDEN_BIAS) = range(11)
SHARD_COLUMNS = 3
COLUMNS = 16
FAR = 1 << 30
SECTION, DP, TENSOR = "section", "dp", "tensor"
IN_SECTION, IN_CHIP, IN_CORE, IN_DP = range(4)
FEED, ATTEND, HEAD, FEED_STEP, ATTEND_STEP = range(5)
ASIDE = {
    (HEAD, 1, 1): [(FEED, 1)],
    (HEAD, 1, 0): [(FEED_STEP, 1)],
    (FEED, 0, 1): [(ATTEND, 1)],
    (FEED, 0, 0): [(FEED, 0), (ATTEND_STEP, 1)],
    (ATTEND, 0, 1): [(FEED_STEP, 0)],
    (HEAD, 0, 1): [(FEED_STEP, 1), (ATTEND_STEP, 1)],
}
VMEM_MB = 14


def nn(a, b):
    return lax.dot_general(a, b, (((1,), (0,)), ((), ())), preferred_element_type=F32)


def tn(a, b):
    return lax.dot_general(a, b, (((0,), (0,)), ((), ())), preferred_element_type=F32)


def nt(a, b):
    return lax.dot_general(a, b, (((1,), (1,)), ((), ())), preferred_element_type=F32)


def column(vec_ref, index, start=0, size=None):
    size = vec_ref.shape[0] if size is None else size
    return vec_ref[start : start + size, index : index + 1]


def shard_column(vec_ref, index, shard):
    return column(vec_ref, index + shard * SHARD_COLUMNS)


def head_column(vec_ref, part, shard, size):
    return column(vec_ref, HEADS + shard, part * size, size)


def row_total(values):
    return jnp.sum(values, axis=0, keepdims=True)


def token_stats(values):
    count = values.shape[0]
    mean = row_total(values) / count
    return mean, lax.rsqrt(row_total(values * values) / count - mean * mean + EPS)


def three_parts(row):
    high = row.astype(BF).astype(F32)
    middle = (row - high).astype(BF).astype(F32)
    return [high, middle, row - high - middle]


def rows_of(rows, first, count, dtype):
    width = rows[0].shape[1]
    index = lax.broadcasted_iota(jnp.int32, (count, width), 0)
    total = jnp.zeros((count, width), F32)
    for place, row in enumerate(rows):
        total = jnp.where(index == first + place, row, total)
    return total.astype(dtype)


def sum_parts(block, first):
    return block[first : first + 1] + block[first + 1 : first + 2] + block[first + 2 : first + 3]


def folded(values):
    total = values[:, :128]
    for place in range(128, values.shape[1], 128):
        total = total + values[:, place : place + 128]
    return total


def token_sum_row(part):
    return row_total(part.T)


def gelu_pair(values):
    cdf = 0.5 * (1.0 + lax.erf(values * (0.5**0.5)))
    density = jnp.exp(values * values * -0.5) * 0.3989422804014327
    return values * cdf, cdf + values * density


def gelu(values):
    return values * (0.5 * (1.0 + lax.erf(values * (0.5**0.5))))


def split_product(out_ref, parts, weights, gains):
    count = sum(part.shape[0] for part in parts)
    first_sum = sum(row_total(part) for part in parts)
    second_sum = sum(row_total(part * part) for part in parts)
    mean = first_sum / count
    product = None
    for part, weight, gain in zip(parts, weights, gains):
        term = tn(weight[...], ((part - mean) * gain).astype(BF))
        product = term if product is None else product + term
    low = product.astype(BF)
    width = product.shape[0]
    out_ref[:width, :] = low
    out_ref[width:, :] = rows_of(three_parts(first_sum) + three_parts(second_sum), 0, STAT_ROWS, BF)
    return low, first_sum, second_sum


def whole_stats(firsts, seconds, share):
    count = len(firsts) * share
    mean = sum(firsts) / count
    return mean, lax.rsqrt(sum(seconds) / count - mean * mean + EPS)


def combined(own_ref, recv_ref, vec_ref, first_column, share):
    width = own_ref.shape[0] - STAT_ROWS
    extra = [ref[width:, :].astype(F32) for ref in (own_ref, recv_ref)]
    firsts = [sum_parts(rows, 0) for rows in extra]
    mean, rstd = whole_stats(firsts, [sum_parts(rows, 3) for rows in extra], share)
    total = own_ref[:width, :].astype(F32) + recv_ref[:width, :].astype(F32)
    for place, first in enumerate(firsts):
        total = total + (first / share - mean) * column(vec_ref, first_column + place)
    return total * rstd, mean, rstd


def write_stats(ref, mean, rstd):
    ref[...] = rows_of([mean, rstd], 0, ref.shape[0], F32)


def project(normed, heads, vec_ref, q_ref, kv_ref):
    width = q_ref.shape[0] // 2
    for shard in range(2):
        projected = nn(heads[shard][...], normed)
        query = projected[:width] + head_column(vec_ref, 0, shard, width)
        value = projected[2 * width :] + head_column(vec_ref, 1, shard, width)
        q_ref[shard * width : (shard + 1) * width, :] = query.astype(BF)
        first = 2 * width * shard
        kv_ref[first : first + width, :] = projected[width : 2 * width].astype(BF)
        kv_ref[first + width : first + 2 * width, :] = value.astype(BF)


def norm_and_project(low, vec_ref, heads, h_ref, n_ref, q_ref, kv_ref):
    h_ref[...] = low
    values = low.astype(F32)
    mean, rstd = token_stats(values)
    normed = (
        (values - mean) * rstd * column(vec_ref, NORM_GAIN) + column(vec_ref, NORM_BIAS)
    ).astype(BF)
    n_ref[...] = normed
    project(normed, heads, vec_ref, q_ref, kv_ref)


def first_kernel(flag_ref, mine_ref, came_ref, share_ref, input_ref, change_ref):
    first = flag_ref[IN_SECTION] == 0
    block, width = mine_ref.shape
    mine, came = mine_ref[...], came_ref[...]
    input_ref[:block, :] = jnp.where(first, mine, came)
    change_ref[...] = jnp.where(first, came, mine)
    parts = three_parts(share_ref[...]) + [jnp.zeros(share_ref.shape, F32)]
    input_ref[block:, :] = jnp.concatenate(parts, axis=0).astype(BF)


def chunk_tokens(flag_ref, chunk, here_ref, there_ref, block):
    here, there = here_ref[:block, :], there_ref[:block, :]
    return jnp.where(flag_ref[IN_CHIP] == chunk, here, there).astype(F32).T


def start_kernel(chunk, flag_ref, here_ref, there_ref, vec_ref, heads_own, heads_peer, *outs):
    values = chunk_tokens(flag_ref, chunk, here_ref, there_ref, outs[0].shape[1])
    norm_and_project(values.astype(BF), vec_ref, (heads_own, heads_peer), *outs)


def columns_of(rows, out_ref):
    filled = jnp.concatenate([rows, jnp.zeros((128 - rows.shape[0], rows.shape[1]), F32)], axis=0)
    out_ref[...] = filled.T


def early_kernel(flag_ref, own_ref, came_ref, own_peer_ref, came_peer_ref, *out_refs):
    first = flag_ref[IN_SECTION] == 0
    sets = []
    for ref, peer in ((own_ref, own_peer_ref[0:1, :]), (came_ref, came_peer_ref[2:3, :])):
        rows = [ref[0:1, :], ref[1:2, :], ref[2:3, :], peer]
        sets.append(rows_of(rows, 0, 8, F32))
    columns_of(jnp.where(first, sets[0], sets[1]), out_refs[0])
    columns_of(jnp.where(first, sets[1], sets[0]), out_refs[1])


def late_rows_kernel(
    flag_ref, share_ref, arrived_ref, plain_ref, table_ref, peer_ref, merge_ref, rows_ref, out_ref
):
    def row(ref, index):
        return ref[index : index + 1, :]

    arrived = arrived_ref[arrived_ref.shape[0] - STAT_ROWS :, :].astype(F32)
    there = arrived[:4] + arrived[4:8] + arrived[8:12]
    both = [row(share_ref, index) + there[index : index + 1] for index in (2, 3)]
    rows = [row(plain_ref, 0) + both[0], row(plain_ref, 1), row(plain_ref, 2), row(plain_ref, 3) + both[1]]
    for index in range(2):
        rows += [row(share_ref, index), there[index : index + 1]]
    rows += [row(ref, index) for ref in (table_ref, peer_ref) for index in range(1, 4)]
    rows = rows_of(rows, 0, COLUMNS, F32)
    rows_ref[...] = rows
    half = merge_ref.shape[0] // 2
    first = pl.multiple_of(flag_ref[IN_DP] * half, 16)
    out_ref[:half, :] = merge_ref[pl.ds(first, half), :]
    for place, part in enumerate(three_parts(rows)):
        out_ref[half + place * COLUMNS : half + (place + 1) * COLUMNS, :] = part.astype(BF)


def late_kernel(flag_ref, own_ref, came_ref, *out_refs):
    first = flag_ref[IN_SECTION] == 0
    half = came_ref.shape[0] - 3 * COLUMNS
    parts = came_ref[half:, :].astype(F32)
    came = parts[:COLUMNS] + parts[COLUMNS : 2 * COLUMNS] + parts[2 * COLUMNS :]
    columns_of(jnp.where(first, own_ref[...], came), out_refs[0])
    columns_of(jnp.where(first, came, own_ref[...]), out_refs[1])


def pick_kernel(flag_ref, *refs):
    here = flag_ref[IN_CHIP] == 0
    count = (len(refs) - 1) // 3
    pairs, out_refs = refs[: 2 * count], refs[2 * count :]
    for place in range(count):
        left, right = pairs[2 * place][...], pairs[2 * place + 1][...]
        out_refs[place][...] = jnp.where(here, left, right)
        if not place:
            out_refs[-1][...] = jnp.where(here, right, left)


def between_kernel(
    share,
    own_ref,
    recv_ref,
    middle_ref,
    vec_ref,
    next_ref,
    heads_own,
    heads_peer,
    t_ref,
    stat_ref,
    *outs,
):
    product, mean, rstd = combined(own_ref, recv_ref, vec_ref, SHRINK_GW, share)
    write_stats(stat_ref, mean, rstd)
    t_ref[...] = product.astype(BF)
    low = (middle_ref[...] + (product + column(vec_ref, SHRINK_ADD))).astype(BF)
    norm_and_project(low, next_ref, (heads_own, heads_peer), *outs)


def key_pieces(chunk, size, core, start_row, kv_refs):
    block = start_row.shape[1]
    rows = kv_refs[0].shape[0]
    far = pl.multiple_of((1 - core) * rows, rows)
    pieces = []
    for index in range(chunk + 1):
        own_ref, both_ref = kv_refs[2 * index : 2 * index + 2]
        last = index == chunk
        peer_start = jnp.where(core == 1, start_row, FAR) if last else start_row
        places = (index * size + core * block, index * size + (1 - core) * block)
        pieces.append((own_ref, (0, rows // 2), places[0], start_row, last))
        pieces.append((both_ref, (far + rows // 2, far), places[1], peer_start, False))
    return pieces


def piece_rows(piece, shard, row):
    first = piece[1][shard] + row
    if not isinstance(first, int):
        first = pl.multiple_of(first, HEAD_DIM)
    return piece[0][pl.ds(first, HEAD_DIM), :]


def piece_mask(piece, queries):
    ref, rows, first, start_row, diagonal = piece
    shape = (ref.shape[1], queries)
    rows = lax.broadcasted_iota(jnp.int32, shape, 0)
    mask = first + rows >= start_row
    if diagonal:
        mask = mask & (rows <= lax.broadcasted_iota(jnp.int32, shape, 1))
    return mask


def attention_forward_kernel(chunk, size, *refs):
    flag_ref, start_ref, q_ref, merge_own, merge_peer, vec_ref = refs[:6]
    kv_refs = refs[6 : 8 + 2 * chunk]
    out_ref, mixed_ref, lse_ref = refs[8 + 2 * chunk :]
    width = q_ref.shape[0] // 2
    queries = q_ref.shape[1]
    pieces = key_pieces(chunk, size, flag_ref[IN_CORE], start_ref[...], kv_refs)
    masks = [piece_mask(piece, queries) for piece in pieces]
    heads = width // HEAD_DIM
    lse_rows = []
    for shard in range(2):
        for head in range(heads):
            first = shard * width + head * HEAD_DIM
            base = head * HEAD_DIM
            query = (q_ref[first : first + HEAD_DIM, :] * HEAD_DIM ** (-0.5)).astype(BF)
            scores, values, top = [], [], None
            for piece, mask in zip(pieces, masks):
                keys = piece_rows(piece, shard, base)
                values.append(piece_rows(piece, shard, base + width))
                score = jnp.where(mask, tn(keys, query), MASKED)
                scores.append(score)
                piece_top = jnp.max(score, axis=0, keepdims=True)
                top = piece_top if top is None else jnp.maximum(top, piece_top)
            weights = [jnp.exp(score - top) for score in scores]
            total = sum(row_total(weight) for weight in weights)
            inverse = 1.0 / total
            mixed = None
            for weight, value in zip(weights, values):
                term = nn(value, (weight * inverse).astype(BF))
                mixed = term if mixed is None else mixed + term
            mixed_ref[first : first + HEAD_DIM, :] = mixed
            lse_rows.append(top + jnp.log(total))
    lse_ref[...] = rows_of(lse_rows, 0, lse_ref.shape[0], F32)
    split_product(
        out_ref,
        [mixed_ref[:width, :], mixed_ref[width:, :]],
        [merge_own, merge_peer],
        [head_column(vec_ref, 2, shard, width) for shard in range(2)],
    )


def feed_forward_kernel(share, last, chunk, *refs):
    own_ref, recv_ref, h_ref, vec_ref = refs[:4]
    expand, shrink = refs[4:6], refs[6:8]
    refs = refs[8:]
    if last:
        change_ref, refs = refs[0], refs[1:]
        before_refs, refs = refs[: chunk > 0], refs[chunk > 0 :]
    out_ref, middle_ref, second_ref, t_ref, stat_ref, expanded_ref = refs[:6]
    product, mean, rstd = combined(own_ref, recv_ref, vec_ref, MERGE_GW, share)
    write_stats(stat_ref, mean, rstd)
    t_ref[...] = product.astype(BF)
    middle = h_ref[...].astype(F32) + (product + column(vec_ref, MERGE_ADD))
    middle_ref[...] = middle
    mean, rstd = token_stats(middle)
    second = (
        (middle - mean) * rstd * column(vec_ref, SECOND_GAIN) + column(vec_ref, SECOND_BIAS)
    ).astype(BF)
    second_ref[...] = second
    shard = expanded_ref.shape[0] // 2
    hidden = []
    for index in range(2):
        expanded = tn(expand[index][...], second) + shard_column(vec_ref, EXPAND_BIAS, index)
        expanded_ref[index * shard : (index + 1) * shard, :] = expanded
        hidden.append(gelu(expanded))
    gains = [shard_column(vec_ref, HIDDEN_GAIN, index) for index in range(2)]
    low, first_sum, second_sum = split_product(out_ref, hidden, shrink, gains)
    if last:
        dot = row_total(low.astype(F32) * change_ref[...].astype(F32))
        for ref in before_refs:
            refs[6][: 8 * chunk, :] = ref[...]
        refs[6][8 * chunk :, :] = rows_of([first_sum, second_sum, dot], 0, 8, F32)


def cotangent_kernel(chunk, flag_ref, here_ref, there_ref, vec_ref, low_ref, dots_ref):
    change = chunk_tokens(flag_ref, chunk, here_ref, there_ref, low_ref.shape[1])
    low_ref[...] = change.astype(BF)
    dots_ref[...] = rows_of(
        [row_total(change * column(vec_ref, SHRINK_GW + place)) for place in range(2)], 0, 8, F32
    )


def output_kernel(share, own_ref, recv_ref, middle_ref, vec_ref, out_ref):
    product, mean, rstd = combined(own_ref, recv_ref, vec_ref, SHRINK_GW, share)
    output = middle_ref[...] + (product + column(vec_ref, SHRINK_ADD))
    out_ref[...] = output.T.astype(BF)


def upstream_rows(values, product, vec_ref, first_column, count):
    total = column(vec_ref, first_column) + column(vec_ref, first_column + 1)
    return row_total(values * total) / count, row_total(values * product) / count


def norm_back(own_ref, recv_ref, change_ref, h_ref, vec_ref):
    width = own_ref.shape[0]
    normed_change = own_ref[...].astype(F32) + recv_ref[...].astype(F32)
    values = h_ref[...].astype(F32)
    mean, rstd = token_stats(values)
    unit = (values - mean) * rstd
    scaled = normed_change * column(vec_ref, NORM_GAIN)
    first = row_total(scaled) / width
    second = row_total(scaled * unit) / width
    change = change_ref[...] + rstd * (scaled - first - unit * second)
    return change, (normed_change * unit, normed_change)


def feed_backward(low, first, second, mean, rstd, rows, refs):
    vec_ref = refs[0]
    expand, shrink, expanded_ref = refs[1:3], refs[3:5], refs[5]
    out_ref, change_ref, shrunk_ref, sums_ref = refs[6:]
    shard = expanded_ref.shape[0] // 2
    sums = []
    product = None
    for index in range(2):
        here = slice(index * shard, (index + 1) * shard)
        gain = shard_column(vec_ref, HIDDEN_GAIN, index)
        shrunk_change = nn(shrink[index][...], low)
        hidden, slope = gelu_pair(expanded_ref[here, :])
        unit = (hidden - mean) * rstd
        shrunk_ref[here, :] = (unit * gain + shard_column(vec_ref, HIDDEN_BIAS, index)).astype(BF)
        expanded_change = rstd * (shrunk_change * gain - first - unit * second) * slope
        sums.append(
            [
                token_sum_row(folded(part))
                for part in (shrunk_change * unit, shrunk_change, expanded_change)
            ]
        )
        expanded_low = expanded_change.astype(BF)
        change_ref[here, :] = expanded_low
        term = nn(expand[index][...], expanded_low)
        product = term if product is None else product + term
    out_ref[...] = product.astype(BF)
    rows = [row for pair in zip(*sums) for row in pair] + rows
    sums_ref[...] = rows_of(rows, 0, 16, F32)


def turn_kernel(share, chunk, own_ref, recv_ref, low_ref, dots_ref, *refs):
    at = 8 * chunk
    firsts = [ref[at : at + 1, :] for ref in (own_ref, recv_ref)]
    seconds = [ref[at + 1 : at + 2, :] for ref in (own_ref, recv_ref)]
    mean, rstd = whole_stats(firsts, seconds, share)
    count = 2 * share
    second = own_ref[at + 2 : at + 3, :] + recv_ref[at + 2 : at + 3, :]
    first = 0.0
    for place, total in enumerate(firsts):
        dot = dots_ref[place : place + 1, :]
        first = first + dot
        second = second + (total / share - mean) * dot
    low = low_ref[...]
    zero = jnp.zeros((1, low.shape[0]), F32)
    rows = [zero, zero, token_sum_row(folded(low.astype(F32)))]
    feed_backward(low, first / count, second * rstd / count, mean, rstd, rows, refs)


def layer_back_kernel(
    share, own_ref, recv_ref, change_ref, h_ref, upper_ref, t_ref, stat_ref, *refs
):
    change, rows = norm_back(own_ref, recv_ref, change_ref, h_ref, upper_ref)
    low = change.astype(BF)
    up_ref, refs = refs[6], refs[:6] + refs[7:]
    up_ref[...] = low
    values = low.astype(F32)
    first, second = upstream_rows(values, t_ref[...].astype(F32), refs[0], SHRINK_GW, 2 * share)
    rows = [token_sum_row(folded(part)) for part in rows + (values,)]
    feed_backward(low, first, second, stat_ref[0:1, :], stat_ref[1:2, :], rows, refs)


def write_pieces(refs, first, values):
    rows = refs[0].shape[0]
    for place, ref in enumerate(refs):
        ref[:, first : first + values.shape[1]] = values[place * rows : (place + 1) * rows].astype(BF)


def feed_weights_kernel(pieces, *refs):
    refs, outs = refs[: -1 - pieces], refs[-1 - pieces :]
    shard = outs[0].shape[1] // 2
    chunks = len(refs) // 4
    for index, out_refs in ((1, outs[1:]), (0, outs[:1])):
        here = slice(index * shard, (index + 1) * shard)
        shrink = expand = None
        for chunk in range(chunks):
            up, shrunk, change, second = refs[4 * chunk : 4 * chunk + 4]
            term = nt(up[...], shrunk[here, :])
            shrink = term if shrink is None else shrink + term
            term = nt(second[...], change[here, :])
            expand = term if expand is None else expand + term
        write_pieces(out_refs, 0, shrink)
        write_pieces(out_refs, shard, expand)


def attention_backward_kernel(chunk, size, later, *refs):
    own_part, recv_part, up_ref, middle_ref, t_ref, stat_ref, late_ref, vec_ref = refs[:8]
    flag_ref, start_ref, q_ref, merge_own, merge_peer, mixed_ref, lse_ref = refs[8:15]
    refs = refs[15:]
    kv_refs, refs = refs[: 2 * chunk + 2], refs[2 * chunk + 2 :]
    later_refs, refs = refs[:later], refs[later:]
    low_ref, change_ref, gq_ref, merged_ref = refs[:4]
    own_sum, recv_low, sums_ref = refs[4:7]
    before_sums = refs[7 : 7 + 2 * chunk]
    recv_sum, mixed_change_ref = refs[7 + 2 * chunk :]

    width = up_ref.shape[0]
    second_change = own_part[...].astype(F32) + recv_part[...].astype(F32)
    middle = middle_ref[...]
    mean, rstd = token_stats(middle)
    unit = (middle - mean) * rstd
    scaled = second_change * column(late_ref, SECOND_GAIN)
    first = row_total(scaled) / width
    second = row_total(scaled * unit) / width
    change = up_ref[...].astype(F32) + rstd * (scaled - first - unit * second)
    change_ref[...] = change
    low = change.astype(BF)
    low_ref[...] = low
    rows = [
        token_sum_row(folded(part)) for part in (second_change * unit, second_change, change)
    ]
    first, second = upstream_rows(
        low.astype(F32), t_ref[...].astype(F32), late_ref, MERGE_GW, width
    )
    mean, rstd = stat_ref[0:1, :], stat_ref[1:2, :]
    head_width = q_ref.shape[0] // 2
    norm_parts = []
    for shard, merge in ((0, merge_own), (1, merge_peer)):
        here = slice(shard * head_width, (shard + 1) * head_width)
        gain = head_column(vec_ref, 2, shard, head_width)
        merged_change = nn(merge[...], low)
        unit = (mixed_ref[here, :] - mean) * rstd
        merged_ref[here, :] = (unit * gain + head_column(vec_ref, 3, shard, head_width)).astype(BF)
        norm_parts.append((folded(merged_change * unit), folded(merged_change)))
        mixed_change_ref[here, :] = (
            rstd * (merged_change * gain - first - unit * second)
        ).astype(BF)

    queries = q_ref.shape[1]
    pieces = key_pieces(chunk, size, flag_ref[IN_CORE], start_ref[...], kv_refs)
    masks = [piece_mask(piece, queries) for piece in pieces]
    totals = list(before_sums) + [own_sum, recv_sum]
    for place, ref in enumerate((own_sum, recv_sum)):
        ref[...] = later_refs[place][...] if later else jnp.zeros(ref.shape, F32)
    for ref in before_sums:
        ref[...] = jnp.zeros(ref.shape, F32)
    factor = HEAD_DIM ** (-0.5)
    query_parts = []
    for shard in range(2):
        query_folds = []
        for head in range(head_width // HEAD_DIM):
            place = shard * head_width + head * HEAD_DIM
            here = slice(place, place + HEAD_DIM)
            query = q_ref[here, :]
            scaled_query = (query * factor).astype(BF)
            mixed_change = mixed_change_ref[here, :]
            row = shard * (head_width // HEAD_DIM) + head
            lse = lse_ref[row : row + 1, :]
            delta = row_total(mixed_change.astype(F32) * mixed_ref[here, :])
            query_change = None
            for index, (piece, mask, total_ref) in enumerate(zip(pieces, masks, totals)):
                keys = piece_rows(piece, shard, head * HEAD_DIM)
                values = piece_rows(piece, shard, head_width + head * HEAD_DIM)
                first = 2 * head_width * ((1 - shard) if index % 2 else shard) + head * HEAD_DIM
                key_rows = slice(first, first + HEAD_DIM)
                value_rows = slice(first + head_width, first + head_width + HEAD_DIM)
                probs = jnp.where(mask, jnp.exp(tn(keys, scaled_query) - lse), 0.0)
                score_change = (probs * (tn(values, mixed_change) - delta)).astype(BF)
                term = nn(keys, score_change)
                query_change = term if query_change is None else query_change + term
                total_ref[key_rows, :] += nt(scaled_query, score_change)
                total_ref[value_rows, :] += nt(mixed_change, probs.astype(BF))
            query_change = query_change * factor
            query_folds.append(folded(query_change))
            gq_ref[here, :] = query_change.astype(BF)
        query_parts.append(jnp.concatenate(query_folds, axis=0))
    recv_low[...] = recv_sum[...].astype(BF)
    for shard in range(2):
        gain_part, bias_part = norm_parts[shard]
        packed = [query_parts[shard], jnp.zeros(gain_part.shape, F32), gain_part, bias_part]
        rows.append(token_sum_row(jnp.concatenate(packed, axis=0)))
    sums_ref[...] = rows_of(rows, 0, 8, F32)


def heads_backward_kernel(norm, *refs):
    flag_ref, gq_ref, own_sum, came_ref = refs[:4]
    heads_refs = refs[4:6]
    out_ref, joined_ref, sums_ref = refs[-3:]
    width = gq_ref.shape[0] // 2
    product = None
    rows = []
    for shard in range(2):
        rows_here = own_sum.shape[0]
        first = pl.multiple_of((1 - flag_ref[IN_CORE]) * rows_here + shard * 2 * width, 2 * width)
        came = came_ref[pl.ds(first, 2 * width), :].astype(F32)
        total = own_sum[2 * width * shard : 2 * width * (shard + 1), :] + came
        value_part = folded(total[width:])
        zero = jnp.zeros(value_part.shape, F32)
        rows.append(token_sum_row(jnp.concatenate([zero, value_part, zero, zero], axis=0)))
        first = 3 * width * shard
        joined_ref[first : first + width, :] = gq_ref[shard * width : (shard + 1) * width, :]
        joined_ref[first + width : first + 3 * width, :] = total.astype(BF)
        term = tn(heads_refs[shard][...], joined_ref[first : first + 3 * width, :])
        product = term if product is None else product + term
    low = product.astype(BF)
    out_ref[...] = low
    if norm:
        normed_change = low.astype(F32)
        values = refs[6][...].astype(F32)
        mean, rstd = token_stats(values)
        for part in (normed_change * ((values - mean) * rstd), normed_change):
            rows.append(token_sum_row(folded(part)))
    sums_ref[...] = rows_of(rows, 0, 8, F32)


def attention_weights_kernel(pieces, *refs):
    refs, outs = refs[: -1 - pieces], refs[-1 - pieces :]
    chunks = len(refs) // 4
    width = refs[3].shape[0] // 2
    for index, out_refs in ((1, outs[1:]), (0, outs[:1])):
        heads = merge = None
        for chunk in range(chunks):
            up, joined, normed, merged = refs[4 * chunk : 4 * chunk + 4]
            term = nt(normed[...], joined[3 * width * index : 3 * width * (index + 1), :])
            heads = term if heads is None else heads + term
            term = nt(up[...], merged[width * index : width * (index + 1), :])
            merge = term if merge is None else merge + term
        write_pieces(out_refs, 0, heads)
        write_pieces(out_refs, 3 * width, merge)


def final_kernel(own_ref, recv_ref, change_ref, h_ref, vec_ref, out_ref):
    out_ref[...] = norm_back(own_ref, recv_ref, change_ref, h_ref, vec_ref)[0].T.astype(BF)


def fold_kernel(after_bit, flag, flag_ref, stay_ref, *refs):
    came_refs, (keep_ref, give_ref) = refs[:-2], refs[-2:]
    each = came_refs[0].shape[0]
    bit = flag_ref[flag]
    for out_ref, mine in ((give_ref, 1 - bit), (keep_ref, bit)):
        for place in range(keep_ref.shape[0]):
            high, low = place // after_bit, place % after_bit
            if len(came_refs) == 1:
                index = (2 * high + mine) * after_bit + low
                out_ref[place] = (
                    stay_ref[index].astype(F32) + came_refs[0][index].astype(F32)
                ).astype(BF)
                continue
            first = 2 * high * after_bit + low
            pair = [
                stay_ref[index].astype(F32) + came_refs[index // each][index % each].astype(F32)
                for index in (first, first + after_bit)
            ]
            out_ref[place] = jnp.where(mine == 0, pair[0], pair[1]).astype(BF)


def settle_kernel(stay_ref, came_ref, out_ref):
    out_ref[...] = stay_ref[...].astype(F32) + came_ref[...].astype(F32)


def finish_kernel(flag_ref, stay_ref, came_ref, upper_ref, given_ref, kept_ref):
    first = flag_ref[IN_SECTION] == 0
    lower = stay_ref[0].astype(F32) + came_ref[0].astype(F32)
    upper = upper_ref[0]
    given_ref[...] = jnp.where(first, upper, lower).astype(BF)
    kept_ref[...] = jnp.where(first, lower, upper)


def collect_kernel(layers, counts, flag_ref, *refs):
    give_ref, keep_ref = refs[-2:]
    refs = list(refs[:-2])
    groups = {}
    for name, count in counts:
        groups[name] = refs[:count]
        refs = refs[count:]
    first_section, first_chip = flag_ref[IN_SECTION] == 0, flag_ref[IN_CHIP] == 0
    tables = []
    for layer in range(layers):

        def row(index, name, at=layer):
            return sum(ref[index : index + 1, :] for ref in groups[name, at])

        norm = [
            row(6 + place, "feed", layer - 1) if layer else row(2 + place, "heads")
            for place in range(2)
        ]
        shared = norm + [row(2, "attend"), row(8, "feed"), row(0, "attend"), row(1, "attend")]
        shared = [
            item if not layer and place < 2 else jnp.where(first_chip, item, 0.0)
            for place, item in enumerate(shared)
        ]
        split = []
        for shard in range(2):
            split += [row(2 * place + shard, "feed") for place in range(3)]
            split.append(row(3 + shard, "attend") + row(shard, "heads"))
        tables.append(rows_of(shared, 0, 16, F32) + rows_of(split, 8, 16, F32))
    keep_ref[...] = jnp.where(first_section, tables[0], tables[1])
    give_ref[...] = jnp.where(first_section, tables[1], tables[0])


def call(kernel, outs, args, scratch=(), scalars=(), deps=(), token=False):
    specs = [
        pl.BlockSpec(memory_space=pltpu.SMEM if place in scalars else pltpu.VMEM)
        for place in range(len(args))
    ]
    specs += [pl.BlockSpec(memory_space=pl.ANY)] * len(deps)
    used, given = len(args), len(args) + len(deps)
    outs = list(outs) + [arr((8, 128), F32)] * token

    def run(*refs):
        out_refs, inner = refs[given : given + len(outs)], refs[given + len(outs) :]
        kernel(*refs[:used], *out_refs[: len(outs) - token], *inner)
        if token:
            out_refs[-1][...] = jnp.zeros((8, 128), F32)

    return pl.pallas_call(
        run,
        out_shape=outs,
        in_specs=specs,
        out_specs=[pl.BlockSpec(memory_space=pltpu.VMEM)] * len(outs),
        scratch_shapes=list(scratch),
        compiler_params=pltpu.CompilerParams(vmem_limit_bytes=VMEM_MB * 1024 * 1024),
        cost_estimate=pl.CostEstimate(flops=0, bytes_accessed=0, transcendentals=0),
        name=(kernel.func if isinstance(kernel, partial) else kernel).__name__,
    )(*args, *deps)


def arr(shape, dtype):
    return jax.ShapeDtypeStruct(shape, dtype)


def step_swap(values, axis, step):
    count = lax.axis_size(axis)
    return lax.ppermute(values, axis, [(i, i ^ step) for i in range(count)])


def core_swap(block):
    return step_swap(block, TENSOR, 1)


def both_cores_of(block):
    count = lax.axis_size(TENSOR)
    groups = [[i, i + 1] for i in range(0, count, CORES)]
    return lax.all_gather(block, TENSOR, axis=0, tiled=True, axis_index_groups=groups)


def chip_swap(block):
    return step_swap(block, TENSOR, 2)


def section_swap(block):
    return step_swap(block, SECTION, 1)


class OverRows:
    def __init__(self, flags, own, peers, sections_last=False):
        count = lax.axis_size(DP)
        rows, columns = own.shape[0] // count, own.shape[1]
        steps = []
        while 1 << len(steps) < count:
            steps.append((DP, 1 << len(steps), IN_DP + len(steps)))
        sections = (SECTION, 1, IN_SECTION)
        self.flags = flags
        self.bits = steps[::-1] + [sections]
        self.steps = steps + [sections] if sections_last else [sections] + steps
        shape = (2 * count, rows // 2, columns)
        self.stay = own.reshape(shape)
        each = (shape[0] // len(peers),) + shape[1:]
        self.came = [core_swap(peer.reshape(each)) for peer in peers]

    def advance(self, deps):
        item = self.steps.pop(0)
        axis, step, flag = item
        place = self.bits.index(item)
        self.bits.pop(place)
        half = self.stay.shape[0] // 2
        out = arr((half,) + self.stay.shape[1:], BF)
        keep, give, token = call(
            partial(fold_kernel, 1 << (len(self.bits) - place), flag),
            [out, out],
            [self.flags, self.stay, *self.came],
            scalars=(0,),
            deps=deps,
            token=True,
        )
        self.stay, self.came = keep, [step_swap(give, axis, step)]
        return [token]


def settle(item, deps):
    while item.steps:
        deps = item.advance(deps)
    out, token = call(
        settle_kernel, [arr(item.stay.shape, F32)], [item.stay, item.came[0]], deps=deps, token=True
    )
    return out, [token]


def after(value, *others):
    return lax.optimization_barrier((value,) + others)[0]


def other_section(weight, *behind):
    odd = lax.axis_index(DP) & 1
    rows = weight.shape[0] // 2
    half = lax.dynamic_slice_in_dim(weight, odd * rows, rows, 0)
    return section_swap(after(half, *behind))


def both_halves(came, *behind):
    return came, step_swap(after(came, *behind), DP, 1)


def body(
    boundary,
    document_lengths,
    norm_gain,
    norm_bias,
    pair_weight,
    value_weight,
    query_bias,
    value_bias,
    inner_gain,
    inner_bias,
    merge_weight,
    merge_bias,
    second_gain,
    second_bias,
    expand_weight,
    expand_bias,
    hidden_gain,
    hidden_bias,
    shrink_weight,
    shrink_bias,
):
    section = lax.axis_index(SECTION)
    first = section == 0
    place = lax.axis_index(TENSOR)
    core = place & (CORES - 1)
    chip = place >> (CORES - 1)
    block = boundary.shape[2]
    width = boundary.shape[4]
    head_width = value_weight.shape[-1]
    shard = expand_weight.shape[-1]
    chunks = lax.axis_size(TENSOR) // CORES
    size = CORES * block
    row_length = chunks * size
    layers = 2
    row_place = lax.axis_index(DP)
    odd = row_place & 1
    bits = [(row_place >> bit) & 1 for bit in range(max(1, (lax.axis_size(DP) - 1).bit_length()))]
    flags = jnp.stack([section, chip, core] + bits).astype(jnp.int32)

    own = boundary[0, :, :, 0, :]
    mine = lax.dynamic_index_in_dim(own, section, 0, False)
    away = lax.dynamic_index_in_dim(own, 1 - section, 0, False)
    came = section_swap(away)
    heads_vector = jnp.concatenate(
        [after(query_bias[0], away), value_bias[0], inner_gain[0], inner_bias[0]]
    )
    early = jnp.concatenate(
        [norm_gain, norm_bias, heads_vector[None], jnp.zeros((1, width), F32)], axis=0
    )
    early_came = section_swap(after(early, away))
    lengths = jnp.where(first, document_lengths[0, 0], document_lengths[1, 0])
    ends = jnp.cumsum(lengths)
    positions = jnp.arange(row_length, dtype=jnp.int32)
    starts = jnp.max(
        jnp.where(positions[:, None] >= ends[None, :], ends[None, :], 0), axis=-1
    ).astype(jnp.int32)[None]
    starts = [
        lax.dynamic_slice_in_dim(starts, i * size + core * block, block, 1) for i in range(chunks)
    ]

    table = jnp.stack([heads_vector, expand_bias[0], hidden_gain[0], hidden_bias[0]])
    table_peer = core_swap(table)
    vector_columns = arr((width, 128), F32)
    early = call(
        early_kernel,
        [vector_columns] * layers,
        [flags, early, early_came, table_peer, core_swap(early_came)],
        scalars=(0,),
    )
    merge32 = after(merge_weight[0], away).astype(F32)
    shrink32 = after(shrink_weight[0], away).astype(F32)
    shares = jnp.stack(
        [
            jnp.sum(merge32 * inner_gain[0][:, None], axis=0),
            jnp.sum(shrink32 * hidden_gain[0][:, None], axis=0),
            jnp.sum(merge32 * inner_bias[0][:, None], axis=0),
            jnp.sum(shrink32 * hidden_bias[0][:, None], axis=0),
        ]
    )
    shares = shares + core_swap(shares)
    inputs, cotangent = call(
        first_kernel,
        [arr((block + STAT_ROWS, width), BF), arr((block, width), BF)],
        [flags, mine, came, shares],
        scalars=(0,),
    )
    inputs_there = chip_swap(inputs)
    cotangent_there = chip_swap(after(cotangent, inputs_there))
    plain = jnp.concatenate([merge_bias, second_gain, second_bias, shrink_bias], axis=0)
    half_merge = merge_weight.shape[1] // 2
    late_rows, merge_given = call(
        late_rows_kernel,
        [arr((COLUMNS, width), F32), arr((half_merge + 3 * COLUMNS, width), BF)],
        [flags, shares, inputs_there, plain, table, table_peer, merge_weight[0]],
        scalars=(0,),
    )

    heads_weight = jnp.concatenate(
        [
            pair_weight[0].transpose(1, 2, 0).reshape(2 * head_width, width),
            value_weight[0].T,
        ],
        axis=0,
    )
    given = (heads_weight, merge_weight[0], expand_weight[0], shrink_weight[0])
    given_peer = [core_swap(item) for item in given]
    heads_half = other_section(given[0], away)
    merge_half = section_swap(merge_given)
    late = call(
        late_kernel, [vector_columns] * layers, [flags, late_rows, merge_half], scalars=(0,)
    )
    expand_half = other_section(given[2], merge_given)
    shrink_whole = section_swap(after(given[3], merge_given))
    there = [both_halves(heads_half, inputs), both_halves(merge_half, inputs_there)]
    there.append(both_halves(expand_half, there[0][1]))
    there_peer = [[core_swap(item) for item in pair] for pair in there[:2]]

    even = odd == 0

    def layer_weight(layer, own, came, other=None):
        if other is None:
            away = came
        else:
            upper = jnp.where(even, came, other)
            lower = jnp.where(even, other, came)
            rows = own.shape[0] // 2
            away = jnp.concatenate([upper[:rows], lower[:rows]], axis=0)
        return jnp.where(first, away, own) if layer else jnp.where(first, own, away)

    def both_cores(index, pair, pair_peer):
        return [
            (
                layer_weight(layer, given[index], *pair),
                layer_weight(layer, given_peer[index], *pair_peer),
            )
            for layer in range(layers)
        ]

    heads_w, merge_w = [both_cores(index, there[index], there_peer[index]) for index in range(2)]

    act = arr((width, block), BF)
    act32 = arr((width, block), F32)
    carried = arr((width + STAT_ROWS, block), BF)
    stats = arr((8, block), F32)
    heads2 = arr((2 * head_width, block), BF)
    keyed = arr((4 * head_width, block), BF)
    keyed32 = arr((4 * head_width, block), F32)
    wide = arr((2 * shard, block), BF)
    few = arr((8, width), F32)
    many = arr((16, width), F32)
    inner_share = 2 * head_width
    hidden_share = 2 * shard

    sums_of = {}

    def note(name, layer, table):
        sums_of.setdefault((name, layer), []).append(table)

    keyed = arr((4 * head_width, block), BF)
    keyed32 = arr((4 * head_width, block), F32)
    changes = [
        call(
            partial(cotangent_kernel, i),
            [act, stats],
            [flags, cotangent, cotangent_there, late[layers - 1]],
            scalars=(0,),
        )
        for i in range(chunks)
    ]
    kept = []
    previous = [dots for low, dots in changes]
    for layer in range(layers):
        save = [dict() for i in range(chunks)]
        for i in range(chunks):
            item = save[i]
            outs = [act, act, heads2, keyed]
            if layer:
                lower = kept[-1][i]
                results = call(
                    partial(between_kernel, hidden_share),
                    [act, stats] + outs,
                    [*lower["part"], lower["middle"], late[layer - 1], early[layer], *heads_w[layer]],
                    deps=previous,
                )
                lower.update(t_shrink=results[0], stat_shrink=results[1])
                results = results[2:]
            else:
                results = call(
                    partial(start_kernel, i),
                    outs,
                    [flags, inputs, inputs_there, early[0], *heads_w[0]],
                    scalars=(0,),
                    deps=previous,
                )
            item["h"], item["n"], item["q"] = results[:3]
            item["kv"] = [results[3], both_cores_of(results[3])]
            before = [ref for j in range(i + 1) for ref in save[j]["kv"]]
            chip_part, item["mixed"], item["lse"] = call(
                partial(attention_forward_kernel, i, size),
                [carried, arr((2 * head_width, block), F32), stats],
                [flags, starts[i], item["q"], *merge_w[layer], early[layer], *before],
                scalars=(0,),
                deps=previous,
            )
            item["part"] = (chip_part, chip_swap(chip_part))
            previous = [chip_part]
        if not layer:
            there.append((after(shrink_whole, save[0]["part"][1]),))
            there_peer.append([core_swap(after(item, save[0]["part"][0])) for item in there[2]])
            there_peer.append([core_swap(there[3][0])])
            expand_w, shrink_w = [
                both_cores(index, there[index], there_peer[index]) for index in (2, 3)
            ]
        turn_rows = []
        for i in range(chunks):
            item = save[i]
            last = layer + 1 == layers
            results = call(
                partial(feed_forward_kernel, inner_share, last, i),
                [carried, act32, act, act, stats, arr((2 * shard, block), F32)]
                + ([arr((8 * i + 8, block), F32)] if last else []),
                [*item["part"], item["h"], late[layer], *expand_w[layer], *shrink_w[layer]]
                + ([changes[i][0]] + turn_rows if last else []),
                deps=previous,
            )
            chip_part, item["middle"], item["second"] = results[:3]
            item["t_merge"], item["stat_merge"], item["expanded"] = results[3:6]
            if last:
                item["part"] = chip_part
                turn_rows = [results[6]]
            else:
                item["part"] = (chip_part, chip_swap(chip_part))
            previous = [chip_part]
        kept.append(save)
    turn_rows.append(chip_swap(turn_rows[0]))

    top = kept[-1]
    keep, keep_middle, give = call(
        pick_kernel,
        [carried, act32, carried],
        [flags, top[0]["part"], top[1]["part"], top[0]["middle"], top[1]["middle"]],
        scalars=(0,),
        deps=previous,
    )
    output_parts = (keep, chip_swap(after(give, turn_rows[1])), keep_middle)
    previous = [keep]

    feed_sums = [None] * layers
    attend_sums = [None] * layers

    def feed_weights(layer, deps):
        args = []
        for item in kept[layer]:
            args += [item[name] for name in ("up", "shrunk", "change", "second")]
        grad = arr((width, 2 * shard), BF)
        pieces = 4
        piece = arr((width // pieces, 2 * shard), BF)
        own, *peers, token = call(
            partial(feed_weights_kernel, pieces), [grad] + [piece] * pieces, args, deps=deps, token=True
        )
        feed_sums[layer] = OverRows(flags, own, peers)
        return [token]

    def attention_weights(layer, deps):
        args = []
        for item in kept[layer]:
            args += [item[name] for name in ("up_middle", "joined", "n", "merged")]
        grad = arr((width, 4 * head_width), BF)
        pieces = 2
        piece = arr((width // pieces, 4 * head_width), BF)
        own, *peers, token = call(
            partial(attention_weights_kernel, pieces),
            [grad] + [piece] * pieces,
            args,
            deps=deps,
            token=True,
        )
        attend_sums[layer] = OverRows(flags, own, peers, layer > 0)
        return [token]

    def aside(point, deps):
        for kind, layer in ASIDE.get(point, ()):
            if kind == FEED:
                deps = feed_weights(layer, deps)
            elif kind == ATTEND:
                deps = attention_weights(layer, deps)
            else:
                deps = (feed_sums if kind == FEED_STEP else attend_sums)[layer].advance(deps)
        return deps

    for layer in reversed(range(layers)):
        save = kept[layer]
        for i in reversed(range(chunks)):
            item = save[i]
            common = [late[layer], *expand_w[layer], *shrink_w[layer], item["expanded"]]
            outs = [act, wide, wide, many]
            if layer + 1 == layers:
                item["up"], dots = changes[i]
                results = call(
                    partial(turn_kernel, hidden_share, i),
                    outs,
                    [*turn_rows, item["up"], dots] + common,
                    deps=previous,
                )
            else:
                upper = kept[layer + 1][i]
                results = call(
                    partial(layer_back_kernel, hidden_share),
                    [act] + outs,
                    [
                        *upper["part"],
                        upper["middle_change"],
                        upper["h"],
                        early[layer + 1],
                        item["t_shrink"],
                        item["stat_shrink"],
                    ]
                    + common,
                    deps=previous,
                )
                item["up"], results = results[0], results[1:]
            chip_part, item["change"], item["shrunk"], table = results
            note("feed", layer, table)
            item["part"] = (chip_part, chip_swap(chip_part))
            previous = [chip_part]
            previous = aside((FEED, layer, i), previous)
        later = [[] for i in range(chunks)]
        for i in reversed(range(chunks)):
            item = save[i]
            before = [ref for j in range(i + 1) for ref in save[j]["kv"]]
            results = call(
                partial(attention_backward_kernel, i, size, len(later[i])),
                [act, act32, heads2, heads2, keyed32, keyed, few] + [keyed32] * (2 * i),
                [
                    *item["part"],
                    item["up"],
                    item["middle"],
                    item["t_merge"],
                    item["stat_merge"],
                    late[layer],
                    early[layer],
                    flags,
                    starts[i],
                    item["q"],
                    *merge_w[layer],
                    item["mixed"],
                    item["lse"],
                    *before,
                    *later[i],
                ],
                scratch=[
                    pltpu.VMEM((4 * head_width, block), F32),
                    pltpu.VMEM((2 * head_width, block), BF),
                ],
                scalars=(8,),
                deps=previous,
            )
            item["up_middle"], item["middle_change"], gq, item["merged"] = results[:4]
            own_sum, recv_low, table = results[4:7]
            for j in range(i):
                later[j] += results[7 + 2 * j : 9 + 2 * j]
            note("attend", layer, table)
            previous = aside((ATTEND, layer, i), [table])
            chip_part, item["joined"], table = call(
                partial(heads_backward_kernel, not layer),
                [act, arr((6 * head_width, block), BF), few],
                [flags, gq, own_sum, both_cores_of(recv_low), *heads_w[layer]]
                + ([] if layer else [item["h"]]),
                scalars=(0,),
                deps=previous,
            )
            note("heads", layer, table)
            item["part"] = (chip_part, chip_swap(chip_part)) if layer else chip_part
            previous = [chip_part]
            previous = aside((HEAD, layer, i), previous)

    previous = attend_sums[1].advance(previous)
    previous = attention_weights(0, previous)
    keep, keep_change, keep_h, give = call(
        pick_kernel,
        [act, act32, act, act],
        [flags] + [kept[0][i][name] for name in ("part", "middle_change", "h") for i in range(2)],
        scalars=(0,),
        deps=previous,
    )
    keep_there = chip_swap(give)
    previous = feed_sums[1].advance([keep])
    previous = feed_sums[0].advance(previous)
    previous = attend_sums[0].advance(previous)
    feed_above, previous = settle(feed_sums[1], previous)
    counts = [(key, len(tables)) for key, tables in sums_of.items()]
    give, keep_rows = call(
        partial(collect_kernel, layers, counts),
        [many, many],
        [flags] + [table for tables in sums_of.values() for table in tables],
        scalars=(0,),
        deps=previous,
    )
    previous = [give]
    last = call(
        final_kernel,
        [arr((block, width), BF)],
        [keep, keep_there, keep_change, keep_h, early[0]],
        deps=previous,
    )[0]
    previous = attend_sums[0].advance([last])
    rows = keep_rows + after(section_swap(give), *previous)
    rows_peer = core_swap(rows)
    rows = jnp.concatenate([rows[:8] + rows_peer[:8], rows[8:12] + rows_peer[12:]])
    if feed_sums[0].steps:
        previous = feed_sums[0].advance(previous)
    came_rows = step_swap(after(rows, *previous), DP, 1)
    output = call(
        partial(output_kernel, hidden_share),
        [arr((block, width), BF)],
        [*output_parts, late[layers - 1]],
        deps=previous,
    )[0]
    previous = [output]
    theirs = section_swap(jnp.where(first, output, last))
    for item in (attend_sums[0], feed_sums[0]):
        while item.steps:
            previous = item.advance(previous)
    rows = rows + after(came_rows, *previous)
    steps = [1 << bit for bit in range(1, (lax.axis_size(DP) - 1).bit_length())]
    came_rows = step_swap(rows, DP, steps[0])

    def own_layer(item, above, deps):
        shape = above.shape[1:]
        given, kept_half, token = call(
            finish_kernel,
            [arr(shape, BF), arr(shape, F32)],
            [flags, item.stay, item.came[0], above],
            scalars=(0,),
            deps=deps,
            token=True,
        )
        came_half = section_swap(given).astype(F32)
        upper = jnp.where(first, kept_half, came_half)
        lower = jnp.where(first, came_half, kept_half)
        return jnp.concatenate([upper, lower], axis=0), [token]

    feed, previous = own_layer(feed_sums[0], feed_above, previous)
    attend_above, previous = settle(attend_sums[1], previous)
    rows = rows + after(came_rows, *previous)
    for step in steps[1:]:
        rows = rows + step_swap(rows, DP, step)
    shared = rows[:8]
    shared_there = chip_swap(shared)
    theirs = after(theirs, *previous)
    attend, previous = own_layer(attend_sums[0], attend_above, previous)
    shared = (shared + after(shared_there, *previous))[:6, None]
    split = rows[8:12, None]

    kept_here = jnp.where(first, last, output)
    final = jnp.stack(
        [jnp.where(first, kept_here, theirs), jnp.where(first, theirs, kept_here)]
    )[None, :, :, None, :]

    rows_here = attend.shape[0]
    pair_gradient = attend[:, : 2 * head_width].reshape(rows_here, 2, head_width)
    value_gradient = attend[:, 2 * head_width : 3 * head_width]
    merge_gradient = attend[:, 3 * head_width :].T
    shrink_gradient = feed[:, :shard].T
    expand_gradient = feed[:, shard:]
    packed = split[3]

    def packed_part(index):
        return packed[:, index * head_width : (index + 1) * head_width]

    return (
        final,
        shared[0],
        shared[1],
        pair_gradient[None],
        value_gradient[None],
        packed_part(0),
        packed_part(1),
        packed_part(2),
        packed_part(3),
        merge_gradient[None],
        shared[2],
        shared[4],
        shared[5],
        expand_gradient[None],
        split[2],
        split[0],
        split[1],
        shrink_gradient[None],
        shared[3],
    )


def solution(mesh):
    in_specs = (
        P(SECTION, None, TENSOR, DP, None),
        P(None, DP, None),
        P(SECTION, None),
        P(SECTION, None),
        P(SECTION, None, None, TENSOR),
        P(SECTION, None, TENSOR),
        P(SECTION, TENSOR),
        P(SECTION, TENSOR),
        P(SECTION, TENSOR),
        P(SECTION, TENSOR),
        P(SECTION, TENSOR, None),
        P(SECTION, None),
        P(SECTION, None),
        P(SECTION, None),
        P(SECTION, None, TENSOR),
        P(SECTION, TENSOR),
        P(SECTION, TENSOR),
        P(SECTION, TENSOR),
        P(SECTION, TENSOR, None),
        P(SECTION, None),
    )
    out_specs = (
        P(SECTION, None, TENSOR, DP, None),
        P(SECTION, None),
        P(SECTION, None),
        P(SECTION, DP, None, TENSOR),
        P(SECTION, DP, TENSOR),
        P(SECTION, TENSOR),
        P(SECTION, TENSOR),
        P(SECTION, TENSOR),
        P(SECTION, TENSOR),
        P(SECTION, TENSOR, DP),
        P(SECTION, None),
        P(SECTION, None),
        P(SECTION, None),
        P(SECTION, DP, TENSOR),
        P(SECTION, TENSOR),
        P(SECTION, TENSOR),
        P(SECTION, TENSOR),
        P(SECTION, TENSOR, DP),
        P(SECTION, None),
    )
    return jax.shard_map(body, mesh=mesh, in_specs=in_specs, out_specs=out_specs, check_vma=False)
```

```python
from functools import partial

import jax
import jax.numpy as jnp
from jax import lax
from jax.experimental import pallas as pl
from jax.experimental.pallas import tpu as pltpu
from jax.sharding import PartitionSpec as P

HEAD_DIM = 64
EPS = 1e-05
MASKED = -1e30
CORES = 2
STAT_ROWS = 16
BF = jnp.bfloat16
F32 = jnp.float32

NORM_GAIN, NORM_BIAS, HEADS = range(3)
(MERGE_ADD, SECOND_GAIN, SECOND_BIAS, SHRINK_ADD, MERGE_GW, MERGE_GW_THERE, SHRINK_GW,
 SHRINK_GW_THERE, EXPAND_BIAS, HIDDEN_GAIN, HIDDEN_BIAS) = range(11)
SHARD_COLUMNS = 3
COLUMNS = 16
FAR = 1 << 30
SECTION, DP, TENSOR = "section", "dp", "tensor"
IN_SECTION, IN_CHIP, IN_CORE, IN_DP = range(4)
FEED, ATTEND, HEAD, FEED_STEP, ATTEND_STEP = range(5)
ASIDE = {
    (HEAD, 1, 1): [(FEED, 1)],
    (HEAD, 1, 0): [(FEED_STEP, 1)],
    (FEED, 0, 1): [(ATTEND, 1)],
    (FEED, 0, 0): [(FEED, 0), (ATTEND_STEP, 1)],
    (ATTEND, 0, 1): [(FEED_STEP, 0)],
    (HEAD, 0, 1): [(FEED_STEP, 1), (ATTEND_STEP, 1)],
}
VMEM_MB = 14


def nn(a, b):
    return lax.dot_general(a, b, (((1,), (0,)), ((), ())), preferred_element_type=F32)


def tn(a, b):
    return lax.dot_general(a, b, (((0,), (0,)), ((), ())), preferred_element_type=F32)


def nt(a, b):
    return lax.dot_general(a, b, (((1,), (1,)), ((), ())), preferred_element_type=F32)


def column(vec_ref, index, start=0, size=None):
    size = vec_ref.shape[0] if size is None else size
    return vec_ref[start : start + size, index : index + 1]


def shard_column(vec_ref, index, shard):
    return column(vec_ref, index + shard * SHARD_COLUMNS)


def head_column(vec_ref, part, shard, size):
    return column(vec_ref, HEADS + shard, part * size, size)


def row_total(values):
    return jnp.sum(values, axis=0, keepdims=True)


def token_stats(values):
    count = values.shape[0]
    mean = row_total(values) / count
    return mean, lax.rsqrt(row_total(values * values) / count - mean * mean + EPS)


def three_parts(row):
    high = row.astype(BF).astype(F32)
    middle = (row - high).astype(BF).astype(F32)
    return [high, middle, row - high - middle]


def rows_of(rows, first, count, dtype):
    width = rows[0].shape[1]
    index = lax.broadcasted_iota(jnp.int32, (count, width), 0)
    total = jnp.zeros((count, width), F32)
    for place, row in enumerate(rows):
        total = jnp.where(index == first + place, row, total)
    return total.astype(dtype)


def sum_parts(block, first):
    return block[first : first + 1] + block[first + 1 : first + 2] + block[first + 2 : first + 3]


def folded(values):
    total = values[:, :128]
    for place in range(128, values.shape[1], 128):
        total = total + values[:, place : place + 128]
    return total


def token_sum_row(part):
    return row_total(part.T)


def gelu_pair(values):
    cdf = 0.5 * (1.0 + lax.erf(values * (0.5**0.5)))
    density = jnp.exp(values * values * -0.5) * 0.3989422804014327
    return values * cdf, cdf + values * density


def gelu(values):
    return values * (0.5 * (1.0 + lax.erf(values * (0.5**0.5))))


def split_product(out_ref, parts, weights, gains):
    count = sum(part.shape[0] for part in parts)
    first_sum = sum(row_total(part) for part in parts)
    second_sum = sum(row_total(part * part) for part in parts)
    mean = first_sum / count
    product = None
    for part, weight, gain in zip(parts, weights, gains):
        term = tn(weight[...], ((part - mean) * gain).astype(BF))
        product = term if product is None else product + term
    low = product.astype(BF)
    width = product.shape[0]
    out_ref[:width, :] = low
    out_ref[width:, :] = rows_of(three_parts(first_sum) + three_parts(second_sum), 0, STAT_ROWS, BF)
    return low, first_sum, second_sum


def whole_stats(firsts, seconds, share):
    count = len(firsts) * share
    mean = sum(firsts) / count
    return mean, lax.rsqrt(sum(seconds) / count - mean * mean + EPS)


def combined(own_ref, recv_ref, vec_ref, first_column, share):
    width = own_ref.shape[0] - STAT_ROWS
    extra = [ref[width:, :].astype(F32) for ref in (own_ref, recv_ref)]
    firsts = [sum_parts(rows, 0) for rows in extra]
    mean, rstd = whole_stats(firsts, [sum_parts(rows, 3) for rows in extra], share)
    total = own_ref[:width, :].astype(F32) + recv_ref[:width, :].astype(F32)
    for place, first in enumerate(firsts):
        total = total + (first / share - mean) * column(vec_ref, first_column + place)
    return total * rstd, mean, rstd


def write_stats(ref, mean, rstd):
    ref[...] = rows_of([mean, rstd], 0, ref.shape[0], F32)


def project(normed, heads, vec_ref, q_ref, kv_ref):
    width = q_ref.shape[0] // 2
    for shard in range(2):
        projected = nn(heads[shard][...], normed)
        query = projected[:width] + head_column(vec_ref, 0, shard, width)
        value = projected[2 * width :] + head_column(vec_ref, 1, shard, width)
        q_ref[shard * width : (shard + 1) * width, :] = query.astype(BF)
        first = 2 * width * shard
        kv_ref[first : first + width, :] = projected[width : 2 * width].astype(BF)
        kv_ref[first + width : first + 2 * width, :] = value.astype(BF)


def norm_and_project(low, vec_ref, heads, h_ref, n_ref, q_ref, kv_ref):
    h_ref[...] = low
    values = low.astype(F32)
    mean, rstd = token_stats(values)
    normed = (
        (values - mean) * rstd * column(vec_ref, NORM_GAIN) + column(vec_ref, NORM_BIAS)
    ).astype(BF)
    n_ref[...] = normed
    project(normed, heads, vec_ref, q_ref, kv_ref)


def first_kernel(flag_ref, mine_ref, came_ref, share_ref, input_ref, change_ref):
    first = flag_ref[IN_SECTION] == 0
    block, width = mine_ref.shape
    mine, came = mine_ref[...], came_ref[...]
    input_ref[:block, :] = jnp.where(first, mine, came)
    change_ref[...] = jnp.where(first, came, mine)
    parts = three_parts(share_ref[...]) + [jnp.zeros(share_ref.shape, F32)]
    input_ref[block:, :] = jnp.concatenate(parts, axis=0).astype(BF)


def chunk_tokens(flag_ref, chunk, here_ref, there_ref, block):
    here, there = here_ref[:block, :], there_ref[:block, :]
    return jnp.where(flag_ref[IN_CHIP] == chunk, here, there).astype(F32).T


def start_kernel(chunk, flag_ref, here_ref, there_ref, vec_ref, heads_own, heads_peer, *outs):
    values = chunk_tokens(flag_ref, chunk, here_ref, there_ref, outs[0].shape[1])
    norm_and_project(values.astype(BF), vec_ref, (heads_own, heads_peer), *outs)


def columns_of(rows, out_ref):
    filled = jnp.concatenate([rows, jnp.zeros((128 - rows.shape[0], rows.shape[1]), F32)], axis=0)
    out_ref[...] = filled.T


def early_kernel(flag_ref, own_ref, came_ref, own_peer_ref, came_peer_ref, *out_refs):
    first = flag_ref[IN_SECTION] == 0
    sets = []
    for ref, peer in ((own_ref, own_peer_ref[0:1, :]), (came_ref, came_peer_ref[2:3, :])):
        rows = [ref[0:1, :], ref[1:2, :], ref[2:3, :], peer]
        sets.append(rows_of(rows, 0, 8, F32))
    columns_of(jnp.where(first, sets[0], sets[1]), out_refs[0])
    columns_of(jnp.where(first, sets[1], sets[0]), out_refs[1])


def late_rows_kernel(
    flag_ref, share_ref, arrived_ref, plain_ref, table_ref, peer_ref, merge_ref, rows_ref, out_ref
):
    def row(ref, index):
        return ref[index : index + 1, :]

    arrived = arrived_ref[arrived_ref.shape[0] - STAT_ROWS :, :].astype(F32)
    there = arrived[:4] + arrived[4:8] + arrived[8:12]
    both = [row(share_ref, index) + there[index : index + 1] for index in (2, 3)]
    rows = [row(plain_ref, 0) + both[0], row(plain_ref, 1), row(plain_ref, 2), row(plain_ref, 3) + both[1]]
    for index in range(2):
        rows += [row(share_ref, index), there[index : index + 1]]
    rows += [row(ref, index) for ref in (table_ref, peer_ref) for index in range(1, 4)]
    rows = rows_of(rows, 0, COLUMNS, F32)
    rows_ref[...] = rows
    half = merge_ref.shape[0] // 2
    first = pl.multiple_of(flag_ref[IN_DP] * half, 16)
    out_ref[:half, :] = merge_ref[pl.ds(first, half), :]
    for place, part in enumerate(three_parts(rows)):
        out_ref[half + place * COLUMNS : half + (place + 1) * COLUMNS, :] = part.astype(BF)


def late_kernel(flag_ref, own_ref, came_ref, *out_refs):
    first = flag_ref[IN_SECTION] == 0
    half = came_ref.shape[0] - 3 * COLUMNS
    parts = came_ref[half:, :].astype(F32)
    came = parts[:COLUMNS] + parts[COLUMNS : 2 * COLUMNS] + parts[2 * COLUMNS :]
    columns_of(jnp.where(first, own_ref[...], came), out_refs[0])
    columns_of(jnp.where(first, came, own_ref[...]), out_refs[1])


def pick_kernel(flag_ref, *refs):
    here = flag_ref[IN_CHIP] == 0
    count = (len(refs) - 1) // 3
    pairs, out_refs = refs[: 2 * count], refs[2 * count :]
    for place in range(count):
        left, right = pairs[2 * place][...], pairs[2 * place + 1][...]
        out_refs[place][...] = jnp.where(here, left, right)
        if not place:
            out_refs[-1][...] = jnp.where(here, right, left)


def between_kernel(
    share,
    own_ref,
    recv_ref,
    middle_ref,
    vec_ref,
    next_ref,
    heads_own,
    heads_peer,
    t_ref,
    stat_ref,
    *outs,
):
    product, mean, rstd = combined(own_ref, recv_ref, vec_ref, SHRINK_GW, share)
    write_stats(stat_ref, mean, rstd)
    t_ref[...] = product.astype(BF)
    low = (middle_ref[...] + (product + column(vec_ref, SHRINK_ADD))).astype(BF)
    norm_and_project(low, next_ref, (heads_own, heads_peer), *outs)


def key_pieces(chunk, size, core, start_row, kv_refs):
    block = start_row.shape[1]
    rows = kv_refs[0].shape[0]
    far = pl.multiple_of((1 - core) * rows, rows)
    pieces = []
    for index in range(chunk + 1):
        own_ref, both_ref = kv_refs[2 * index : 2 * index + 2]
        last = index == chunk
        peer_start = jnp.where(core == 1, start_row, FAR) if last else start_row
        places = (index * size + core * block, index * size + (1 - core) * block)
        pieces.append((own_ref, (0, rows // 2), places[0], start_row, last))
        pieces.append((both_ref, (far + rows // 2, far), places[1], peer_start, False))
    return pieces


def piece_rows(piece, shard, row):
    first = piece[1][shard] + row
    if not isinstance(first, int):
        first = pl.multiple_of(first, HEAD_DIM)
    return piece[0][pl.ds(first, HEAD_DIM), :]


def piece_mask(piece, queries):
    ref, rows, first, start_row, diagonal = piece
    shape = (ref.shape[1], queries)
    rows = lax.broadcasted_iota(jnp.int32, shape, 0)
    mask = first + rows >= start_row
    if diagonal:
        mask = mask & (rows <= lax.broadcasted_iota(jnp.int32, shape, 1))
    return mask


def attention_forward_kernel(chunk, size, *refs):
    flag_ref, start_ref, q_ref, merge_own, merge_peer, vec_ref = refs[:6]
    kv_refs = refs[6 : 8 + 2 * chunk]
    out_ref, mixed_ref, lse_ref = refs[8 + 2 * chunk :]
    width = q_ref.shape[0] // 2
    queries = q_ref.shape[1]
    pieces = key_pieces(chunk, size, flag_ref[IN_CORE], start_ref[...], kv_refs)
    masks = [piece_mask(piece, queries) for piece in pieces]
    heads = width // HEAD_DIM
    lse_rows = []
    for shard in range(2):
        for head in range(heads):
            first = shard * width + head * HEAD_DIM
            base = head * HEAD_DIM
            query = (q_ref[first : first + HEAD_DIM, :] * HEAD_DIM ** (-0.5)).astype(BF)
            scores, values, top = [], [], None
            for piece, mask in zip(pieces, masks):
                keys = piece_rows(piece, shard, base)
                values.append(piece_rows(piece, shard, base + width))
                score = jnp.where(mask, tn(keys, query), MASKED)
                scores.append(score)
                piece_top = jnp.max(score, axis=0, keepdims=True)
                top = piece_top if top is None else jnp.maximum(top, piece_top)
            weights = [jnp.exp(score - top) for score in scores]
            total = sum(row_total(weight) for weight in weights)
            inverse = 1.0 / total
            mixed = None
            for weight, value in zip(weights, values):
                term = nn(value, (weight * inverse).astype(BF))
                mixed = term if mixed is None else mixed + term
            mixed_ref[first : first + HEAD_DIM, :] = mixed
            lse_rows.append(top + jnp.log(total))
    lse_ref[...] = rows_of(lse_rows, 0, lse_ref.shape[0], F32)
    split_product(
        out_ref,
        [mixed_ref[:width, :], mixed_ref[width:, :]],
        [merge_own, merge_peer],
        [head_column(vec_ref, 2, shard, width) for shard in range(2)],
    )


def feed_forward_kernel(share, last, chunk, *refs):
    own_ref, recv_ref, h_ref, vec_ref = refs[:4]
    expand, shrink = refs[4:6], refs[6:8]
    refs = refs[8:]
    if last:
        change_ref, refs = refs[0], refs[1:]
        before_refs, refs = refs[: chunk > 0], refs[chunk > 0 :]
    out_ref, middle_ref, second_ref, t_ref, stat_ref, expanded_ref = refs[:6]
    product, mean, rstd = combined(own_ref, recv_ref, vec_ref, MERGE_GW, share)
    write_stats(stat_ref, mean, rstd)
    t_ref[...] = product.astype(BF)
    middle = h_ref[...].astype(F32) + (product + column(vec_ref, MERGE_ADD))
    middle_ref[...] = middle
    mean, rstd = token_stats(middle)
    second = (
        (middle - mean) * rstd * column(vec_ref, SECOND_GAIN) + column(vec_ref, SECOND_BIAS)
    ).astype(BF)
    second_ref[...] = second
    shard = expanded_ref.shape[0] // 2
    hidden = []
    for index in range(2):
        expanded = tn(expand[index][...], second) + shard_column(vec_ref, EXPAND_BIAS, index)
        expanded_ref[index * shard : (index + 1) * shard, :] = expanded
        hidden.append(gelu(expanded))
    gains = [shard_column(vec_ref, HIDDEN_GAIN, index) for index in range(2)]
    low, first_sum, second_sum = split_product(out_ref, hidden, shrink, gains)
    if last:
        dot = row_total(low.astype(F32) * change_ref[...].astype(F32))
        for ref in before_refs:
            refs[6][: 8 * chunk, :] = ref[...]
        refs[6][8 * chunk :, :] = rows_of([first_sum, second_sum, dot], 0, 8, F32)


def cotangent_kernel(chunk, flag_ref, here_ref, there_ref, vec_ref, low_ref, dots_ref):
    change = chunk_tokens(flag_ref, chunk, here_ref, there_ref, low_ref.shape[1])
    low_ref[...] = change.astype(BF)
    dots_ref[...] = rows_of(
        [row_total(change * column(vec_ref, SHRINK_GW + place)) for place in range(2)], 0, 8, F32
    )


def output_kernel(share, own_ref, recv_ref, middle_ref, vec_ref, out_ref):
    product, mean, rstd = combined(own_ref, recv_ref, vec_ref, SHRINK_GW, share)
    output = middle_ref[...] + (product + column(vec_ref, SHRINK_ADD))
    out_ref[...] = output.T.astype(BF)


def upstream_rows(values, product, vec_ref, first_column, count):
    total = column(vec_ref, first_column) + column(vec_ref, first_column + 1)
    return row_total(values * total) / count, row_total(values * product) / count


def norm_back(own_ref, recv_ref, change_ref, h_ref, vec_ref):
    width = own_ref.shape[0]
    normed_change = own_ref[...].astype(F32) + recv_ref[...].astype(F32)
    values = h_ref[...].astype(F32)
    mean, rstd = token_stats(values)
    unit = (values - mean) * rstd
    scaled = normed_change * column(vec_ref, NORM_GAIN)
    first = row_total(scaled) / width
    second = row_total(scaled * unit) / width
    change = change_ref[...] + rstd * (scaled - first - unit * second)
    return change, (normed_change * unit, normed_change)


def feed_backward(low, first, second, mean, rstd, rows, refs):
    vec_ref = refs[0]
    expand, shrink, expanded_ref = refs[1:3], refs[3:5], refs[5]
    out_ref, change_ref, shrunk_ref, sums_ref = refs[6:]
    shard = expanded_ref.shape[0] // 2
    sums = []
    product = None
    for index in range(2):
        here = slice(index * shard, (index + 1) * shard)
        gain = shard_column(vec_ref, HIDDEN_GAIN, index)
        shrunk_change = nn(shrink[index][...], low)
        hidden, slope = gelu_pair(expanded_ref[here, :])
        unit = (hidden - mean) * rstd
        shrunk_ref[here, :] = (unit * gain + shard_column(vec_ref, HIDDEN_BIAS, index)).astype(BF)
        expanded_change = rstd * (shrunk_change * gain - first - unit * second) * slope
        sums.append(
            [
                token_sum_row(folded(part))
                for part in (shrunk_change * unit, shrunk_change, expanded_change)
            ]
        )
        expanded_low = expanded_change.astype(BF)
        change_ref[here, :] = expanded_low
        term = nn(expand[index][...], expanded_low)
        product = term if product is None else product + term
    out_ref[...] = product.astype(BF)
    rows = [row for pair in zip(*sums) for row in pair] + rows
    sums_ref[...] = rows_of(rows, 0, 16, F32)


def turn_kernel(share, chunk, own_ref, recv_ref, low_ref, dots_ref, *refs):
    at = 8 * chunk
    firsts = [ref[at : at + 1, :] for ref in (own_ref, recv_ref)]
    seconds = [ref[at + 1 : at + 2, :] for ref in (own_ref, recv_ref)]
    mean, rstd = whole_stats(firsts, seconds, share)
    count = 2 * share
    second = own_ref[at + 2 : at + 3, :] + recv_ref[at + 2 : at + 3, :]
    first = 0.0
    for place, total in enumerate(firsts):
        dot = dots_ref[place : place + 1, :]
        first = first + dot
        second = second + (total / share - mean) * dot
    low = low_ref[...]
    zero = jnp.zeros((1, low.shape[0]), F32)
    rows = [zero, zero, token_sum_row(folded(low.astype(F32)))]
    feed_backward(low, first / count, second * rstd / count, mean, rstd, rows, refs)


def layer_back_kernel(
    share, own_ref, recv_ref, change_ref, h_ref, upper_ref, t_ref, stat_ref, *refs
):
    change, rows = norm_back(own_ref, recv_ref, change_ref, h_ref, upper_ref)
    low = change.astype(BF)
    up_ref, refs = refs[6], refs[:6] + refs[7:]
    up_ref[...] = low
    values = low.astype(F32)
    first, second = upstream_rows(values, t_ref[...].astype(F32), refs[0], SHRINK_GW, 2 * share)
    rows = [token_sum_row(folded(part)) for part in rows + (values,)]
    feed_backward(low, first, second, stat_ref[0:1, :], stat_ref[1:2, :], rows, refs)


def write_pieces(refs, first, values):
    rows = refs[0].shape[0]
    for place, ref in enumerate(refs):
        ref[:, first : first + values.shape[1]] = values[place * rows : (place + 1) * rows].astype(BF)


def feed_weights_kernel(pieces, *refs):
    refs, outs = refs[: -1 - pieces], refs[-1 - pieces :]
    shard = outs[0].shape[1] // 2
    chunks = len(refs) // 4
    for index, out_refs in ((1, outs[1:]), (0, outs[:1])):
        here = slice(index * shard, (index + 1) * shard)
        shrink = expand = None
        for chunk in range(chunks):
            up, shrunk, change, second = refs[4 * chunk : 4 * chunk + 4]
            term = nt(up[...], shrunk[here, :])
            shrink = term if shrink is None else shrink + term
            term = nt(second[...], change[here, :])
            expand = term if expand is None else expand + term
        write_pieces(out_refs, 0, shrink)
        write_pieces(out_refs, shard, expand)


def attention_backward_kernel(chunk, size, later, *refs):
    own_part, recv_part, up_ref, middle_ref, t_ref, stat_ref, late_ref, vec_ref = refs[:8]
    flag_ref, start_ref, q_ref, merge_own, merge_peer, mixed_ref, lse_ref = refs[8:15]
    refs = refs[15:]
    kv_refs, refs = refs[: 2 * chunk + 2], refs[2 * chunk + 2 :]
    later_refs, refs = refs[:later], refs[later:]
    low_ref, change_ref, gq_ref, merged_ref = refs[:4]
    own_sum, recv_low, sums_ref = refs[4:7]
    before_sums = refs[7 : 7 + 2 * chunk]
    recv_sum, mixed_change_ref = refs[7 + 2 * chunk :]

    width = up_ref.shape[0]
    second_change = own_part[...].astype(F32) + recv_part[...].astype(F32)
    middle = middle_ref[...]
    mean, rstd = token_stats(middle)
    unit = (middle - mean) * rstd
    scaled = second_change * column(late_ref, SECOND_GAIN)
    first = row_total(scaled) / width
    second = row_total(scaled * unit) / width
    change = up_ref[...].astype(F32) + rstd * (scaled - first - unit * second)
    change_ref[...] = change
    low = change.astype(BF)
    low_ref[...] = low
    rows = [
        token_sum_row(folded(part)) for part in (second_change * unit, second_change, change)
    ]
    first, second = upstream_rows(
        low.astype(F32), t_ref[...].astype(F32), late_ref, MERGE_GW, width
    )
    mean, rstd = stat_ref[0:1, :], stat_ref[1:2, :]
    head_width = q_ref.shape[0] // 2
    norm_parts = []
    for shard, merge in ((0, merge_own), (1, merge_peer)):
        here = slice(shard * head_width, (shard + 1) * head_width)
        gain = head_column(vec_ref, 2, shard, head_width)
        merged_change = nn(merge[...], low)
        unit = (mixed_ref[here, :] - mean) * rstd
        merged_ref[here, :] = (unit * gain + head_column(vec_ref, 3, shard, head_width)).astype(BF)
        norm_parts.append((folded(merged_change * unit), folded(merged_change)))
        mixed_change_ref[here, :] = (
            rstd * (merged_change * gain - first - unit * second)
        ).astype(BF)

    queries = q_ref.shape[1]
    pieces = key_pieces(chunk, size, flag_ref[IN_CORE], start_ref[...], kv_refs)
    masks = [piece_mask(piece, queries) for piece in pieces]
    totals = list(before_sums) + [own_sum, recv_sum]
    for place, ref in enumerate((own_sum, recv_sum)):
        ref[...] = later_refs[place][...] if later else jnp.zeros(ref.shape, F32)
    for ref in before_sums:
        ref[...] = jnp.zeros(ref.shape, F32)
    factor = HEAD_DIM ** (-0.5)
    query_parts = []
    for shard in range(2):
        query_folds = []
        for head in range(head_width // HEAD_DIM):
            place = shard * head_width + head * HEAD_DIM
            here = slice(place, place + HEAD_DIM)
            query = q_ref[here, :]
            scaled_query = (query * factor).astype(BF)
            mixed_change = mixed_change_ref[here, :]
            row = shard * (head_width // HEAD_DIM) + head
            lse = lse_ref[row : row + 1, :]
            delta = row_total(mixed_change.astype(F32) * mixed_ref[here, :])
            query_change = None
            for index, (piece, mask, total_ref) in enumerate(zip(pieces, masks, totals)):
                keys = piece_rows(piece, shard, head * HEAD_DIM)
                values = piece_rows(piece, shard, head_width + head * HEAD_DIM)
                first = 2 * head_width * ((1 - shard) if index % 2 else shard) + head * HEAD_DIM
                key_rows = slice(first, first + HEAD_DIM)
                value_rows = slice(first + head_width, first + head_width + HEAD_DIM)
                probs = jnp.where(mask, jnp.exp(tn(keys, scaled_query) - lse), 0.0)
                score_change = (probs * (tn(values, mixed_change) - delta)).astype(BF)
                term = nn(keys, score_change)
                query_change = term if query_change is None else query_change + term
                total_ref[key_rows, :] += nt(scaled_query, score_change)
                total_ref[value_rows, :] += nt(mixed_change, probs.astype(BF))
            query_change = query_change * factor
            query_folds.append(folded(query_change))
            gq_ref[here, :] = query_change.astype(BF)
        query_parts.append(jnp.concatenate(query_folds, axis=0))
    recv_low[...] = recv_sum[...].astype(BF)
    for shard in range(2):
        gain_part, bias_part = norm_parts[shard]
        packed = [query_parts[shard], jnp.zeros(gain_part.shape, F32), gain_part, bias_part]
        rows.append(token_sum_row(jnp.concatenate(packed, axis=0)))
    sums_ref[...] = rows_of(rows, 0, 8, F32)


def heads_backward_kernel(norm, *refs):
    flag_ref, gq_ref, own_sum, came_ref = refs[:4]
    heads_refs = refs[4:6]
    out_ref, joined_ref, sums_ref = refs[-3:]
    width = gq_ref.shape[0] // 2
    product = None
    rows = []
    for shard in range(2):
        rows_here = own_sum.shape[0]
        first = pl.multiple_of((1 - flag_ref[IN_CORE]) * rows_here + shard * 2 * width, 2 * width)
        came = came_ref[pl.ds(first, 2 * width), :].astype(F32)
        total = own_sum[2 * width * shard : 2 * width * (shard + 1), :] + came
        value_part = folded(total[width:])
        zero = jnp.zeros(value_part.shape, F32)
        rows.append(token_sum_row(jnp.concatenate([zero, value_part, zero, zero], axis=0)))
        first = 3 * width * shard
        joined_ref[first : first + width, :] = gq_ref[shard * width : (shard + 1) * width, :]
        joined_ref[first + width : first + 3 * width, :] = total.astype(BF)
        term = tn(heads_refs[shard][...], joined_ref[first : first + 3 * width, :])
        product = term if product is None else product + term
    low = product.astype(BF)
    out_ref[...] = low
    if norm:
        normed_change = low.astype(F32)
        values = refs[6][...].astype(F32)
        mean, rstd = token_stats(values)
        for part in (normed_change * ((values - mean) * rstd), normed_change):
            rows.append(token_sum_row(folded(part)))
    sums_ref[...] = rows_of(rows, 0, 8, F32)


def attention_weights_kernel(pieces, *refs):
    refs, outs = refs[: -1 - pieces], refs[-1 - pieces :]
    chunks = len(refs) // 4
    width = refs[3].shape[0] // 2
    for index, out_refs in ((1, outs[1:]), (0, outs[:1])):
        heads = merge = None
        for chunk in range(chunks):
            up, joined, normed, merged = refs[4 * chunk : 4 * chunk + 4]
            term = nt(normed[...], joined[3 * width * index : 3 * width * (index + 1), :])
            heads = term if heads is None else heads + term
            term = nt(up[...], merged[width * index : width * (index + 1), :])
            merge = term if merge is None else merge + term
        write_pieces(out_refs, 0, heads)
        write_pieces(out_refs, 3 * width, merge)


def final_kernel(own_ref, recv_ref, change_ref, h_ref, vec_ref, out_ref):
    out_ref[...] = norm_back(own_ref, recv_ref, change_ref, h_ref, vec_ref)[0].T.astype(BF)


def fold_kernel(after_bit, flag, flag_ref, stay_ref, *refs):
    came_refs, (keep_ref, give_ref) = refs[:-2], refs[-2:]
    each = came_refs[0].shape[0]
    bit = flag_ref[flag]
    for out_ref, mine in ((give_ref, 1 - bit), (keep_ref, bit)):
        for place in range(keep_ref.shape[0]):
            high, low = place // after_bit, place % after_bit
            if len(came_refs) == 1:
                index = (2 * high + mine) * after_bit + low
                out_ref[place] = (
                    stay_ref[index].astype(F32) + came_refs[0][index].astype(F32)
                ).astype(BF)
                continue
            first = 2 * high * after_bit + low
            pair = [
                stay_ref[index].astype(F32) + came_refs[index // each][index % each].astype(F32)
                for index in (first, first + after_bit)
            ]
            out_ref[place] = jnp.where(mine == 0, pair[0], pair[1]).astype(BF)


def settle_kernel(stay_ref, came_ref, out_ref):
    out_ref[...] = stay_ref[...].astype(F32) + came_ref[...].astype(F32)


def finish_kernel(flag_ref, stay_ref, came_ref, upper_ref, given_ref, kept_ref):
    first = flag_ref[IN_SECTION] == 0
    lower = stay_ref[0].astype(F32) + came_ref[0].astype(F32)
    upper = upper_ref[0]
    given_ref[...] = jnp.where(first, upper, lower).astype(BF)
    kept_ref[...] = jnp.where(first, lower, upper)


def collect_kernel(layers, counts, flag_ref, *refs):
    give_ref, keep_ref = refs[-2:]
    refs = list(refs[:-2])
    groups = {}
    for name, count in counts:
        groups[name] = refs[:count]
        refs = refs[count:]
    first_section, first_chip = flag_ref[IN_SECTION] == 0, flag_ref[IN_CHIP] == 0
    tables = []
    for layer in range(layers):

        def row(index, name, at=layer):
            return sum(ref[index : index + 1, :] for ref in groups[name, at])

        norm = [
            row(6 + place, "feed", layer - 1) if layer else row(2 + place, "heads")
            for place in range(2)
        ]
        shared = norm + [row(2, "attend"), row(8, "feed"), row(0, "attend"), row(1, "attend")]
        shared = [
            item if not layer and place < 2 else jnp.where(first_chip, item, 0.0)
            for place, item in enumerate(shared)
        ]
        split = []
        for shard in range(2):
            split += [row(2 * place + shard, "feed") for place in range(3)]
            split.append(row(3 + shard, "attend") + row(shard, "heads"))
        tables.append(rows_of(shared, 0, 16, F32) + rows_of(split, 8, 16, F32))
    keep_ref[...] = jnp.where(first_section, tables[0], tables[1])
    give_ref[...] = jnp.where(first_section, tables[1], tables[0])


def call(kernel, outs, args, scratch=(), scalars=(), deps=(), token=False):
    specs = [
        pl.BlockSpec(memory_space=pltpu.SMEM if place in scalars else pltpu.VMEM)
        for place in range(len(args))
    ]
    specs += [pl.BlockSpec(memory_space=pl.ANY)] * len(deps)
    used, given = len(args), len(args) + len(deps)
    outs = list(outs) + [arr((8, 128), F32)] * token

    def run(*refs):
        out_refs, inner = refs[given : given + len(outs)], refs[given + len(outs) :]
        kernel(*refs[:used], *out_refs[: len(outs) - token], *inner)
        if token:
            out_refs[-1][...] = jnp.zeros((8, 128), F32)

    return pl.pallas_call(
        run,
        out_shape=outs,
        in_specs=specs,
        out_specs=[pl.BlockSpec(memory_space=pltpu.VMEM)] * len(outs),
        scratch_shapes=list(scratch),
        compiler_params=pltpu.CompilerParams(vmem_limit_bytes=VMEM_MB * 1024 * 1024),
        cost_estimate=pl.CostEstimate(flops=0, bytes_accessed=0, transcendentals=0),
        name=(kernel.func if isinstance(kernel, partial) else kernel).__name__,
    )(*args, *deps)


def arr(shape, dtype):
    return jax.ShapeDtypeStruct(shape, dtype)


def step_swap(values, axis, step):
    count = lax.axis_size(axis)
    return lax.ppermute(values, axis, [(i, i ^ step) for i in range(count)])


def core_swap(block):
    return step_swap(block, TENSOR, 1)


def both_cores_of(block):
    count = lax.axis_size(TENSOR)
    groups = [[i, i + 1] for i in range(0, count, CORES)]
    return lax.all_gather(block, TENSOR, axis=0, tiled=True, axis_index_groups=groups)


def chip_swap(block):
    return step_swap(block, TENSOR, 2)


def section_swap(block):
    return step_swap(block, SECTION, 1)


class OverRows:
    def __init__(self, flags, own, peers, sections_last=False):
        count = lax.axis_size(DP)
        rows, columns = own.shape[0] // count, own.shape[1]
        steps = []
        while 1 << len(steps) < count:
            steps.append((DP, 1 << len(steps), IN_DP + len(steps)))
        sections = (SECTION, 1, IN_SECTION)
        self.flags = flags
        self.bits = steps[::-1] + [sections]
        self.steps = steps + [sections] if sections_last else [sections] + steps
        shape = (2 * count, rows // 2, columns)
        self.stay = own.reshape(shape)
        each = (shape[0] // len(peers),) + shape[1:]
        self.came = [core_swap(peer.reshape(each)) for peer in peers]

    def advance(self, deps):
        item = self.steps.pop(0)
        axis, step, flag = item
        place = self.bits.index(item)
        self.bits.pop(place)
        half = self.stay.shape[0] // 2
        out = arr((half,) + self.stay.shape[1:], BF)
        keep, give, token = call(
            partial(fold_kernel, 1 << (len(self.bits) - place), flag),
            [out, out],
            [self.flags, self.stay, *self.came],
            scalars=(0,),
            deps=deps,
            token=True,
        )
        self.stay, self.came = keep, [step_swap(give, axis, step)]
        return [token]


def settle(item, deps):
    while item.steps:
        deps = item.advance(deps)
    out, token = call(
        settle_kernel, [arr(item.stay.shape, F32)], [item.stay, item.came[0]], deps=deps, token=True
    )
    return out, [token]


def after(value, *others):
    return lax.optimization_barrier((value,) + others)[0]


def other_section(weight, *behind):
    odd = lax.axis_index(DP) & 1
    rows = weight.shape[0] // 2
    half = lax.dynamic_slice_in_dim(weight, odd * rows, rows, 0)
    return section_swap(after(half, *behind))


def both_halves(came, *behind):
    return came, step_swap(after(came, *behind), DP, 1)


def body(
    boundary,
    document_lengths,
    norm_gain,
    norm_bias,
    pair_weight,
    value_weight,
    query_bias,
    value_bias,
    inner_gain,
    inner_bias,
    merge_weight,
    merge_bias,
    second_gain,
    second_bias,
    expand_weight,
    expand_bias,
    hidden_gain,
    hidden_bias,
    shrink_weight,
    shrink_bias,
):
    section = lax.axis_index(SECTION)
    first = section == 0
    place = lax.axis_index(TENSOR)
    core = place & (CORES - 1)
    chip = place >> (CORES - 1)
    block = boundary.shape[2]
    width = boundary.shape[4]
    head_width = value_weight.shape[-1]
    shard = expand_weight.shape[-1]
    chunks = lax.axis_size(TENSOR) // CORES
    size = CORES * block
    row_length = chunks * size
    layers = 2
    row_place = lax.axis_index(DP)
    odd = row_place & 1
    bits = [(row_place >> bit) & 1 for bit in range(max(1, (lax.axis_size(DP) - 1).bit_length()))]
    flags = jnp.stack([section, chip, core] + bits).astype(jnp.int32)

    own = boundary[0, :, :, 0, :]
    mine = lax.dynamic_index_in_dim(own, section, 0, False)
    away = lax.dynamic_index_in_dim(own, 1 - section, 0, False)
    came = section_swap(away)
    heads_vector = jnp.concatenate(
        [after(query_bias[0], away), value_bias[0], inner_gain[0], inner_bias[0]]
    )
    early = jnp.concatenate(
        [norm_gain, norm_bias, heads_vector[None], jnp.zeros((1, width), F32)], axis=0
    )
    early_came = section_swap(after(early, away))
    lengths = jnp.where(first, document_lengths[0, 0], document_lengths[1, 0])
    ends = jnp.cumsum(lengths)
    positions = jnp.arange(row_length, dtype=jnp.int32)
    starts = jnp.max(
        jnp.where(positions[:, None] >= ends[None, :], ends[None, :], 0), axis=-1
    ).astype(jnp.int32)[None]
    starts = [
        lax.dynamic_slice_in_dim(starts, i * size + core * block, block, 1) for i in range(chunks)
    ]

    table = jnp.stack([heads_vector, expand_bias[0], hidden_gain[0], hidden_bias[0]])
    table_peer = core_swap(table)
    vector_columns = arr((width, 128), F32)
    early = call(
        early_kernel,
        [vector_columns] * layers,
        [flags, early, early_came, table_peer, core_swap(early_came)],
        scalars=(0,),
    )
    merge32 = after(merge_weight[0], away).astype(F32)
    shrink32 = after(shrink_weight[0], away).astype(F32)
    shares = jnp.stack(
        [
            jnp.sum(merge32 * inner_gain[0][:, None], axis=0),
            jnp.sum(shrink32 * hidden_gain[0][:, None], axis=0),
            jnp.sum(merge32 * inner_bias[0][:, None], axis=0),
            jnp.sum(shrink32 * hidden_bias[0][:, None], axis=0),
        ]
    )
    shares = shares + core_swap(shares)
    inputs, cotangent = call(
        first_kernel,
        [arr((block + STAT_ROWS, width), BF), arr((block, width), BF)],
        [flags, mine, came, shares],
        scalars=(0,),
    )
    inputs_there = chip_swap(inputs)
    cotangent_there = chip_swap(after(cotangent, inputs_there))
    plain = jnp.concatenate([merge_bias, second_gain, second_bias, shrink_bias], axis=0)
    half_merge = merge_weight.shape[1] // 2
    late_rows, merge_given = call(
        late_rows_kernel,
        [arr((COLUMNS, width), F32), arr((half_merge + 3 * COLUMNS, width), BF)],
        [flags, shares, inputs_there, plain, table, table_peer, merge_weight[0]],
        scalars=(0,),
    )

    heads_weight = jnp.concatenate(
        [
            pair_weight[0].transpose(1, 2, 0).reshape(2 * head_width, width),
            value_weight[0].T,
        ],
        axis=0,
    )
    given = (heads_weight, merge_weight[0], expand_weight[0], shrink_weight[0])
    given_peer = [core_swap(item) for item in given]
    heads_half = other_section(given[0], away)
    merge_half = section_swap(merge_given)
    late = call(
        late_kernel, [vector_columns] * layers, [flags, late_rows, merge_half], scalars=(0,)
    )
    expand_half = other_section(given[2], merge_given)
    shrink_whole = section_swap(after(given[3], merge_given))
    there = [both_halves(heads_half, inputs), both_halves(merge_half, inputs_there)]
    there.append(both_halves(expand_half, there[0][1]))
    there_peer = [[core_swap(item) for item in pair] for pair in there[:2]]

    even = odd == 0

    def layer_weight(layer, own, came, other=None):
        if other is None:
            away = came
        else:
            upper = jnp.where(even, came, other)
            lower = jnp.where(even, other, came)
            rows = own.shape[0] // 2
            away = jnp.concatenate([upper[:rows], lower[:rows]], axis=0)
        return jnp.where(first, away, own) if layer else jnp.where(first, own, away)

    def both_cores(index, pair, pair_peer):
        return [
            (
                layer_weight(layer, given[index], *pair),
                layer_weight(layer, given_peer[index], *pair_peer),
            )
            for layer in range(layers)
        ]

    heads_w, merge_w = [both_cores(index, there[index], there_peer[index]) for index in range(2)]

    act = arr((width, block), BF)
    act32 = arr((width, block), F32)
    carried = arr((width + STAT_ROWS, block), BF)
    stats = arr((8, block), F32)
    heads2 = arr((2 * head_width, block), BF)
    keyed = arr((4 * head_width, block), BF)
    keyed32 = arr((4 * head_width, block), F32)
    wide = arr((2 * shard, block), BF)
    few = arr((8, width), F32)
    many = arr((16, width), F32)
    inner_share = 2 * head_width
    hidden_share = 2 * shard

    sums_of = {}

    def note(name, layer, table):
        sums_of.setdefault((name, layer), []).append(table)

    keyed = arr((4 * head_width, block), BF)
    keyed32 = arr((4 * head_width, block), F32)
    changes = [
        call(
            partial(cotangent_kernel, i),
            [act, stats],
            [flags, cotangent, cotangent_there, late[layers - 1]],
            scalars=(0,),
        )
        for i in range(chunks)
    ]
    kept = []
    previous = [dots for low, dots in changes]
    for layer in range(layers):
        save = [dict() for i in range(chunks)]
        for i in range(chunks):
            item = save[i]
            outs = [act, act, heads2, keyed]
            if layer:
                lower = kept[-1][i]
                results = call(
                    partial(between_kernel, hidden_share),
                    [act, stats] + outs,
                    [*lower["part"], lower["middle"], late[layer - 1], early[layer], *heads_w[layer]],
                    deps=previous,
                )
                lower.update(t_shrink=results[0], stat_shrink=results[1])
                results = results[2:]
            else:
                results = call(
                    partial(start_kernel, i),
                    outs,
                    [flags, inputs, inputs_there, early[0], *heads_w[0]],
                    scalars=(0,),
                    deps=previous,
                )
            item["h"], item["n"], item["q"] = results[:3]
            item["kv"] = [results[3], both_cores_of(results[3])]
            before = [ref for j in range(i + 1) for ref in save[j]["kv"]]
            chip_part, item["mixed"], item["lse"] = call(
                partial(attention_forward_kernel, i, size),
                [carried, arr((2 * head_width, block), F32), stats],
                [flags, starts[i], item["q"], *merge_w[layer], early[layer], *before],
                scalars=(0,),
                deps=previous,
            )
            item["part"] = (chip_part, chip_swap(chip_part))
            previous = [chip_part]
        if not layer:
            there.append((after(shrink_whole, save[0]["part"][1]),))
            there_peer.append([core_swap(after(item, save[0]["part"][0])) for item in there[2]])
            there_peer.append([core_swap(there[3][0])])
            expand_w, shrink_w = [
                both_cores(index, there[index], there_peer[index]) for index in (2, 3)
            ]
        turn_rows = []
        for i in range(chunks):
            item = save[i]
            last = layer + 1 == layers
            results = call(
                partial(feed_forward_kernel, inner_share, last, i),
                [carried, act32, act, act, stats, arr((2 * shard, block), F32)]
                + ([arr((8 * i + 8, block), F32)] if last else []),
                [*item["part"], item["h"], late[layer], *expand_w[layer], *shrink_w[layer]]
                + ([changes[i][0]] + turn_rows if last else []),
                deps=previous,
            )
            chip_part, item["middle"], item["second"] = results[:3]
            item["t_merge"], item["stat_merge"], item["expanded"] = results[3:6]
            if last:
                item["part"] = chip_part
                turn_rows = [results[6]]
            else:
                item["part"] = (chip_part, chip_swap(chip_part))
            previous = [chip_part]
        kept.append(save)
    turn_rows.append(chip_swap(turn_rows[0]))

    top = kept[-1]
    keep, keep_middle, give = call(
        pick_kernel,
        [carried, act32, carried],
        [flags, top[0]["part"], top[1]["part"], top[0]["middle"], top[1]["middle"]],
        scalars=(0,),
        deps=previous,
    )
    output_parts = (keep, chip_swap(after(give, turn_rows[1])), keep_middle)
    previous = [keep]

    feed_sums = [None] * layers
    attend_sums = [None] * layers

    def feed_weights(layer, deps):
        args = []
        for item in kept[layer]:
            args += [item[name] for name in ("up", "shrunk", "change", "second")]
        grad = arr((width, 2 * shard), BF)
        pieces = 4
        piece = arr((width // pieces, 2 * shard), BF)
        own, *peers, token = call(
            partial(feed_weights_kernel, pieces), [grad] + [piece] * pieces, args, deps=deps, token=True
        )
        feed_sums[layer] = OverRows(flags, own, peers)
        return [token]

    def attention_weights(layer, deps):
        args = []
        for item in kept[layer]:
            args += [item[name] for name in ("up_middle", "joined", "n", "merged")]
        grad = arr((width, 4 * head_width), BF)
        pieces = 2
        piece = arr((width // pieces, 4 * head_width), BF)
        own, *peers, token = call(
            partial(attention_weights_kernel, pieces),
            [grad] + [piece] * pieces,
            args,
            deps=deps,
            token=True,
        )
        attend_sums[layer] = OverRows(flags, own, peers, layer > 0)
        return [token]

    def aside(point, deps):
        for kind, layer in ASIDE.get(point, ()):
            if kind == FEED:
                deps = feed_weights(layer, deps)
            elif kind == ATTEND:
                deps = attention_weights(layer, deps)
            else:
                deps = (feed_sums if kind == FEED_STEP else attend_sums)[layer].advance(deps)
        return deps

    for layer in reversed(range(layers)):
        save = kept[layer]
        for i in reversed(range(chunks)):
            item = save[i]
            common = [late[layer], *expand_w[layer], *shrink_w[layer], item["expanded"]]
            outs = [act, wide, wide, many]
            if layer + 1 == layers:
                item["up"], dots = changes[i]
                results = call(
                    partial(turn_kernel, hidden_share, i),
                    outs,
                    [*turn_rows, item["up"], dots] + common,
                    deps=previous,
                )
            else:
                upper = kept[layer + 1][i]
                results = call(
                    partial(layer_back_kernel, hidden_share),
                    [act] + outs,
                    [
                        *upper["part"],
                        upper["middle_change"],
                        upper["h"],
                        early[layer + 1],
                        item["t_shrink"],
                        item["stat_shrink"],
                    ]
                    + common,
                    deps=previous,
                )
                item["up"], results = results[0], results[1:]
            chip_part, item["change"], item["shrunk"], table = results
            note("feed", layer, table)
            item["part"] = (chip_part, chip_swap(chip_part))
            previous = [chip_part]
            previous = aside((FEED, layer, i), previous)
        later = [[] for i in range(chunks)]
        for i in reversed(range(chunks)):
            item = save[i]
            before = [ref for j in range(i + 1) for ref in save[j]["kv"]]
            results = call(
                partial(attention_backward_kernel, i, size, len(later[i])),
                [act, act32, heads2, heads2, keyed32, keyed, few] + [keyed32] * (2 * i),
                [
                    *item["part"],
                    item["up"],
                    item["middle"],
                    item["t_merge"],
                    item["stat_merge"],
                    late[layer],
                    early[layer],
                    flags,
                    starts[i],
                    item["q"],
                    *merge_w[layer],
                    item["mixed"],
                    item["lse"],
                    *before,
                    *later[i],
                ],
                scratch=[
                    pltpu.VMEM((4 * head_width, block), F32),
                    pltpu.VMEM((2 * head_width, block), BF),
                ],
                scalars=(8,),
                deps=previous,
            )
            item["up_middle"], item["middle_change"], gq, item["merged"] = results[:4]
            own_sum, recv_low, table = results[4:7]
            for j in range(i):
                later[j] += results[7 + 2 * j : 9 + 2 * j]
            note("attend", layer, table)
            previous = aside((ATTEND, layer, i), [table])
            chip_part, item["joined"], table = call(
                partial(heads_backward_kernel, not layer),
                [act, arr((6 * head_width, block), BF), few],
                [flags, gq, own_sum, both_cores_of(recv_low), *heads_w[layer]]
                + ([] if layer else [item["h"]]),
                scalars=(0,),
                deps=previous,
            )
            note("heads", layer, table)
            item["part"] = (chip_part, chip_swap(chip_part)) if layer else chip_part
            previous = [chip_part]
            previous = aside((HEAD, layer, i), previous)

    previous = attend_sums[1].advance(previous)
    previous = attention_weights(0, previous)
    keep, keep_change, keep_h, give = call(
        pick_kernel,
        [act, act32, act, act],
        [flags] + [kept[0][i][name] for name in ("part", "middle_change", "h") for i in range(2)],
        scalars=(0,),
        deps=previous,
    )
    keep_there = chip_swap(give)
    previous = feed_sums[1].advance([keep])
    previous = feed_sums[0].advance(previous)
    previous = attend_sums[0].advance(previous)
    counts = [(key, len(tables)) for key, tables in sums_of.items()]
    give, keep_rows = call(
        partial(collect_kernel, layers, counts),
        [many, many],
        [flags] + [table for tables in sums_of.values() for table in tables],
        scalars=(0,),
        deps=previous,
    )
    previous = [give]
    last = call(
        final_kernel,
        [arr((block, width), BF)],
        [keep, keep_there, keep_change, keep_h, early[0]],
        deps=previous,
    )[0]
    previous = attend_sums[0].advance([last])
    rows = keep_rows + after(section_swap(give), *previous)
    rows_peer = core_swap(rows)
    rows = jnp.concatenate([rows[:8] + rows_peer[:8], rows[8:12] + rows_peer[12:]])
    if feed_sums[0].steps:
        previous = feed_sums[0].advance(previous)
    feed_above, previous = settle(feed_sums[1], previous)
    came_rows = step_swap(after(rows, *previous), DP, 1)
    output = call(
        partial(output_kernel, hidden_share),
        [arr((block, width), BF)],
        [*output_parts, late[layers - 1]],
        deps=previous,
    )[0]
    previous = [output]
    theirs = section_swap(jnp.where(first, output, last))
    for item in (attend_sums[0], feed_sums[0]):
        while item.steps:
            previous = item.advance(previous)
    rows = rows + after(came_rows, *previous)
    steps = [1 << bit for bit in range(1, (lax.axis_size(DP) - 1).bit_length())]
    came_rows = step_swap(rows, DP, steps[0])

    def own_layer(item, above, deps):
        shape = above.shape[1:]
        given, kept_half, token = call(
            finish_kernel,
            [arr(shape, BF), arr(shape, F32)],
            [flags, item.stay, item.came[0], above],
            scalars=(0,),
            deps=deps,
            token=True,
        )
        came_half = section_swap(given).astype(F32)
        upper = jnp.where(first, kept_half, came_half)
        lower = jnp.where(first, came_half, kept_half)
        return jnp.concatenate([upper, lower], axis=0), [token]

    feed, previous = own_layer(feed_sums[0], feed_above, previous)
    attend_above, previous = settle(attend_sums[1], previous)
    rows = rows + after(came_rows, *previous)
    for step in steps[1:]:
        rows = rows + step_swap(rows, DP, step)
    shared = rows[:8]
    shared_there = chip_swap(shared)
    theirs = after(theirs, *previous)
    attend, previous = own_layer(attend_sums[0], attend_above, previous)
    shared = (shared + after(shared_there, *previous))[:6, None]
    split = rows[8:12, None]

    kept_here = jnp.where(first, last, output)
    final = jnp.stack(
        [jnp.where(first, kept_here, theirs), jnp.where(first, theirs, kept_here)]
    )[None, :, :, None, :]

    rows_here = attend.shape[0]
    pair_gradient = attend[:, : 2 * head_width].reshape(rows_here, 2, head_width)
    value_gradient = attend[:, 2 * head_width : 3 * head_width]
    merge_gradient = attend[:, 3 * head_width :].T
    shrink_gradient = feed[:, :shard].T
    expand_gradient = feed[:, shard:]
    packed = split[3]

    def packed_part(index):
        return packed[:, index * head_width : (index + 1) * head_width]

    return (
        final,
        shared[0],
        shared[1],
        pair_gradient[None],
        value_gradient[None],
        packed_part(0),
        packed_part(1),
        packed_part(2),
        packed_part(3),
        merge_gradient[None],
        shared[2],
        shared[4],
        shared[5],
        expand_gradient[None],
        split[2],
        split[0],
        split[1],
        shrink_gradient[None],
        shared[3],
    )


def solution(mesh):
    in_specs = (
        P(SECTION, None, TENSOR, DP, None),
        P(None, DP, None),
        P(SECTION, None),
        P(SECTION, None),
        P(SECTION, None, None, TENSOR),
        P(SECTION, None, TENSOR),
        P(SECTION, TENSOR),
        P(SECTION, TENSOR),
        P(SECTION, TENSOR),
        P(SECTION, TENSOR),
        P(SECTION, TENSOR, None),
        P(SECTION, None),
        P(SECTION, None),
        P(SECTION, None),
        P(SECTION, None, TENSOR),
        P(SECTION, TENSOR),
        P(SECTION, TENSOR),
        P(SECTION, TENSOR),
        P(SECTION, TENSOR, None),
        P(SECTION, None),
    )
    out_specs = (
        P(SECTION, None, TENSOR, DP, None),
        P(SECTION, None),
        P(SECTION, None),
        P(SECTION, DP, None, TENSOR),
        P(SECTION, DP, TENSOR),
        P(SECTION, TENSOR),
        P(SECTION, TENSOR),
        P(SECTION, TENSOR),
        P(SECTION, TENSOR),
        P(SECTION, TENSOR, DP),
        P(SECTION, None),
        P(SECTION, None),
        P(SECTION, None),
        P(SECTION, DP, TENSOR),
        P(SECTION, TENSOR),
        P(SECTION, TENSOR),
        P(SECTION, TENSOR),
        P(SECTION, TENSOR, DP),
        P(SECTION, None),
    )
    return jax.shard_map(body, mesh=mesh, in_specs=in_specs, out_specs=out_specs, check_vma=False)
```
